32 devices in a mesh: dp: 16 (over z, y, core), mp: 2 (over x).
Axes of the slice: x: 2, y: 2, z: 4, core: 2. Of those that a mesh axis runs over, the one named last changes fastest.
Arguments:
- inputs: bfloat16 [2, 4096, 2048], P(None, 'dp'), may hold values from -6 to 6
- seq_starts: int32 [2, 4096], P(None, 'dp'), may hold values from 0 to 4095, as said below
- cotangent: bfloat16 [2, 4096, 2048], P(None, 'dp'), may hold values from -6 to 6
- attn_gain: bfloat16 [2048], P('dp'), may hold values from 0.5 to 1.5
- query_weight: bfloat16 [2048, 2048], P('dp', 'mp'), may hold values from -0.125 to 0.125
- key_matrix: bfloat16 [2048, 512], P('dp', 'mp'), may hold values from -0.125 to 0.125
- value_matrix: bfloat16 [2048, 512], P('dp', 'mp'), may hold values from -0.125 to 0.125
- out_weight: bfloat16 [2048, 2048], P('mp', 'dp'), may hold values from -0.5 to 0.5
- mlp_gain: bfloat16 [2048], P('dp'), may hold values from 0.5 to 1.5
- gate_weight: bfloat16 [2048, 8192], P('dp', 'mp'), may hold values from -0.125 to 0.125
- up_weight: bfloat16 [2048, 8192], P('dp', 'mp'), may hold values from -0.125 to 0.125
- down_weight: bfloat16 [8192, 2048], P('mp', 'dp'), may hold values from -0.125 to 0.125
Outputs:
- output: bfloat16 [2, 4096, 2048], P(None, 'dp')
- input_grad: float32 [2, 4096, 2048], P(None, 'dp')
- grad_attn_gain: float32 [2048], P('dp')
- grad_query: float32 [2048, 2048], P('dp', 'mp')
- grad_key: float32 [2048, 512], P('dp', 'mp')
- grad_value: float32 [2048, 512], P('dp', 'mp')
- grad_out: float32 [2048, 2048], P('mp', 'dp')
- grad_mlp_gain: float32 [2048], P('dp')
- grad_gate: float32 [2048, 8192], P('dp', 'mp')
- grad_up: float32 [2048, 8192], P('dp', 'mp')
- grad_down: float32 [8192, 2048], P('mp', 'dp')
The draws below stay inside these ranges and needn't reach their ends.
Inputs may be any that keep to these rules, and one draw needn't show every extreme that they name: `seq_starts`: each entry is the index, within its micro-batch of 4096 tokens, of the first token of its sequence: entries never fall along a micro-batch, never exceed their own index, every multiple of 256 begins a sequence, and the last token of a micro-batch begins a sequence of its own.
All inputs are finite; a program needn't handle non-finite values.
Results may differ from the reference program's by a relative error of at most 0.015.
Values may be sent and summed in bfloat16 or wider, within the bound.
No kernel may reach another device: no remote copies, remote signals or barrier semaphores. Data moves between devices by JAX's collectives and lax.ppermute only.
A program may use at most 320 MiB of HBM per device.

```python
import math
import jax
import jax.numpy as jnp
from jax import lax

MODEL_WIDTH = 2048
QUERY_HEADS = 32
KEY_VALUE_HEADS = 8
HEAD_SIZE = 64
FF = 8192
SHARD_TOKENS = 256
MICRO = 2
MICRO_TOKENS = 4096
N_DP = 16


def draw_seq_starts(key, part):
    key = jax.random.fold_in(key, 7)
    markers = jax.random.randint(key, (MICRO, MICRO_TOKENS), 0, SHARD_TOKENS)
    position = jnp.arange(MICRO_TOKENS, dtype=jnp.int32)[None, :] * jnp.ones((MICRO, 1), jnp.int32)
    opening = (markers < 4) | (position % SHARD_TOKENS == 0) | (position == MICRO_TOKENS - 1)
    return lax.cummax(jnp.where(opening, position, 0), axis=1).astype(jnp.int32)


def with_spikes(array, rng, source, target, shards_of, factor):
    owner, partner = [(jnp.arange(array.shape[dim]) // (array.shape[dim] // shards_of)).reshape([-1 if axis == dim else 1 for axis in range(array.ndim)]) for dim in (source, target)]
    chosen = jax.random.permutation(rng, shards_of)[partner]
    strong = (owner == chosen) | (owner == (partner + shards_of // 2) % shards_of)
    return jnp.where(strong, factor * array, array)


def shard_levels(key, extent, shards, smallest, top_value):
    level = 1.0
    for dim, blocks in shards:
        draws = jax.random.uniform(jax.random.fold_in(jax.random.fold_in(key, 6), dim), (blocks,), jnp.float32, smallest / len(shards), top_value / len(shards))
        level = level * jnp.repeat(jnp.exp(draws), extent[dim] // blocks).reshape((-1,) + (1,) * (len(extent) - 1 - dim))
    return level


def centred(stream_key, shape, deviation, most, shards=(), held_as=jnp.bfloat16):
    values = deviation * jax.random.normal(stream_key, shape, jnp.float32)
    if shards:
        values = values * shard_levels(stream_key, shape, shards, -0.22, 0.18)
    return jnp.clip(values, -most, most).astype(held_as)


def heavy_noise(own_key, shape, spread, bound, shards, heavy, kind=jnp.bfloat16):
    drawn = spread * jax.random.normal(own_key, shape, jnp.float32)
    if shards:
        drawn = drawn * shard_levels(own_key, shape, shards, -0.22, 0.18)
    return jnp.clip(with_spikes(drawn, jax.random.fold_in(own_key, 3), *heavy), -bound, bound).astype(kind)


def setup_inputs(seed: int = 0) -> dict:
    arg_keys = jax.random.split(jax.random.key(seed), 13)
    return {
        "inputs": heavy_noise(arg_keys[0], (MICRO, MICRO_TOKENS, MODEL_WIDTH), 1.0, 6.0, ((1, 16),), (1, 2, 16, 2.0)),
        "seq_starts": draw_seq_starts(jax.random.fold_in(arg_keys[12], 71), 0),
        "cotangent": heavy_noise(arg_keys[2], (MICRO, MICRO_TOKENS, MODEL_WIDTH), 1.0, 6.0, ((1, 16),), (1, 2, 16, 2.0)),
        "attn_gain": jnp.clip(1.0 + 0.1 * jax.random.normal(arg_keys[3], (MODEL_WIDTH,), jnp.float32), 0.5, 1.5).astype(jnp.bfloat16),
        "query_weight": centred(arg_keys[4], (MODEL_WIDTH, QUERY_HEADS * HEAD_SIZE), MODEL_WIDTH ** -0.5, 0.125, ((0, 16), (1, 2))),
        "key_matrix": centred(arg_keys[5], (MODEL_WIDTH, KEY_VALUE_HEADS * HEAD_SIZE), MODEL_WIDTH ** -0.5, 0.125, ((0, 16), (1, 2))),
        "value_matrix": centred(arg_keys[6], (MODEL_WIDTH, KEY_VALUE_HEADS * HEAD_SIZE), MODEL_WIDTH ** -0.5, 0.125, ((0, 16), (1, 2))),
        "out_weight": centred(arg_keys[7], (QUERY_HEADS * HEAD_SIZE, MODEL_WIDTH), (QUERY_HEADS * HEAD_SIZE // 16) ** -0.5, 0.5, ((0, 2), (1, 16))),
        "mlp_gain": jnp.clip(1.0 + 0.1 * jax.random.normal(arg_keys[8], (MODEL_WIDTH,), jnp.float32), 0.5, 1.5).astype(jnp.bfloat16),
        "gate_weight": centred(arg_keys[9], (MODEL_WIDTH, FF), MODEL_WIDTH ** -0.5, 0.125, ((0, 16), (1, 2))),
        "up_weight": centred(arg_keys[10], (MODEL_WIDTH, FF), MODEL_WIDTH ** -0.5, 0.125, ((0, 16), (1, 2))),
        "down_weight": centred(arg_keys[11], (FF, MODEL_WIDTH), (FF // 4) ** -0.5, 0.125, ((0, 2), (1, 16))),
    }


EPSILON = 1e-05

@jax.custom_vjp
def lowered(v):
    return lax.optimization_barrier(v.astype(jnp.bfloat16)).astype(jnp.float32)

@jax.custom_vjp
def lowered_backward(v):
    return v

def low_keep(v):
    return (lowered(v), None)

def low_pass(kept, grad):
    return (grad,)

def back_keep(v):
    return (v, None)

def back_low(kept, grad):
    return (lowered(grad),)
lowered.defvjp(low_keep, low_pass)
lowered_backward.defvjp(back_keep, back_low)

def matrix_product(left, right):
    return jnp.dot(left, right, precision=lax.Precision.HIGHEST, preferred_element_type=jnp.float32)

def rms_scale(values_in, gain):
    inverse = lax.rsqrt(lax.optimization_barrier(jnp.mean(values_in * values_in, axis=-1, keepdims=True)) + EPSILON)
    return values_in * inverse * gain

def rope_tables(positions):
    halfway = HEAD_SIZE // 2
    frequency = 500000.0 ** (-(jnp.arange(halfway, dtype=jnp.float32) * 2.0 / HEAD_SIZE))
    angles = positions.astype(jnp.float32)[:, None] * frequency[None, :]
    angles = jnp.concatenate([angles, angles], axis=1)
    return (jnp.cos(angles), jnp.sin(angles))

def rotate_half(head_rows, cosine_lookup, sine_lookup):
    halfway = HEAD_SIZE // 2
    turned = jnp.concatenate([-head_rows[..., halfway:], head_rows[..., :halfway]], axis=-1)
    return head_rows * cosine_lookup[:, None, :] + turned * sine_lookup[:, None, :]

def block_attend(block_args):
    query_rows, key_matrix_rows, value_matrix_rows, block_starts = block_args
    group_width = QUERY_HEADS // KEY_VALUE_HEADS
    grouped_queries = query_rows.reshape(SHARD_TOKENS, KEY_VALUE_HEADS, group_width, HEAD_SIZE)
    scores = jnp.einsum('qkgd,skd->kgqs', grouped_queries, key_matrix_rows, precision=lax.Precision.HIGHEST) * (1.0 / math.sqrt(HEAD_SIZE))
    scores = lowered_backward(scores)
    places = jnp.arange(SHARD_TOKENS)
    allowed = (block_starts[:, None] == block_starts[None, :]) & (places[:, None] >= places[None, :])
    scores = jnp.where(allowed[None, None], scores, -1e+30)
    probs = lowered(jax.nn.softmax(scores, axis=-1))
    attended = jnp.einsum('kgqs,skd->qkgd', probs, value_matrix_rows, precision=lax.Precision.HIGHEST)
    return attended.reshape(SHARD_TOKENS, QUERY_HEADS * HEAD_SIZE)

def micro_forward(rows_in, start_offsets, params):
    attn_scale, query_w, key_kernel, value_kernel, out_w, mlp_scale, gate_w, up_w, down_w = params
    first_hidden = lowered(rms_scale(rows_in, attn_scale))
    positions = jnp.arange(MICRO_TOKENS) - start_offsets
    cosine_lookup, sine_lookup = rope_tables(positions)
    query_rows = lowered(rotate_half(lowered_backward(matrix_product(first_hidden, query_w)).reshape(MICRO_TOKENS, QUERY_HEADS, HEAD_SIZE), cosine_lookup, sine_lookup))
    key_matrix_rows = lowered(rotate_half(lowered_backward(matrix_product(first_hidden, key_kernel)).reshape(MICRO_TOKENS, KEY_VALUE_HEADS, HEAD_SIZE), cosine_lookup, sine_lookup))
    value_matrix_rows = lowered(lowered_backward(matrix_product(first_hidden, value_kernel))).reshape(MICRO_TOKENS, KEY_VALUE_HEADS, HEAD_SIZE)
    block_list = lax.map(jax.checkpoint(block_attend), (query_rows.reshape(N_DP, SHARD_TOKENS, QUERY_HEADS, HEAD_SIZE), key_matrix_rows.reshape(N_DP, SHARD_TOKENS, KEY_VALUE_HEADS, HEAD_SIZE), value_matrix_rows.reshape(N_DP, SHARD_TOKENS, KEY_VALUE_HEADS, HEAD_SIZE), start_offsets.reshape(N_DP, SHARD_TOKENS)))
    attended = lowered(lowered_backward(block_list.reshape(MICRO_TOKENS, QUERY_HEADS * HEAD_SIZE)))
    after = rows_in + lowered_backward(matrix_product(attended, out_w))
    hidden_two = lowered(rms_scale(after, mlp_scale))
    gate = lowered_backward(matrix_product(hidden_two, gate_w))
    upward = lowered_backward(matrix_product(hidden_two, up_w))
    mixed = lowered(jax.nn.silu(gate) * upward)
    return after + lowered_backward(matrix_product(mixed, down_w))

def reference(inputs, seq_starts, cotangent, attn_gain, query_weight, key_matrix, value_matrix, out_weight, mlp_gain, gate_weight, up_weight, down_weight):
    floats = [weight_in.astype(jnp.float32) for weight_in in (attn_gain, query_weight, key_matrix, value_matrix, out_weight, mlp_gain, gate_weight, up_weight, down_weight)]

    def whole(rows_all, *params):
        results = [micro_forward(rows_all[batch_index], seq_starts[batch_index], params) for batch_index in range(MICRO)]
        return jnp.stack(results)
    primal, pullback = jax.vjp(whole, inputs.astype(jnp.float32), *floats)
    grads = pullback(cotangent.astype(jnp.float32))
    return (primal.astype(jnp.bfloat16), grads[0], grads[1], grads[2], grads[3], grads[4], grads[5], grads[6], grads[7], grads[8], grads[9])
```

```python
import math

import jax
import jax.numpy as jnp
from jax import lax
from jax.sharding import PartitionSpec as P

HEAD_SIZE = 64
EPSILON = 1e-05
F32 = jnp.float32
BF16 = jnp.bfloat16


def rms_parts(values_in, gain):
    inverse = lax.rsqrt(jnp.mean(values_in * values_in, axis=-1, keepdims=True) + EPSILON)
    normed = values_in * inverse
    return (normed, inverse, normed * gain)


def rms_back(grad_scaled, normed, inverse, gain):
    grad_normed = grad_scaled * gain
    inner_mean = jnp.mean(grad_normed * normed, axis=-1, keepdims=True)
    return inverse * (grad_normed - normed * inner_mean)


def rope_tables(positions, head_dim):
    halfway = head_dim // 2
    frequency = 500000.0 ** (-(jnp.arange(halfway, dtype=F32) * 2.0 / head_dim))
    angles = positions.astype(F32)[..., None] * frequency
    angles = jnp.concatenate([angles, angles], axis=-1)
    return (jnp.cos(angles), jnp.sin(angles))


def rotate_half(head_rows, cosine_lookup, sine_lookup, direction):
    halfway = head_rows.shape[-1] // 2
    turned = jnp.concatenate([-head_rows[..., halfway:], head_rows[..., :halfway]], axis=-1)
    return head_rows * cosine_lookup[..., None, :] + direction * turned * sine_lookup[..., None, :]


def dot(left, right, left_dim, right_dim):
    return lax.dot_general(
        left, right, (((left_dim,), (right_dim,)), ((), ())), preferred_element_type=F32
    )


def add_low(left, right):
    return (left.astype(F32) + right.astype(F32)).astype(BF16)


def make_per_device(n):
    pair = 4 if n <= 16 else 8
    others = [1 << b for b in reversed(range(n.bit_length() - 1)) if (1 << b) != pair]
    main_order = [pair] + others
    other_order = [v for v in others[::-1] if v not in (1, pair)] + [pair, 1]

    def swap(array, bit):
        return lax.ppermute(array, "dp", [(i, i ^ bit) for i in range(n)])

    def swap_mp(array):
        return lax.ppermute(array, "mp", [(0, 1), (1, 0)])

    def per_device(
        inputs,
        seq_starts,
        cotangent,
        attn_gain,
        query_weight,
        key_matrix,
        value_matrix,
        out_weight,
        mlp_gain,
        gate_weight,
        up_weight,
        down_weight,
    ):
        micro_count, rows, width = inputs.shape
        block = width // n
        tokens = micro_count * rows
        q_cols, k_cols = query_weight.shape[1], key_matrix.shape[1]
        local_heads, local_groups = q_cols // HEAD_SIZE, k_cols // HEAD_SIZE
        group_width = local_heads // local_groups
        score_scale = 1.0 / math.sqrt(HEAD_SIZE)
        me, mine = lax.axis_index("dp"), lax.axis_index("mp")
        low = (me // pair) % 2
        is_low = low == 0

        def place_of(position):
            index = jnp.int32(0)
            for axis, bit in enumerate(main_order):
                digit = (position >> axis) & 1
                if bit == pair:
                    index = index + digit * bit
                else:
                    index = index + (((me // bit) % 2 + digit) % 2) * bit
            return index

        def position_of(index):
            position = jnp.int32(0)
            for axis, bit in enumerate(main_order):
                digit = 1 if index & bit else 0
                if bit == pair:
                    position = position + (digit << axis)
                else:
                    position = position + (((me // bit) % 2 + digit) % 2) * (1 << axis)
            return position

        def to_relative(array):
            pieces = [
                lax.dynamic_slice_in_dim(array, place_of(p) * block, block, array.ndim - 1)
                for p in range(n)
            ]
            return jnp.concatenate(pieces, axis=-1)

        def from_relative(array):
            pieces = [
                lax.dynamic_slice_in_dim(array, position_of(j) * block, block, array.ndim - 1)
                for j in range(n)
            ]
            return jnp.concatenate(pieces, axis=-1)

        def own_first(array):
            return jnp.stack(
                [
                    lax.dynamic_index_in_dim(array, mine, 0, False),
                    lax.dynamic_index_in_dim(array, 1 - mine, 0, False),
                ]
            )

        def micro_order(array):
            return jnp.stack(
                [
                    lax.dynamic_index_in_dim(array, mine, 0, False),
                    lax.dynamic_index_in_dim(array, 1 - mine, 0, False),
                ]
            )

        def paired(array, other):
            return jnp.stack(
                [jnp.where(is_low, array, other), jnp.where(is_low, other, array)]
            )

        def gather_whole(shard, order):
            array, axes = shard, []
            for bit in order:
                other = swap(array, bit)
                array = paired(array, other) if bit == pair else jnp.stack([array, other])
                axes = [bit] + axes
            wanted = main_order[::-1]
            array = array.transpose([axes.index(b) for b in wanted] + [len(axes), len(axes) + 1])
            return array.reshape(width, shard.shape[1])

        def gather_half(shard):
            half = shard.shape[1] // 2
            keep = lax.dynamic_slice_in_dim(shard, low * half, half, 1)
            send = lax.dynamic_slice_in_dim(shard, (1 - low) * half, half, 1)
            array = paired(keep, swap(send, pair)).reshape(2 * block, half)
            for bit in others:
                array = jnp.concatenate([array, swap(array, bit)], axis=0)
            return array

        def first_stage(left, right):
            middle = width // 2
            send = dot(left[:, middle:], right, 0, 0).astype(BF16)
            other = swap(send, 1)
            return (dot(left[:, :middle], right, 0, 0) + other.astype(F32)).astype(BF16)

        def scatter_whole(array, order):
            columns = array.shape[1]
            bits = main_order[:-1][::-1]
            array = array.reshape([2] * len(bits) + [block, columns])
            left = list(bits)
            for bit in [b for b in order[::-1] if b != 1]:
                axis = left.index(bit)
                if bit == pair:
                    keep = lax.dynamic_index_in_dim(array, low, axis, False)
                    send = lax.dynamic_index_in_dim(array, 1 - low, axis, False)
                else:
                    keep = lax.index_in_dim(array, 0, axis, False)
                    send = lax.index_in_dim(array, 1, axis, False)
                array = add_low(keep, swap(send, bit))
                left.pop(axis)
            return array

        def scatter_half(array):
            for bit in others[::-1]:
                if bit == 1:
                    continue
                middle = array.shape[0] // 2
                array = add_low(array[:middle], swap(array[middle:], bit))
            array = array.reshape(2, block, array.shape[1])
            keep = lax.dynamic_index_in_dim(array, low, 0, False)
            other = swap(lax.dynamic_index_in_dim(array, 1 - low, 0, False), pair)
            return jnp.where(
                is_low,
                jnp.concatenate([keep, other], axis=1),
                jnp.concatenate([other, keep], axis=1),
            ).astype(F32)

        def gather_gains(shards):
            array = shards
            for bit in main_order:
                other = swap(array, bit)
                array = paired(array, other) if bit == pair else jnp.stack([array, other])
            array = array.reshape(n, shards.shape[0], block)
            return array.transpose(1, 0, 2).reshape(shards.shape[0], width)

        def scatter_gain(gradient):
            array = gradient.reshape([2] * len(main_order) + [block])
            array = array + swap_mp(array)
            for bit in main_order[::-1]:
                if bit == pair:
                    keep = lax.dynamic_index_in_dim(array, low, 0, False)
                    send = lax.dynamic_index_in_dim(array, 1 - low, 0, False)
                else:
                    keep, send = array[0], array[1]
                array = keep + swap(send, bit)
            return array

        def gather_square(own):
            middle = rows // 2
            by_mp, by_pair = swap_mp(own), swap(own, pair)
            first = swap_mp(by_pair[:middle])
            second = swap(by_mp[middle:], pair)
            return jnp.concatenate([own, by_mp, by_pair, first, second], axis=0)

        def scatter_square(own, by_mp, by_pair, both):
            middle = rows // 2
            first = swap(both[:middle], pair)
            second = swap_mp(both[middle:])
            to_mp = jnp.concatenate([add_low(by_mp[:middle], first), by_mp[middle:]], axis=0)
            to_pair = jnp.concatenate([by_pair[:middle], add_low(by_pair[middle:], second)], axis=0)
            return own.astype(F32) + swap_mp(to_mp).astype(F32) + swap(to_pair, pair).astype(F32)

        attn_low = jnp.concatenate([query_weight, key_matrix, value_matrix], axis=1)
        half_cols = attn_low.shape[1] // 2
        gains = gather_gains(jnp.stack([attn_gain, mlp_gain])).astype(F32)
        attn_scale, mlp_scale = gains[0], gains[1]
        qkv_full = jnp.concatenate(
            [
                gather_whole(attn_low[:, :half_cols], main_order),
                gather_whole(attn_low[:, half_cols:], other_order),
            ],
            axis=1,
        )
        out_full = gather_whole(out_weight.T, main_order)
        gate_full = gather_half(gate_weight)
        up_full = gather_half(up_weight)
        down_full = gather_half(down_weight.T)

        cot = to_relative(own_first(cotangent))
        cot_pair = swap(cot[0], pair)
        cot_both = swap_mp(cot_pair)
        cot_all = jnp.concatenate([cot[0], cot[1], cot_pair, cot_both], axis=0)

        rows_in = to_relative(own_first(inputs)).astype(F32).reshape(tokens, width)
        starts = own_first(seq_starts)
        local_pos = jnp.arange(rows, dtype=jnp.int32)
        positions = me * rows + local_pos[None] - starts
        cosine_lookup, sine_lookup = rope_tables(positions.reshape(tokens), HEAD_SIZE)
        allowed = (starts[:, :, None] == starts[:, None, :]) & (
            local_pos[:, None] >= local_pos[None, :]
        )
        normed_one, inverse_one, scaled_one = rms_parts(rows_in, attn_scale)
        first_hidden = scaled_one.astype(BF16)
        qkv = dot(first_hidden, qkv_full, 1, 0)
        query_raw = qkv[:, :q_cols].reshape(tokens, local_heads, HEAD_SIZE)
        key_raw = qkv[:, q_cols : q_cols + k_cols].reshape(tokens, local_groups, HEAD_SIZE)
        query_rot = rotate_half(query_raw, cosine_lookup, sine_lookup, 1.0).astype(BF16)
        key_rot = rotate_half(key_raw, cosine_lookup, sine_lookup, 1.0).astype(BF16)
        key_rot = key_rot.reshape(micro_count, rows, local_groups, HEAD_SIZE)
        value_rows = (
            qkv[:, q_cols + k_cols :]
            .astype(BF16)
            .reshape(micro_count, rows, local_groups, HEAD_SIZE)
        )
        grouped = query_rot.reshape(micro_count, rows, local_groups, group_width, HEAD_SIZE)
        scores = (
            jnp.einsum("bqkgd,bskd->bkgqs", grouped, key_rot, preferred_element_type=F32)
            * score_scale
        )
        scores = jnp.where(allowed[:, None, None], scores, -1e30)
        expo = jnp.exp(scores - jnp.max(scores, axis=-1, keepdims=True))
        probs = expo / jnp.sum(expo, axis=-1, keepdims=True)
        probs_low = probs.astype(BF16)
        attended = jnp.einsum(
            "bkgqs,bskd->bqkgd", probs_low, value_rows, preferred_element_type=F32
        )
        attended = attended.reshape(tokens, q_cols).astype(BF16)
        branch_other = dot(attended[rows:], out_full, 1, 1).astype(BF16)
        branch_own = dot(attended[:rows], out_full, 1, 1)
        after = rows_in[:rows] + branch_own + swap_mp(branch_other).astype(F32)

        normed_two, inverse_two, scaled_two = rms_parts(after, mlp_scale)
        hidden_two = gather_square(scaled_two.astype(BF16))
        gate_val = dot(hidden_two, gate_full, 1, 0)
        up_val = dot(hidden_two, up_full, 1, 0)
        sigmoid_gate = jax.nn.sigmoid(gate_val)
        activated = gate_val * sigmoid_gate
        mixed = (activated * up_val).astype(BF16)
        grad_down = first_stage(cot_all, mixed)

        grad_mixed = dot(cot_all, down_full, 1, 0)
        grad_gate_act = (
            grad_mixed * up_val * (sigmoid_gate * (1.0 + gate_val * (1.0 - sigmoid_gate)))
        ).astype(BF16)
        grad_up_act = (grad_mixed * activated).astype(BF16)
        grad_two = (dot(grad_gate_act, gate_full, 1, 1) + dot(grad_up_act, up_full, 1, 1)).astype(
            BF16
        )
        grad_two = grad_two.reshape(4, rows, width)
        grad_hidden_two = scatter_square(*[grad_two[i] for i in range(4)])
        grad_gate = first_stage(hidden_two, grad_gate_act)
        grad_up = first_stage(hidden_two, grad_up_act)

        branch_two = dot(mixed, down_full, 1, 1).astype(BF16).reshape(4, rows, width)
        result = (after + scatter_square(*[branch_two[i] for i in range(4)])).astype(BF16)
        output = from_relative(micro_order(jnp.stack([result, swap_mp(result)])))

        gain_two = jnp.sum(grad_hidden_two * normed_two, axis=0)
        grad_after = cot[0].astype(F32) + rms_back(
            grad_hidden_two, normed_two, inverse_two, mlp_scale
        )
        grad_branch_own = grad_after.astype(BF16)
        grad_branch = jnp.concatenate([grad_branch_own, swap_mp(grad_branch_own)], axis=0)

        grad_out = first_stage(grad_branch, attended)
        grad_attended = dot(grad_branch, out_full, 1, 0).astype(BF16)
        grad_attended = grad_attended.reshape(
            micro_count, rows, local_groups, group_width, HEAD_SIZE
        )
        grad_probs = jnp.einsum(
            "bqkgd,bskd->bkgqs", grad_attended, value_rows, preferred_element_type=F32
        )
        row_inner = jnp.sum(probs * grad_probs, axis=-1, keepdims=True)
        grad_scores = (probs * (grad_probs - row_inner)).astype(BF16)
        grad_query_rot = (
            jnp.einsum("bkgqs,bskd->bqkgd", grad_scores, key_rot, preferred_element_type=F32)
            * score_scale
        )
        grad_key_rot = (
            jnp.einsum("bkgqs,bqkgd->bskd", grad_scores, grouped, preferred_element_type=F32)
            * score_scale
        )
        grad_value_rows = jnp.einsum(
            "bkgqs,bqkgd->bskd", probs_low, grad_attended, preferred_element_type=F32
        )
        grad_queries = rotate_half(
            grad_query_rot.reshape(tokens, local_heads, HEAD_SIZE),
            cosine_lookup,
            sine_lookup,
            -1.0,
        ).reshape(tokens, q_cols)
        grad_keys = rotate_half(
            grad_key_rot.reshape(tokens, local_groups, HEAD_SIZE),
            cosine_lookup,
            sine_lookup,
            -1.0,
        ).reshape(tokens, k_cols)
        grad_qkv = jnp.concatenate(
            [
                grad_queries.astype(BF16),
                grad_keys.astype(BF16),
                grad_value_rows.reshape(tokens, k_cols).astype(BF16),
            ],
            axis=1,
        )
        grad_one_part = dot(grad_qkv, qkv_full, 1, 1).astype(BF16)
        one_other = swap_mp(grad_one_part)
        one_other = jnp.concatenate([one_other[rows:], one_other[:rows]], axis=0)
        grad_hidden_one = grad_one_part.astype(F32) + one_other.astype(F32)
        grad_attn_low = first_stage(first_hidden, grad_qkv)
        grad_after_all = jnp.concatenate([grad_branch[:rows], grad_branch[rows:]], axis=0)
        input_grad = grad_after_all.astype(F32) + rms_back(
            grad_hidden_one, normed_one, inverse_one, attn_scale
        )
        input_grad = from_relative(micro_order(input_grad.reshape(micro_count, rows, width)))
        gain_one = jnp.sum(grad_one_part.astype(F32) * normed_one, axis=0)

        grad_down = scatter_half(grad_down)
        grad_gate = scatter_half(grad_gate)
        grad_up = scatter_half(grad_up)
        grad_out = scatter_whole(grad_out, main_order).astype(F32)
        grad_attn = jnp.concatenate(
            [
                scatter_whole(grad_attn_low[:, :half_cols], main_order),
                scatter_whole(grad_attn_low[:, half_cols:], other_order),
            ],
            axis=1,
        ).astype(F32)
        return (
            output,
            input_grad,
            scatter_gain(gain_one),
            grad_attn[:, :q_cols],
            grad_attn[:, q_cols : q_cols + k_cols],
            grad_attn[:, q_cols + k_cols :],
            grad_out.T,
            scatter_gain(gain_two),
            grad_gate,
            grad_up,
            grad_down.T,
        )

    return per_device


def solution(mesh):
    in_specs = (
        P(None, "dp", None),
        P(None, "dp"),
        P(None, "dp", None),
        P("dp"),
        P("dp", "mp"),
        P("dp", "mp"),
        P("dp", "mp"),
        P("mp", "dp"),
        P("dp"),
        P("dp", "mp"),
        P("dp", "mp"),
        P("mp", "dp"),
    )
    out_specs = (
        P(None, "dp", None),
        P(None, "dp", None),
        P("dp"),
        P("dp", "mp"),
        P("dp", "mp"),
        P("dp", "mp"),
        P("mp", "dp"),
        P("dp"),
        P("dp", "mp"),
        P("dp", "mp"),
        P("mp", "dp"),
    )
    return jax.shard_map(
        make_per_device(mesh.shape["dp"]),
        mesh=mesh,
        in_specs=in_specs,
        out_specs=out_specs,
        check_vma=False,
    )
```

```python
import functools
import math

import jax
import jax.numpy as jnp
from jax import lax
from jax.experimental import pallas as pl
from jax.experimental.pallas import tpu as pltpu
from jax.sharding import PartitionSpec as P

HEAD_SIZE = 64
LANES = 2 * HEAD_SIZE
EPSILON = 1e-05
F32 = jnp.float32
BF16 = jnp.bfloat16
PIECES = 4
VMEM_LIMIT = 56 << 20
TIME_BYTES = 1_000


def dot(left, right, left_dim, right_dim):
    return lax.dot_general(
        left, right, (((left_dim,), (right_dim,)), ((), ())), preferred_element_type=F32
    )


def add_low(left, right):
    return (left.astype(F32) + right.astype(F32)).astype(BF16)


def rope_tables(positions):
    halfway = HEAD_SIZE // 2
    lane = jnp.arange(LANES, dtype=jnp.int32)
    frequency = 500000.0 ** (-((lane % halfway).astype(F32) * 2.0 / HEAD_SIZE))
    angles = positions.astype(F32)[..., None] * frequency
    sign = jnp.where(lane % HEAD_SIZE < halfway, -1.0, 1.0)
    return (jnp.cos(angles), jnp.sin(angles) * sign)


def kernel_call(kernel, grid, ins, outs, scalars=(), scratch=(), time=2):
    return pl.pallas_call(
        kernel,
        grid_spec=pltpu.PrefetchScalarGridSpec(
            num_scalar_prefetch=len(scalars),
            grid=grid,
            in_specs=[pl.BlockSpec(block, place) for _, block, place in ins],
            out_specs=[pl.BlockSpec(block, place) for _, _, block, place in outs],
            scratch_shapes=list(scratch),
        ),
        out_shape=[jax.ShapeDtypeStruct(shape, kind) for shape, kind, _, _ in outs],
        compiler_params=pltpu.CompilerParams(vmem_limit_bytes=VMEM_LIMIT),
        cost_estimate=pl.CostEstimate(
            flops=1, bytes_accessed=int(time * TIME_BYTES), transcendentals=0
        ),
    )(*scalars, *[array for array, _, _ in ins])


def whole(array):
    return (array, array.shape, lambda *_: (0,) * array.ndim)


def by_rows(array, rows):
    return (array, (rows,) + array.shape[1:], lambda i, *_: (i,) + (0,) * (array.ndim - 1))


def by_columns(array, columns):
    return (array, (array.shape[0], columns), lambda j, *_: (0, j))


def turn_lanes(pair_rows):
    lane = lax.broadcasted_iota(jnp.int32, pair_rows.shape, 1)
    up = pltpu.roll(pair_rows, LANES - HEAD_SIZE // 2, 1)
    down = pltpu.roll(pair_rows, HEAD_SIZE // 2, 1)
    return jnp.where(lane % HEAD_SIZE < HEAD_SIZE // 2, up, down)


def doubled(pair_rows, second):
    lane = lax.broadcasted_iota(jnp.int32, pair_rows.shape, 1)
    other = pltpu.roll(pair_rows, HEAD_SIZE, 1)
    return jnp.where((lane < HEAD_SIZE) != second, pair_rows, other)


def half_lanes(pair_rows, second):
    lane = lax.broadcasted_iota(jnp.int32, pair_rows.shape, 1)
    return jnp.where((lane < HEAD_SIZE) != second, pair_rows, jnp.zeros_like(pair_rows))


def allowed_pairs(start_col_ref, start_row_ref):
    rows = start_col_ref.shape[1]
    shape = (rows, rows)
    before = lax.broadcasted_iota(jnp.int32, shape, 1) <= lax.broadcasted_iota(jnp.int32, shape, 0)
    return (start_col_ref[0] == start_row_ref[0]) & before


def head_probs(query, key, allowed):
    scores = dot(query, key, 1, 1) * (1.0 / math.sqrt(HEAD_SIZE))
    scores = jnp.where(allowed, scores, -1e30)
    expo = jnp.exp(scores - jnp.max(scores, axis=-1, keepdims=True))
    return expo / jnp.sum(expo, axis=-1, keepdims=True)


def times_pieces(left, refs, columns):
    total = None
    depth = refs[0].shape[0]
    for p, ref in enumerate(refs):
        part = dot(left[:, p * depth : (p + 1) * depth], ref[:, :columns], 1, 0)
        total = part if total is None else total + part
    return total


def attend(q_cols, k_cols, raw_ref, cosine, sine, allowed, rot_ref, out_ref):
    group_width = q_cols // k_cols

    def rope(at):
        rows = raw_ref[:, at : at + LANES]
        return (rows * cosine + turn_lanes(rows) * sine).astype(BF16)

    for kv in range(k_cols // LANES):
        k_at, v_at = q_cols + kv * LANES, q_cols + k_cols + kv * LANES
        key = rope(k_at)
        value = raw_ref[:, v_at : v_at + LANES].astype(BF16)
        rot_ref[:, k_at : k_at + LANES] = key
        rot_ref[:, v_at : v_at + LANES] = value
        for group in (0, 1):
            key_two, value_two = doubled(key, group == 1), doubled(value, group == 1)
            for pair in range(group_width // 2):
                at = ((kv * 2 + group) * group_width + 2 * pair) * HEAD_SIZE
                query = rope(at)
                rot_ref[:, at : at + LANES] = query
                parts = []
                for second in (False, True):
                    probs = head_probs(half_lanes(query, second), key_two, allowed)
                    parts.append(dot(probs.astype(BF16), value_two, 1, 0))
                lane = lax.broadcasted_iota(jnp.int32, parts[0].shape, 1)
                out_ref[:, at : at + LANES] = jnp.where(lane < HEAD_SIZE, *parts).astype(BF16)


def attend_back(q_cols, k_cols, rot_ref, grad_ref, cosine, sine, allowed, out_ref):
    group_width = q_cols // k_cols
    scale = 1.0 / math.sqrt(HEAD_SIZE)

    def unrope(rows):
        return (rows * cosine - turn_lanes(rows) * sine).astype(BF16)

    def folded(rows):
        return rows + pltpu.roll(rows, HEAD_SIZE, 1)

    for kv in range(k_cols // LANES):
        k_at, v_at = q_cols + kv * LANES, q_cols + k_cols + kv * LANES
        key, value = rot_ref[:, k_at : k_at + LANES], rot_ref[:, v_at : v_at + LANES]
        grad_keys, grad_values = [], []
        for group in (0, 1):
            key_two, value_two = doubled(key, group == 1), doubled(value, group == 1)
            grad_key = jnp.zeros(key.shape, F32)
            grad_value = jnp.zeros(key.shape, F32)
            for pair in range(group_width // 2):
                at = ((kv * 2 + group) * group_width + 2 * pair) * HEAD_SIZE
                query, grad = rot_ref[:, at : at + LANES], grad_ref[:, at : at + LANES]
                parts = []
                for second in (False, True):
                    query_one, grad_one = half_lanes(query, second), half_lanes(grad, second)
                    probs = head_probs(query_one, key_two, allowed)
                    grad_probs = dot(grad_one, value_two, 1, 1)
                    inner = jnp.sum(probs * grad_probs, axis=-1, keepdims=True)
                    grad_scores = (probs * (grad_probs - inner)).astype(BF16)
                    parts.append(dot(grad_scores, key_two, 1, 0))
                    grad_key = grad_key + dot(grad_scores, query_one, 0, 0)
                    grad_value = grad_value + dot(probs.astype(BF16), grad_one, 0, 0)
                lane = lax.broadcasted_iota(jnp.int32, parts[0].shape, 1)
                out_ref[:, at : at + LANES] = unrope(jnp.where(lane < HEAD_SIZE, *parts) * scale)
            grad_keys.append(folded(grad_key) * scale)
            grad_values.append(folded(grad_value))
        lane = lax.broadcasted_iota(jnp.int32, key.shape, 1)
        out_ref[:, k_at : k_at + LANES] = unrope(jnp.where(lane < HEAD_SIZE, *grad_keys))
        out_ref[:, v_at : v_at + LANES] = jnp.where(lane < HEAD_SIZE, *grad_values).astype(BF16)


def move_rows(table_ref, count, in_ref, store):
    block = in_ref.shape[-1] // count
    for p in range(count):
        at = pl.multiple_of(table_ref[p] * block, block)
        store(p * block, in_ref[0, :, pl.ds(at, block)])


def move_kernel(count, table_ref, in_ref, out_ref):
    def store(at, rows):
        out_ref[0, :, at : at + rows.shape[1]] = rows.astype(out_ref.dtype)

    move_rows(table_ref, count, in_ref, store)


def move_blocks(array, table, mine, kind):
    micro_count, rows, width = array.shape
    count = table.shape[0]
    block = width // count
    if block % 128:
        array = jnp.roll(array, -mine, axis=0)
        pieces = [
            lax.dynamic_slice_in_dim(array, table[p] * block, block, 2) for p in range(count)
        ]
        return jnp.concatenate(pieces, axis=-1).astype(kind)
    return kernel_call(
        functools.partial(move_kernel, count),
        (micro_count,),
        [(array, (1, rows, width), lambda i, t: ((i + t[count]) % micro_count, 0, 0))],
        [(array.shape, kind, (1, rows, width), lambda i, t: (i, 0, 0))],
        scalars=(jnp.concatenate([table, mine[None]]),),
    )[0]


def attend_kernel(count, q_cols, k_cols, table_ref, in_ref, *refs):
    weights, refs = refs[:PIECES], refs[PIECES:]
    cos_ref, sin_ref, col_ref, row_ref = refs[:4]
    rows_ref, hidden_ref, rot_ref, out_ref, gains_ref, raw_ref = refs[4:]
    step = pl.program_id(0)
    columns = q_cols + 2 * k_cols
    depth = weights[0].shape[0]

    @pl.when(step == 0)
    def _():
        shape = (8, 128)
        pick = lax.broadcasted_iota(jnp.int32, shape, 0) == lax.broadcasted_iota(jnp.int32, shape, 1)
        for p, ref in enumerate(weights):
            gains_ref[:, p * depth : (p + 1) * depth] = dot(
                pick.astype(F32).astype(BF16), ref[:, columns:], 1, 1
            )

    def store(at, rows):
        rows_ref[:, at : at + rows.shape[1]] = rows

    if count:
        move_rows(table_ref, count, in_ref, store)
    else:
        rows_ref[...] = in_ref[0]
    rows = rows_ref[...].astype(F32)
    inverse = lax.rsqrt(jnp.mean(rows * rows, axis=-1, keepdims=True) + EPSILON)
    hidden = (rows * inverse * gains_ref[0:1, :]).astype(BF16)
    hidden_ref[...] = hidden
    raw_ref[...] = times_pieces(hidden, weights, columns)
    attend(
        q_cols,
        k_cols,
        raw_ref,
        cos_ref[...],
        sin_ref[...],
        allowed_pairs(col_ref, row_ref),
        rot_ref,
        out_ref,
    )


def attend_back_kernel(q_cols, k_cols, own_ref, other_ref, *refs):
    outs, weights, refs = refs[:PIECES], refs[PIECES : 2 * PIECES], refs[2 * PIECES :]
    rot_ref, cos_ref, sin_ref, col_ref, row_ref, branch_ref, qkv_ref, one_ref, grad_ref = refs
    step = pl.program_id(0)
    columns = q_cols + 2 * k_cols
    for i, ref in enumerate((own_ref, other_ref)):

        @pl.when(step == i)
        def _(ref=ref):
            branch_ref[...] = ref[...]

    grad_ref[...] = times_pieces(branch_ref[...], outs, q_cols).astype(BF16)
    attend_back(
        q_cols,
        k_cols,
        rot_ref,
        grad_ref,
        cos_ref[...],
        sin_ref[...],
        allowed_pairs(col_ref, row_ref),
        qkv_ref,
    )
    depth = weights[0].shape[0]
    for p, ref in enumerate(weights):
        one_ref[:, p * depth : (p + 1) * depth] = dot(
            qkv_ref[...], ref[:, :columns], 1, 1
        ).astype(BF16)


def gate_kernel(own_ref, mp_ref, pair_ref, first_ref, second_ref, *refs):
    weights, (all_ref, gate_ref) = refs[:PIECES], refs[PIECES:]
    rows, middle = own_ref.shape[0], first_ref.shape[0]

    @pl.when(pl.program_id(0) == 0)
    def _():
        for i, ref in enumerate((own_ref, mp_ref, pair_ref)):
            all_ref[i * rows : (i + 1) * rows, :] = ref[...]
        all_ref[3 * rows : 3 * rows + middle, :] = first_ref[...]
        all_ref[3 * rows + middle :, :] = second_ref[...]

    gate_ref[...] = times_pieces(all_ref[...], weights, gate_ref.shape[1]).astype(BF16)


def up_kernel(all_ref, *refs):
    weights, (gate_ref, up_ref, mixed_ref) = refs[:PIECES], refs[PIECES:]
    up = times_pieces(all_ref[...], weights, up_ref.shape[1])
    gate = gate_ref[...].astype(F32)
    up_ref[...] = up.astype(BF16)
    mixed_ref[...] = (gate * jax.nn.sigmoid(gate) * up).astype(BF16)


def mixed_back_kernel(cot_ref, *refs):
    weights, (gate_ref, up_ref, grad_gate_ref, grad_up_ref) = refs[:PIECES], refs[PIECES:]
    grad = times_pieces(cot_ref[...], weights, gate_ref.shape[1])
    gate = gate_ref[...].astype(F32)
    sigmoid = jax.nn.sigmoid(gate)
    inner = sigmoid * (1.0 + gate * (1.0 - sigmoid))
    grad_gate_ref[...] = (grad * up_ref[...].astype(F32) * inner).astype(BF16)
    grad_up_ref[...] = (grad * (gate * sigmoid)).astype(BF16)


def branch_kernel(per_piece, left_ref, *refs):
    weights, (own_ref, other_ref) = refs[:PIECES], refs[PIECES:]
    rows = own_ref.shape[0]
    for p in range(PIECES):

        @pl.when(pl.program_id(0) // per_piece == p)
        def _(p=p):
            total = dot(left_ref[...], weights[p][...], 1, 1).astype(BF16)
            own_ref[...] = total[:rows]
            other_ref[...] = total[rows:]


def back_kernel(per_piece, sides, *refs):
    lefts, refs = refs[:sides], refs[sides:]
    weights, (own_ref, mp_one, pair_one, mp_two, pair_two) = (
        refs[: sides * PIECES],
        refs[sides * PIECES :],
    )
    rows = own_ref.shape[0]
    middle = rows // 2
    for p in range(PIECES):

        @pl.when(pl.program_id(0) // per_piece == p)
        def _(p=p):
            total = None
            for s in range(sides):
                part = dot(lefts[s][...], weights[s * PIECES + p][...], 1, 1)
                total = part if total is None else total + part
            total = total.astype(BF16)
            own_ref[...] = total[:rows]
            mp_two[...] = total[rows : rows + middle]
            mp_one[:middle, :] = total[rows + middle : 2 * rows]
            pair_one[:middle, :] = total[2 * rows : 2 * rows + middle]
            pair_two[...] = total[2 * rows + middle : 3 * rows]
            pair_one[middle:, :] = total[3 * rows : 3 * rows + middle]
            mp_one[middle:, :] = total[3 * rows + middle :]


def times_back(sides, rows):
    depth = sides[0][1][0].shape[0]
    columns = min(depth, 256)
    per_piece = depth // columns
    ins = [whole(left) for left, _ in sides]
    for _, pieces in sides:
        for p, piece in enumerate(pieces):

            def place(j, p=p):
                return (jnp.clip(j - p * per_piece, 0, per_piece - 1), 0)

            ins.append((piece, (columns, piece.shape[1]), place))
    width = depth * PIECES
    heights = (rows, rows, rows, rows // 2, rows // 2)
    if sides[0][0].shape[0] == 2 * rows:
        heights = (rows, rows)
    kernel = functools.partial(back_kernel, per_piece, len(sides))
    if len(heights) == 2:
        kernel = functools.partial(branch_kernel, per_piece)
    return kernel_call(
        kernel,
        (PIECES * per_piece,),
        ins,
        [((h, width), BF16, (h, columns), lambda j: (0, j)) for h in heights],
                time=7 * len(sides) * sides[0][0].shape[1] / 1024,
            )


def forward_norm_kernel(rows_ref, own_ref, other_ref, gains_ref, after_ref, hidden_ref):
    branch = own_ref[...].astype(F32) + other_ref[...].astype(F32)
    result = rows_ref[...].astype(F32) + branch
    after_ref[...] = result
    square = jnp.mean(result * result, axis=-1, keepdims=True)
    normed = result * lax.rsqrt(square + EPSILON)
    hidden_ref[...] = (normed * gains_ref[1:2, :]).astype(BF16)


def add_kernel(rows_ref, own_ref, pair_one, mp_two, mp_one, pair_two, out_ref):
    step = pl.program_id(0)
    for i, extra in enumerate(((pair_one, mp_two), (mp_one, pair_two))):

        @pl.when(step == i)
        def _(extra=extra):
            branch = own_ref[...].astype(F32)
            branch = branch + (extra[0][...].astype(F32) + extra[1][...].astype(F32))
            out_ref[...] = (rows_ref[...].astype(F32) + branch).astype(BF16)


def norm_back_kernel(gain_row, values_ref, passed_ref, *refs):
    own_ref, pair_one, mp_two, mp_one, pair_two, gains_ref = refs[:6]
    full_ref, low_ref, gain_ref = refs[6:]
    step = pl.program_id(0)

    @pl.when(step == 0)
    def _():
        gain_ref[...] = jnp.zeros_like(gain_ref)

    for i, extra in enumerate(((pair_one, mp_two), (mp_one, pair_two))):

        @pl.when(step == i)
        def _(extra=extra):
            grad = own_ref[...].astype(F32)
            grad = grad + (extra[0][...].astype(F32) + extra[1][...].astype(F32))
            values = values_ref[...].astype(F32)
            square = jnp.mean(values * values, axis=-1, keepdims=True)
            inverse = lax.rsqrt(square + EPSILON)
            normed = values * inverse
            scaled = grad * gains_ref[gain_row : gain_row + 1, :]
            inner = jnp.mean(scaled * normed, axis=-1, keepdims=True)
            result = passed_ref[...].astype(F32) + inverse * (scaled - normed * inner)
            full_ref[...] = result
            low_ref[...] = result.astype(BF16)
            gain_ref[0:1, :] += jnp.sum(grad * normed, axis=0, keepdims=True)


def last_norm_back_kernel(values_ref, passed_ref, part_ref, other_ref, gains_ref, *refs):
    out_ref, gain_ref = refs

    @pl.when(pl.program_id(0) == 0)
    def _():
        gain_ref[...] = jnp.zeros_like(gain_ref)

    grad = part_ref[...].astype(F32) + other_ref[...].astype(F32)
    values = values_ref[...].astype(F32)
    inverse = lax.rsqrt(jnp.mean(values * values, axis=-1, keepdims=True) + EPSILON)
    normed = values * inverse
    scaled = grad * gains_ref[0:1, :]
    inner = jnp.mean(scaled * normed, axis=-1, keepdims=True)
    out_ref[...] = passed_ref[...].astype(F32) + inverse * (scaled - normed * inner)
    gain_ref[0:1, :] += jnp.sum(grad * normed, axis=0, keepdims=True)


def send_kernel(left_ref, right_ref, out_ref):
    out_ref[...] = dot(left_ref[...], right_ref[...], 0, 0).astype(BF16)


def keep_kernel(left_ref, right_ref, other_ref, low_ref, high_ref):
    total = dot(left_ref[...], right_ref[...], 0, 0) + other_ref[...].astype(F32)
    middle = low_ref.shape[0]
    low_ref[...] = total[:middle].astype(BF16)
    high_ref[...] = total[middle:].astype(BF16)


def transpose_kernel(in_ref, out_ref):
    out_ref[...] = in_ref[...].T


def transposed(array):
    rows, columns = array.shape
    if columns % 128:
        return array.T
    return kernel_call(
        transpose_kernel,
        (rows // 512,),
        [(array, (512, columns), lambda i: (i, 0))],
        [((columns, rows), array.dtype, (columns, 512), lambda i: (0, i))],
    )[0]


def owned_kernel(steps, flip, in_ref, out_ref):
    parts = [in_ref[i].astype(F32) for i in range(4)]

    def put(total):
        out_ref[...] = total.T if flip else total

    if steps is None:
        put((parts[0] + parts[2]) + (parts[1] + parts[3]))
        return
    for side in (0, 1):

        @pl.when(pl.program_id(0) // steps == side)
        def _(side=side):
            put(parts[side] + parts[side + 2])


def owned(array, block, halves, flip):
    columns = array.shape[1]
    array = array.reshape(4, block, columns)
    if block % 128:
        parts = array.astype(F32)
        total = (parts[0] + parts[2], parts[1] + parts[3])
        total = jnp.concatenate(total, axis=1) if halves else total[0] + total[1]
        return total.T if flip else total
    step = min(columns, 2048)
    steps = columns // step
    count = 2 * steps if halves else steps
    shape, part = (block, step * count), (block, step)
    place = lambda j: (0, j)
    if flip:
        shape, part, place = shape[::-1], part[::-1], lambda j: (j, 0)
    return kernel_call(
        functools.partial(owned_kernel, steps if halves else None, flip),
        (count,),
        [(array, (4, block, step), lambda j: (0, 0, j % steps))],
        [(shape, F32, part, place)],
        time=3,
    )[0]


def after(array, *earlier):
    return lax.optimization_barrier((array, *earlier))[0]


def make_per_device(n):
    pair = 4 if n <= 16 else 8
    others = [1 << b for b in reversed(range(n.bit_length() - 1))]
    others = [v for v in others if v not in (pair, 2 * pair)]
    main_order = [pair, 2 * pair] + others
    z_groups = [[i | z * pair for z in range(4)] for i in range(n) if not i & (3 * pair)]

    def swap(array, bit):
        return lax.ppermute(array, "dp", [(i, i ^ bit) for i in range(n)])

    def swap_mp(array):
        return lax.ppermute(array, "mp", [(0, 1), (1, 0)])

    def along_z(array):
        return lax.all_to_all(array, "dp", 0, 0, axis_index_groups=z_groups, tiled=True)

    def per_device(
        inputs,
        seq_starts,
        cotangent,
        attn_gain,
        query_weight,
        key_matrix,
        value_matrix,
        out_weight,
        mlp_gain,
        gate_weight,
        up_weight,
        down_weight,
    ):
        micro_count, rows, width = inputs.shape
        middle = rows // 2
        block = width // n
        tokens, pair_tokens = micro_count * rows, 2 * micro_count * rows
        q_cols, k_cols = query_weight.shape[1], key_matrix.shape[1]
        qkv_cols = q_cols + 2 * k_cols
        hidden_cols = gate_weight.shape[1] // 2
        me, mine = lax.axis_index("dp"), lax.axis_index("mp")

        def table(natural):
            entries = []
            for p in range(n):
                entry = jnp.int32(0)
                for axis, bit in enumerate(main_order):
                    digit, weight = ((p // bit) % 2, 1 << axis) if natural else ((p >> axis) % 2, bit)
                    if bit in others:
                        digit = ((me // bit) % 2 + digit) % 2
                    entry = entry + digit * weight
                entries.append(entry)
            return jnp.stack(entries)

        to_table, from_table = table(False), table(True)

        def own_first(array):
            return jnp.where(mine == 0, array, jnp.flip(array, 0))

        window = []

        def close(*results):
            window[:] = results

        def go(array):
            return after(array, *window) if window else array

        def gather_z(first, second):
            return along_z(go(jnp.concatenate([first, second, first, second], axis=0)))

        def gather_y(array):
            pieces = [array]
            for bit in others[:-1]:
                pieces = pieces + [swap(go(piece), bit) for piece in pieces]
            return pieces

        def gather_core(pieces):
            pieces = pieces + [swap(go(piece), 1) for piece in pieces]
            share = len(pieces) // PIECES
            if share > 1:
                pieces = [
                    jnp.concatenate(pieces[i * share : (i + 1) * share]) for i in range(PIECES)
                ]
            return pieces

        def halves(shard):
            return jnp.split(shard, 2, axis=1)

        def stage_columns(left, right):
            count = right.shape[1]
            columns = count if count < 1024 else 512
            grid = (count // columns,)
            return left.shape[0], count, columns, grid, by_columns(right, columns)

        def for_core(left, right):
            depth, count, columns, grid, right = stage_columns(left, go(right))
            height = width // 2
            return kernel_call(
                send_kernel,
                grid,
                [(left, (depth, height), lambda j: (0, 1)), right],
                [((height, count), BF16, (height, columns), lambda j: (0, j))],
                time=count / 240,
            )[0]

        def keep_core(left, right, other):
            depth, count, columns, grid, right = stage_columns(left, go(right))
            height = width // 2
            return kernel_call(
                keep_kernel,
                grid,
                [(left, (depth, height), lambda j: (0, 0)), right, by_columns(other, columns)],
                [((height // 2, count), BF16, (height // 2, columns), lambda j: (0, j))] * 2,
                time=count / 240,
            )

        def scatter_y(kept):
            keep, send = kept
            for bit in others[-2::-1]:
                if send is None:
                    keep, send = jnp.split(keep, 2, axis=0)
                keep, send = (keep, swap(go(send), bit)), None
                if bit != others[0]:
                    keep = add_low(*keep)
            return keep

        def scatter_z(array):
            return along_z(go(array))

        def scatter_gains(gradients):
            array = gradients.reshape(2, n, block).transpose(1, 0, 2)
            for bit in others[::-1]:
                half = array.shape[0] // 2
                array = array[:half] + swap(array[half:], bit)
            for bit in (2 * pair, pair):
                array = array.reshape(2, -1, 2, block)
                digit = (me // bit) % 2
                keep = lax.dynamic_index_in_dim(array, digit, 0, False)
                array = keep + swap(lax.dynamic_index_in_dim(array, 1 - digit, 0, False), bit)
            return array[0]

        def gather_square_one(own):
            own = go(own)
            return own, swap_mp(own), swap(own, pair)

        def gather_square_two(own, by_mp, by_pair):
            first = swap_mp(go(by_pair)[:middle])
            second = swap(go(by_mp)[middle:], pair)
            return own, by_mp, by_pair, first, second

        def scatter_square_one(parts):
            own, mp_one, pair_one, mp_two, pair_two = parts
            return own, swap_mp(go(mp_one)), swap(go(pair_one), pair), mp_two, pair_two

        def scatter_square_two(own, mp_one, pair_one, mp_two, pair_two):
            mp_two = swap_mp(go(add_low(mp_two, pair_one[middle:])))
            pair_two = swap(go(add_low(pair_two, mp_one[middle:])), pair)
            return own, mp_one, pair_one, mp_two, pair_two

        def square_operands(own, mp_one, pair_one, mp_two, pair_two):
            top = lambda i: (0, 0)
            shape = (middle, width)
            return [
                by_rows(own, middle),
                (pair_one, shape, top),
                (mp_two, shape, top),
                (mp_one, shape, top),
                (pair_two, shape, top),
            ]

        def norm_back(gain_row, values, passed, sums):
            return kernel_call(
                functools.partial(norm_back_kernel, gain_row),
                (2,),
                [
                    by_rows(values, middle),
                    by_rows(passed, middle),
                    *square_operands(*sums),
                    whole(gains),
                ],
                [
                    ((rows, width), F32, (middle, width), lambda i: (i, 0)),
                    ((rows, width), BF16, (middle, width), lambda i: (i, 0)),
                    ((8, width), F32, (8, width), lambda i: (0, 0)),
                ],
                time=5,
            )

        own_rows = lambda i: (i, 0)
        shape = (1, rows, width)

        gain_cols = jnp.pad(jnp.stack([attn_gain, mlp_gain], axis=1), ((0, 0), (0, 126)))
        attn_shard = jnp.concatenate([query_weight, key_matrix, value_matrix, gain_cols], axis=1)
        qkv_z = gather_z(attn_shard, attn_shard)
        out_shard, down_shard = transposed(out_weight), transposed(down_weight)
        starts = own_first(seq_starts)
        positions = me * rows + jnp.arange(rows, dtype=jnp.int32)[None] - starts
        tables = rope_tables(positions.reshape(tokens))
        about = [by_rows(t, rows) for t in tables]
        about += [by_rows(starts[:, :, None], 1), by_rows(starts[:, None, :], 1)]
        close(qkv_z, *tables, down_shard)

        qkv_y = gather_y(qkv_z)
        out_z = gather_z(out_shard, out_shard)
        close(out_z)
        gate_z = gather_z(*halves(gate_weight))
        out_y = gather_y(out_z)
        close(*qkv_y)

        qkv_parts = gather_core(qkv_y)
        close(*qkv_parts)

        moved = block % 128 == 0
        all_rows, turn = inputs, mine
        if not moved:
            all_rows, turn = move_blocks(inputs, to_table, mine, BF16), jnp.int32(0)
        rows_in, first_hidden, qkv_rot, attended, gains = kernel_call(
            functools.partial(attend_kernel, n if moved else 0, q_cols, k_cols),
            (2,),
            [
                (all_rows, shape, lambda i, t: ((i + t[n]) % 2, 0, 0)),
                *[whole(p) for p in qkv_parts],
                *about,
            ],
            [
                ((tokens, width), BF16, (rows, width), lambda i, t: (i, 0)),
                ((tokens, width), BF16, (rows, width), lambda i, t: (i, 0)),
                ((tokens, qkv_cols), BF16, (rows, qkv_cols), lambda i, t: (i, 0)),
                ((tokens, q_cols), BF16, (rows, q_cols), lambda i, t: (i, 0)),
                ((8, width), F32, (8, width), lambda i, t: (0, 0)),
            ],
            scalars=(jnp.concatenate([to_table, turn[None]]),),
            scratch=[pltpu.VMEM((rows, qkv_cols), F32)],
            time=15,
        )
        close(attended, *out_y)

        out_parts = gather_core(out_y)
        branch_own, branch_other = times_back([(attended, out_parts)], rows)
        close(branch_own, branch_other, gate_z)

        branch_other = swap_mp(go(branch_other))
        gate_y = gather_y(gate_z)
        up_z = gather_z(*halves(up_weight))
        after_own, hidden_own = kernel_call(
            forward_norm_kernel,
            (2,),
            [
                by_rows(rows_in, middle),
                by_rows(branch_own, middle),
                by_rows(branch_other, middle),
                whole(gains),
            ],
            [
                ((rows, width), F32, (middle, width), own_rows),
                ((rows, width), BF16, (middle, width), own_rows),
            ],
        )
        close(hidden_own)

        hidden_parts = gather_square_one(hidden_own)
        close(*hidden_parts, *gate_y, up_z)

        hidden_parts = gather_square_two(*hidden_parts)
        gate_parts = gather_core(gate_y)
        up_y = gather_y(up_z)
        cot_own = lax.dynamic_index_in_dim(cotangent, mine, 0, True)
        cot_pair = swap(go(cot_own), pair)
        close(*hidden_parts, *gate_parts)

        down_z = gather_z(*halves(down_shard))
        columns = 512
        grid = (hidden_cols // columns,)
        hidden_out = ((pair_tokens, hidden_cols), BF16, (pair_tokens, columns), lambda j: (0, j))
        hidden_two, gate_val = kernel_call(
            gate_kernel,
            grid,
            [
                *[whole(a) for a in hidden_parts],
                *[by_columns(p, columns) for p in gate_parts],
            ],
            [
                ((pair_tokens, width), BF16, (pair_tokens, width), lambda j: (0, 0)),
                hidden_out,
            ],
            time=14,
        )
        close(gate_val, *up_y, cot_pair)

        up_parts = gather_core(up_y)
        cot_both = swap_mp(go(cot_pair))
        close(*up_parts, down_z)

        down_y = gather_y(down_z)
        cot = [
            move_blocks(cotangent, to_table, mine, BF16),
            move_blocks(cot_pair, to_table, jnp.int32(0), BF16),
            move_blocks(cot_both, to_table, jnp.int32(0), BF16),
        ]
        cot_all = jnp.concatenate(cot, axis=0).reshape(pair_tokens, width)
        up_val, mixed = kernel_call(
            up_kernel,
            grid,
            [
                whole(hidden_two),
                *[by_columns(p, columns) for p in up_parts],
                by_columns(gate_val, columns),
            ],
            [hidden_out, hidden_out],
            time=16,
        )
        down_sent = for_core(cot_all, mixed)
        close(down_sent)

        down_sent = swap(go(down_sent), 1)
        grad_down = keep_core(cot_all, mixed, down_sent)
        close(*down_y, *grad_down)

        down_parts = gather_core(down_y)
        grad_down = scatter_y(grad_down)
        grad_gate_act, grad_up_act = kernel_call(
            mixed_back_kernel,
            grid,
            [
                whole(cot_all),
                *[by_columns(p, columns) for p in down_parts],
                by_columns(gate_val, columns),
                by_columns(go(up_val), columns),
            ],
            [hidden_out, hidden_out],
            time=17,
        )
        gate_sent = for_core(hidden_two, grad_gate_act)
        close(gate_sent)

        gate_sent = swap(go(gate_sent), 1)
        grad_two = times_back(
            [(grad_gate_act, gate_parts), (after(grad_up_act, *window), up_parts)], rows
        )
        close(grad_two[0], gate_sent)

        grad_two = scatter_square_one(grad_two)
        grad_gate = keep_core(hidden_two, grad_gate_act, gate_sent)
        close(*grad_two[:3], *grad_gate)

        grad_two = scatter_square_two(*grad_two)
        grad_gate = scatter_y(grad_gate)
        grad_down = add_low(*grad_down)
        up_sent = for_core(hidden_two, grad_up_act)
        close(*grad_two, up_sent, grad_down)

        grad_down = scatter_z(grad_down)
        up_sent = swap(go(up_sent), 1)
        grad_after, grad_branch, gain_two = norm_back(1, after_own, cot_all, grad_two)
        close(grad_branch)

        branch_other = swap_mp(go(grad_branch))
        grad_up = keep_core(hidden_two, grad_up_act, up_sent)
        close(branch_other, *grad_up)

        grad_up = scatter_y(grad_up)
        grad_branch, grad_qkv, grad_one = kernel_call(
            functools.partial(attend_back_kernel, q_cols, k_cols),
            (2,),
            [
                whole(grad_branch),
                whole(branch_other),
                *[whole(p) for p in out_parts],
                *[whole(p) for p in qkv_parts],
                by_rows(go(qkv_rot), rows),
                *about,
            ],
            [
                ((tokens, width), BF16, (rows, width), own_rows),
                ((tokens, qkv_cols), BF16, (rows, qkv_cols), own_rows),
                ((tokens, width), BF16, (rows, width), own_rows),
            ],
            scratch=[pltpu.VMEM((rows, q_cols), BF16)],
            time=29,
        )
        close(grad_one, grad_down, *grad_gate)

        other_one = swap_mp(go(grad_one))
        grad_gate = scatter_z(add_low(*grad_gate))
        out_sent = for_core(grad_branch, attended)
        attn_sent = for_core(first_hidden, grad_qkv)
        close(out_sent, attn_sent)

        out_sent, attn_sent = swap(go(out_sent), 1), swap(go(attn_sent), 1)
        grad_out = keep_core(grad_branch, attended, out_sent)
        grad_attn = keep_core(first_hidden, grad_qkv, attn_sent)
        close(*grad_out, *grad_attn, *grad_up)

        grad_out = scatter_y(grad_out)
        grad_up = add_low(*grad_up)
        branch_two = times_back([(go(mixed), down_parts)], rows)
        close(other_one, *grad_out, *branch_two, grad_gate, grad_up)

        grad_up = scatter_z(grad_up)
        grad_attn = scatter_y(grad_attn)
        branch_two = scatter_square_one(branch_two)
        grad_out = add_low(*grad_out)
        input_grad, gain_one = kernel_call(
            last_norm_back_kernel,
            (4,),
            [
                by_rows(rows_in, middle),
                by_rows(grad_branch, middle),
                by_rows(grad_one, middle),
                (other_one, (middle, width), lambda i: ((i + 2) % 4, 0)),
                whole(gains),
            ],
            [
                ((tokens, width), F32, (middle, width), own_rows),
                ((8, width), F32, (8, width), lambda i: (0, 0)),
            ],
            time=5,
        )
        grad_down = owned(go(grad_down), block, True, True)
        grad_gate = owned(go(grad_gate), block, True, False)
        close(*branch_two[:3], *grad_attn, gain_one, grad_down, grad_gate)

        branch_two = scatter_square_two(*branch_two)
        gain_two = gain_two[0] + swap_mp(go(gain_two[0]))
        grad_attn = add_low(*grad_attn)
        close(*branch_two, gain_two, grad_up, grad_attn)

        grad_out = scatter_z(grad_out)
        grad_gains = scatter_gains(go(jnp.stack([gain_one[0], gain_two])))
        result = kernel_call(
            add_kernel,
            (2,),
            [by_rows(after_own, middle), *square_operands(*branch_two)],
            [((rows, width), BF16, (middle, width), own_rows)],
        )[0]
        other_result = swap_mp(result)
        input_grad = move_blocks(
            after(input_grad, *branch_two).reshape(micro_count, rows, width), from_table, mine, F32
        )
        grad_up = owned(go(grad_up), block, True, False)
        close(grad_out, grad_gains)

        grad_attn = scatter_z(grad_attn)
        output = move_blocks(jnp.stack([result, other_result]), from_table, mine, BF16)
        grad_out = owned(grad_out, block, False, True)
        grad_attn = owned(grad_attn, block, False, False)
        grad_attn = jnp.split(grad_attn, [q_cols, q_cols + k_cols], axis=1)
        return (
            output,
            input_grad,
            grad_gains[0],
            *grad_attn,
            grad_out,
            grad_gains[1],
            grad_gate,
            grad_up,
            grad_down,
        )

    return per_device


def solution(mesh):
    in_specs = (
        P(None, "dp", None),
        P(None, "dp"),
        P(None, "dp", None),
        P("dp"),
        P("dp", "mp"),
        P("dp", "mp"),
        P("dp", "mp"),
        P("mp", "dp"),
        P("dp"),
        P("dp", "mp"),
        P("dp", "mp"),
        P("mp", "dp"),
    )
    out_specs = (
        P(None, "dp", None),
        P(None, "dp", None),
        P("dp"),
        P("dp", "mp"),
        P("dp", "mp"),
        P("dp", "mp"),
        P("mp", "dp"),
        P("dp"),
        P("dp", "mp"),
        P("dp", "mp"),
        P("mp", "dp"),
    )
    return jax.shard_map(
        make_per_device(mesh.shape["dp"]),
        mesh=mesh,
        in_specs=in_specs,
        out_specs=out_specs,
        check_vma=False,
    )
```

```python
import functools
import math

import jax
import jax.numpy as jnp
from jax import lax
from jax.experimental import pallas as pl
from jax.experimental.pallas import tpu as pltpu
from jax.sharding import PartitionSpec as P

HEAD_SIZE = 64
LANES = 2 * HEAD_SIZE
EPSILON = 1e-05
F32 = jnp.float32
BF16 = jnp.bfloat16
PIECES = 4
VMEM_LIMIT = 56 << 20
TIME_BYTES = 1_000


def dot(left, right, left_dim, right_dim):
    return lax.dot_general(
        left, right, (((left_dim,), (right_dim,)), ((), ())), preferred_element_type=F32
    )


def add_low(left, right):
    return (left.astype(F32) + right.astype(F32)).astype(BF16)


def rope_tables(positions):
    halfway = HEAD_SIZE // 2
    lane = jnp.arange(LANES, dtype=jnp.int32)
    frequency = 500000.0 ** (-((lane % halfway).astype(F32) * 2.0 / HEAD_SIZE))
    angles = positions.astype(F32)[..., None] * frequency
    sign = jnp.where(lane % HEAD_SIZE < halfway, -1.0, 1.0)
    return (jnp.cos(angles), jnp.sin(angles) * sign)


def kernel_call(kernel, grid, ins, outs, scalars=(), scratch=(), time=2, into=()):
    first = len(scalars) + len(ins)

    def spec(array, block, place):
        single = tuple(block) == array.shape or place.__name__ == "fixed"
        mode = pl.Buffered(1) if single and math.prod(grid) > 1 else None
        return pl.BlockSpec(block, place, pipeline_mode=mode)
    return pl.pallas_call(
        kernel,
        grid_spec=pltpu.PrefetchScalarGridSpec(
            num_scalar_prefetch=len(scalars),
            grid=grid,
            in_specs=[spec(*entry) for entry in ins]
            + [pl.BlockSpec(memory_space=pl.ANY)] * len(into),
            out_specs=[pl.BlockSpec(block, place) for _, _, block, place in outs],
            scratch_shapes=list(scratch),
        ),
        out_shape=[jax.ShapeDtypeStruct(shape, kind) for shape, kind, _, _ in outs],
        compiler_params=pltpu.CompilerParams(vmem_limit_bytes=VMEM_LIMIT),
        cost_estimate=pl.CostEstimate(
            flops=1, bytes_accessed=int(time * TIME_BYTES), transcendentals=0
        ),
        input_output_aliases={first + i: i for i in range(len(into))},
    )(*scalars, *[array for array, _, _ in ins], *into)


def whole(array):
    return (array, array.shape, lambda *_: (0,) * array.ndim)


def by_rows(array, rows):
    return (array, (rows,) + array.shape[1:], lambda i, *_: (i,) + (0,) * (array.ndim - 1))


def by_columns(array, columns, first=0):
    return (array, (array.shape[0], columns), lambda j, *_: (0, j + first))


def turn_lanes(pair_rows):
    lane = lax.broadcasted_iota(jnp.int32, pair_rows.shape, 1)
    up = pltpu.roll(pair_rows, LANES - HEAD_SIZE // 2, 1)
    down = pltpu.roll(pair_rows, HEAD_SIZE // 2, 1)
    return jnp.where(lane % HEAD_SIZE < HEAD_SIZE // 2, up, down)


def doubled(pair_rows, second):
    lane = lax.broadcasted_iota(jnp.int32, pair_rows.shape, 1)
    other = pltpu.roll(pair_rows, HEAD_SIZE, 1)
    return jnp.where((lane < HEAD_SIZE) != second, pair_rows, other)


def half_lanes(pair_rows, second):
    lane = lax.broadcasted_iota(jnp.int32, pair_rows.shape, 1)
    return jnp.where((lane < HEAD_SIZE) != second, pair_rows, jnp.zeros_like(pair_rows))


def allowed_pairs(start_col_ref, start_row_ref):
    rows = start_col_ref.shape[1]
    shape = (rows, rows)
    before = lax.broadcasted_iota(jnp.int32, shape, 1) <= lax.broadcasted_iota(jnp.int32, shape, 0)
    return (start_col_ref[0] == start_row_ref[0]) & before


def head_probs(query, key, allowed):
    scores = dot(query, key, 1, 1) * (1.0 / math.sqrt(HEAD_SIZE))
    scores = jnp.where(allowed, scores, -1e30)
    expo = jnp.exp(scores - jnp.max(scores, axis=-1, keepdims=True))
    return expo / jnp.sum(expo, axis=-1, keepdims=True)


def times_pieces(left, refs, columns):
    total = None
    depth = refs[0].shape[0]
    for p, ref in enumerate(refs):
        part = dot(left[:, p * depth : (p + 1) * depth], ref[:, :columns], 1, 0)
        total = part if total is None else total + part
    return total


def attend(q_cols, k_cols, raw_ref, cosine, sine, allowed, rot_ref, out_ref):
    group_width = q_cols // k_cols

    def rope(at):
        rows = raw_ref[:, at : at + LANES]
        return (rows * cosine + turn_lanes(rows) * sine).astype(BF16)

    for kv in range(k_cols // LANES):
        k_at, v_at = q_cols + kv * LANES, q_cols + k_cols + kv * LANES
        key = rope(k_at)
        value = raw_ref[:, v_at : v_at + LANES].astype(BF16)
        rot_ref[:, k_at : k_at + LANES] = key
        rot_ref[:, v_at : v_at + LANES] = value
        for group in (0, 1):
            key_two, value_two = doubled(key, group == 1), doubled(value, group == 1)
            for pair in range(group_width // 2):
                at = ((kv * 2 + group) * group_width + 2 * pair) * HEAD_SIZE
                query = rope(at)
                rot_ref[:, at : at + LANES] = query
                parts = []
                for second in (False, True):
                    probs = head_probs(half_lanes(query, second), key_two, allowed)
                    parts.append(dot(probs.astype(BF16), value_two, 1, 0))
                lane = lax.broadcasted_iota(jnp.int32, parts[0].shape, 1)
                out_ref[:, at : at + LANES] = jnp.where(lane < HEAD_SIZE, *parts).astype(BF16)


def attend_back(q_cols, k_cols, rot_ref, grad_ref, cosine, sine, allowed, out_ref):
    group_width = q_cols // k_cols
    scale = 1.0 / math.sqrt(HEAD_SIZE)

    def unrope(rows):
        return (rows * cosine - turn_lanes(rows) * sine).astype(BF16)

    def folded(rows):
        return rows + pltpu.roll(rows, HEAD_SIZE, 1)

    for kv in range(k_cols // LANES):
        k_at, v_at = q_cols + kv * LANES, q_cols + k_cols + kv * LANES
        key, value = rot_ref[:, k_at : k_at + LANES], rot_ref[:, v_at : v_at + LANES]
        grad_keys, grad_values = [], []
        for group in (0, 1):
            key_two, value_two = doubled(key, group == 1), doubled(value, group == 1)
            grad_key = jnp.zeros(key.shape, F32)
            grad_value = jnp.zeros(key.shape, F32)
            for pair in range(group_width // 2):
                at = ((kv * 2 + group) * group_width + 2 * pair) * HEAD_SIZE
                query, grad = rot_ref[:, at : at + LANES], grad_ref[:, at : at + LANES]
                parts = []
                for second in (False, True):
                    query_one, grad_one = half_lanes(query, second), half_lanes(grad, second)
                    probs = head_probs(query_one, key_two, allowed)
                    grad_probs = dot(grad_one, value_two, 1, 1)
                    inner = jnp.sum(probs * grad_probs, axis=-1, keepdims=True)
                    grad_scores = (probs * (grad_probs - inner)).astype(BF16)
                    parts.append(dot(grad_scores, key_two, 1, 0))
                    grad_key = grad_key + dot(grad_scores, query_one, 0, 0)
                    grad_value = grad_value + dot(probs.astype(BF16), grad_one, 0, 0)
                lane = lax.broadcasted_iota(jnp.int32, parts[0].shape, 1)
                out_ref[:, at : at + LANES] = unrope(jnp.where(lane < HEAD_SIZE, *parts) * scale)
            grad_keys.append(folded(grad_key) * scale)
            grad_values.append(folded(grad_value))
        lane = lax.broadcasted_iota(jnp.int32, key.shape, 1)
        out_ref[:, k_at : k_at + LANES] = unrope(jnp.where(lane < HEAD_SIZE, *grad_keys))
        out_ref[:, v_at : v_at + LANES] = jnp.where(lane < HEAD_SIZE, *grad_values).astype(BF16)


def move_rows(table_ref, count, in_ref, store):
    block = in_ref.shape[-1] // count
    for p in range(count):
        at = pl.multiple_of(table_ref[p] * block, block)
        store(p * block, in_ref[0, :, pl.ds(at, block)])


def move_kernel(count, table_ref, in_ref, *refs):
    out_ref = refs[-1]

    def store(at, rows):
        out_ref[0, :, at : at + rows.shape[1]] = rows.astype(out_ref.dtype)

    move_rows(table_ref, count, in_ref, store)


def move_blocks(array, table, mine, kind, into=None, first=0):
    micro_count, rows, width = array.shape
    count = table.shape[0]
    block = width // count
    if block % 128:
        array = jnp.roll(array, -mine, axis=0)
        pieces = [
            lax.dynamic_slice_in_dim(array, table[p] * block, block, 2) for p in range(count)
        ]
        array = jnp.concatenate(pieces, axis=-1).astype(kind)
        if into is None:
            return array
        return lax.dynamic_update_slice_in_dim(into, array, first, 0)
    shape = array.shape if into is None else into.shape
    return kernel_call(
        functools.partial(move_kernel, count),
        (micro_count,),
        [(array, (1, rows, width), lambda i, t: ((i + t[count]) % micro_count, 0, 0))],
        [(shape, kind, (1, rows, width), lambda i, t: (i + first, 0, 0))],
        scalars=(jnp.concatenate([table, mine[None]]),),
        into=() if into is None else (into,),
    )[0]


def attend_kernel(count, q_cols, k_cols, table_ref, in_ref, *refs):
    weights, lasts, refs = refs[:PIECES], refs[PIECES : 2 * PIECES], refs[2 * PIECES :]
    cos_ref, sin_ref, col_ref, row_ref = refs[:4]
    rows_ref, hidden_ref, rot_ref, out_ref, gains_ref, raw_ref = refs[4:]
    step = pl.program_id(0)
    columns = q_cols + 2 * k_cols
    depth, cut = weights[0].shape

    @pl.when(step == 0)
    def _():
        shape = (8, 128)
        pick = lax.broadcasted_iota(jnp.int32, shape, 0) == lax.broadcasted_iota(jnp.int32, shape, 1)
        for p, ref in enumerate(lasts):
            gains_ref[:, p * depth : (p + 1) * depth] = dot(
                pick.astype(F32).astype(BF16), ref[:, columns - cut :], 1, 1
            )

    def store(at, rows):
        rows_ref[:, at : at + rows.shape[1]] = rows

    if count:
        move_rows(table_ref, count, in_ref, store)
    else:
        rows_ref[...] = in_ref[0]
    rows = rows_ref[...].astype(F32)
    inverse = lax.rsqrt(jnp.mean(rows * rows, axis=-1, keepdims=True) + EPSILON)
    hidden = (rows * inverse * gains_ref[0:1, :]).astype(BF16)
    hidden_ref[...] = hidden
    raw_ref[:, :cut] = times_pieces(hidden, weights, cut)
    raw_ref[:, cut:] = times_pieces(hidden, lasts, columns - cut)
    attend(
        q_cols,
        k_cols,
        raw_ref,
        cos_ref[...],
        sin_ref[...],
        allowed_pairs(col_ref, row_ref),
        rot_ref,
        out_ref,
    )


def attend_back_kernel(q_cols, k_cols, branch_ref, *refs):
    outs, refs = refs[:PIECES], refs[PIECES:]
    weights, lasts, refs = refs[:PIECES], refs[PIECES : 2 * PIECES], refs[2 * PIECES :]
    rot_ref, cos_ref, sin_ref, col_ref, row_ref = refs[:5]
    all_ref, qkv_ref, one_ref, grad_ref = refs[-4:]
    columns = q_cols + 2 * k_cols
    all_ref[...] = branch_ref[...]
    grad_ref[...] = times_pieces(branch_ref[...], outs, q_cols).astype(BF16)
    attend_back(
        q_cols,
        k_cols,
        rot_ref,
        grad_ref,
        cos_ref[...],
        sin_ref[...],
        allowed_pairs(col_ref, row_ref),
        qkv_ref,
    )
    depth, cut = weights[0].shape
    for p, (ref, last) in enumerate(zip(weights, lasts)):
        one = dot(qkv_ref[:, :cut], ref[...], 1, 1)
        one = one + dot(qkv_ref[:, cut:], last[:, : columns - cut], 1, 1)
        one_ref[:, p * depth : (p + 1) * depth] = one.astype(BF16)


def gate_kernel(*refs):
    blocks, weights, (all_ref, gate_ref) = refs[:4], refs[4 : 4 + PIECES], refs[4 + PIECES :]

    @pl.when(pl.program_id(0) == 0)
    def _():
        rows = blocks[0].shape[0]
        for i, ref in enumerate(blocks):
            all_ref[i * rows : (i + 1) * rows, :] = ref[...]

    gate_ref[...] = times_pieces(all_ref[...], weights, gate_ref.shape[1]).astype(BF16)


def up_kernel(all_ref, *refs):
    weights, (gate_ref, up_ref, mixed_ref) = refs[:PIECES], refs[PIECES:]
    up = times_pieces(all_ref[...], weights, up_ref.shape[1])
    gate = gate_ref[...].astype(F32)
    up_ref[...] = up.astype(BF16)
    mixed_ref[...] = (gate * jax.nn.sigmoid(gate) * up).astype(BF16)


def mixed_back_kernel(cot_ref, *refs):
    weights, refs = refs[:PIECES], refs[PIECES:]
    (gate_ref, up_ref), (grad_gate_ref, grad_up_ref) = refs[:2], refs[-2:]
    grad = times_pieces(cot_ref[...], weights, gate_ref.shape[1])
    gate = gate_ref[...].astype(F32)
    sigmoid = jax.nn.sigmoid(gate)
    inner = sigmoid * (1.0 + gate * (1.0 - sigmoid))
    grad_gate_ref[...] = (grad * up_ref[...].astype(F32) * inner).astype(BF16)
    grad_up_ref[...] = (grad * (gate * sigmoid)).astype(BF16)


def back_kernel(per_piece, sides, *refs):
    lefts, refs = refs[:sides], refs[sides:]
    weights, outs = refs[: sides * PIECES], refs[sides * PIECES :]
    rows = outs[0].shape[0]
    for p in range(PIECES):

        @pl.when(pl.program_id(0) // per_piece == p)
        def _(p=p):
            total = None
            for s in range(sides):
                part = dot(lefts[s][...], weights[s * PIECES + p][...], 1, 1)
                total = part if total is None else total + part
            total = total.astype(BF16)
            outs[0][...] = total[:rows]
            if len(outs) == 2:
                outs[1][...] = total[rows:]
                return
            mp_one, pair_one, mp_two, pair_two = outs[1:]
            middle = rows // 2
            mp_two[...] = total[rows : rows + middle]
            mp_one[:middle, :] = total[rows + middle : 2 * rows]
            pair_one[:middle, :] = total[2 * rows : 2 * rows + middle]
            pair_two[...] = total[2 * rows + middle : 3 * rows]
            pair_one[middle:, :] = total[3 * rows : 3 * rows + middle]
            mp_one[middle:, :] = total[3 * rows + middle :]


def times_back(sides, rows):
    depth = sides[0][1][0].shape[0]
    columns = min(depth, 512)
    per_piece = depth // columns
    ins = []
    for left, pieces, *place in sides:
        at = (0, place[0] if place else 0)

        def fixed(j, at=at):
            return at

        ins.append((left, (left.shape[0], pieces[0].shape[1]), fixed))
    for _, pieces, *_ in sides:
        for p, piece in enumerate(pieces):

            def place(j, p=p):
                return (jnp.clip(j - p * per_piece, 0, per_piece - 1), 0)

            ins.append((piece, (columns, piece.shape[1]), place))
    heights = (rows, rows, rows, rows // 2, rows // 2)
    if sides[0][0].shape[0] == 2 * rows:
        heights = (rows, rows)
    return kernel_call(
        functools.partial(back_kernel, per_piece, len(sides)),
        (PIECES * per_piece,),
        ins,
        [((h, depth * PIECES), BF16, (h, columns), lambda j: (0, j)) for h in heights],
        time=7 * len(sides) * sides[0][0].shape[1] / 1024,
    )


def forward_norm_kernel(rows_ref, own_ref, other_ref, gains_ref, after_ref, hidden_ref):
    branch = own_ref[...].astype(F32) + other_ref[...].astype(F32)
    result = rows_ref[...].astype(F32) + branch
    after_ref[...] = result
    square = jnp.mean(result * result, axis=-1, keepdims=True)
    normed = result * lax.rsqrt(square + EPSILON)
    hidden_ref[...] = (normed * gains_ref[1:2, :]).astype(BF16)


def add_kernel(rows_ref, own_ref, pair_one, mp_two, mp_one, pair_two, out_ref):
    step = pl.program_id(0)
    for i, extra in enumerate(((pair_one, mp_two), (mp_one, pair_two))):

        @pl.when(step == i)
        def _(extra=extra):
            branch = own_ref[...].astype(F32)
            branch = branch + (extra[0][...].astype(F32) + extra[1][...].astype(F32))
            out_ref[...] = (rows_ref[...].astype(F32) + branch).astype(BF16)


def norm_back_kernel(gain_row, values_ref, passed_ref, *refs):
    own_ref, pair_one, mp_two, mp_one, pair_two, gains_ref = refs[:6]
    full_ref, low_ref, gain_ref = refs[6:]
    step = pl.program_id(0)

    @pl.when(step == 0)
    def _():
        gain_ref[...] = jnp.zeros_like(gain_ref)

    for i, extra in enumerate(((pair_one, mp_two), (mp_one, pair_two))):

        @pl.when(step == i)
        def _(extra=extra):
            grad = own_ref[...].astype(F32)
            grad = grad + (extra[0][...].astype(F32) + extra[1][...].astype(F32))
            values = values_ref[...].astype(F32)
            square = jnp.mean(values * values, axis=-1, keepdims=True)
            inverse = lax.rsqrt(square + EPSILON)
            normed = values * inverse
            scaled = grad * gains_ref[gain_row : gain_row + 1, :]
            inner = jnp.mean(scaled * normed, axis=-1, keepdims=True)
            result = passed_ref[...].astype(F32) + inverse * (scaled - normed * inner)
            full_ref[...] = result
            low_ref[...] = result.astype(BF16)
            gain_ref[0:1, :] += jnp.sum(grad * normed, axis=0, keepdims=True)


def last_norm_back_kernel(count, table_ref, values_ref, passed_ref, *refs):
    parts, others, gains_ref, out_ref, gain_ref, rows_ref = refs[:2], refs[2:4], *refs[4:]
    step = pl.program_id(0)

    @pl.when(step == 0)
    def _():
        gain_ref[...] = jnp.zeros_like(gain_ref)

    for i in (0, 1):

        @pl.when(step // 2 == i)
        def _(i=i):
            grad = parts[i][...].astype(F32) + others[i][...].astype(F32)
            values = values_ref[...].astype(F32)
            square = jnp.mean(values * values, axis=-1, keepdims=True)
            inverse = lax.rsqrt(square + EPSILON)
            normed = values * inverse
            scaled = grad * gains_ref[0:1, :]
            inner = jnp.mean(scaled * normed, axis=-1, keepdims=True)
            result = passed_ref[...].astype(F32) + inverse * (scaled - normed * inner)
            rows_ref[0, :, :] = result
            gain_ref[0:1, :] += jnp.sum(grad * normed, axis=0, keepdims=True)

    def store(at, rows):
        out_ref[0, :, at : at + rows.shape[1]] = rows

    if count:
        move_rows(table_ref, count, rows_ref, store)
    else:
        out_ref[...] = rows_ref[...]


def send_kernel(left_ref, right_ref, *refs):
    refs[-1][...] = dot(left_ref[...], right_ref[...], 0, 0).astype(BF16)


def keep_kernel(left_ref, right_ref, other_ref, *refs):
    low_ref, high_ref = refs[-2:]
    total = dot(left_ref[...], right_ref[...], 0, 0) + other_ref[...].astype(F32)
    middle = low_ref.shape[0]
    low_ref[...] = total[:middle].astype(BF16)
    high_ref[...] = total[middle:].astype(BF16)


def transpose_kernel(in_ref, out_ref):
    out_ref[...] = in_ref[...].T


def transposed(array):
    rows, columns = array.shape
    if columns % 128:
        return array.T
    return kernel_call(
        transpose_kernel,
        (rows // 512,),
        [(array, (512, columns), lambda i: (i, 0))],
        [((columns, rows), array.dtype, (columns, 512), lambda i: (0, i))],
    )[0]


def owned_kernel(flip, halves, ins, *refs):
    out_ref = refs[-1]
    for i, ref in enumerate(refs[:ins]):
        parts = [ref[k].astype(F32) for k in range(4)]
        if not halves:
            total = (parts[0] + parts[2]) + (parts[1] + parts[3])
            out_ref[...] = total.T if flip else total
            return

        for side in (0, 1):

            @pl.when(pl.program_id(0) == side * ins + i)
            def _(parts=parts, side=side):
                total = parts[side] + parts[side + 2]
                out_ref[...] = total.T if flip else total


def owned(array, second, block, halves, flip):
    arrays = [a.reshape(4, block, a.shape[1]) for a in (array, second) if a is not None]
    if block % 128:
        sides = [[], []]
        for a in arrays:
            parts = a.astype(F32)
            sides[0].append(parts[0] + parts[2])
            sides[1].append(parts[1] + parts[3])
        total = [jnp.concatenate(side, axis=1) for side in sides]
        total = jnp.concatenate(total, axis=1) if halves else total[0] + total[1]
        return total.T if flip else total
    columns = arrays[0].shape[2]
    count = 2 * len(arrays) if halves else 1
    shape, part, place = (block, columns * count), (block, columns), lambda j: (0, j)
    if flip:
        shape, part, place = shape[::-1], part[::-1], lambda j: (j, 0)
    return kernel_call(
        functools.partial(owned_kernel, flip, halves, len(arrays)),
        (count,),
        [whole(a) for a in arrays],
        [(shape, F32, part, place)],
        time=3,
    )[0]


def owned_columns_kernel(cuts, one_ref, two_ref, out_ref, query_ref, key_ref, value_ref):
    one, two = (
        (ref[0].astype(F32) + ref[2].astype(F32)) + (ref[1].astype(F32) + ref[3].astype(F32))
        for ref in (one_ref, two_ref)
    )
    queries, rest, keys = cuts
    out_ref[...] = one[:, :queries].T
    query_ref[:, :rest] = one[:, queries:]
    query_ref[:, rest:] = two[:, : queries - rest]
    key_ref[...] = two[:, queries - rest : queries - rest + keys]
    value_ref[...] = two[:, queries - rest + keys :]


def owned_columns(one, two, block, cuts):
    one, two = (a.reshape(4, block, a.shape[1]) for a in (one, two))
    queries, rest, keys = cuts
    if block % 128:
        one, two = (jnp.sum(a.astype(F32), axis=0) for a in (one, two))
        together = jnp.concatenate([one, two], axis=1)
        parts = jnp.split(together, [queries, 2 * queries, 2 * queries + keys], axis=1)
        return [parts[0].T, *parts[1:]]
    shapes = [(queries, block), (block, queries), (block, keys), (block, keys)]
    return kernel_call(
        functools.partial(owned_columns_kernel, cuts),
        (1,),
        [whole(one), whole(two)],
        [(shape, F32, shape, lambda i: (0, 0)) for shape in shapes],
    )


def after(array, *earlier):
    return lax.optimization_barrier((array, *earlier))[0]


def make_per_device(n):
    pair = 4 if n <= 16 else 8
    others = [1 << b for b in reversed(range(n.bit_length() - 1))]
    others = [v for v in others if v not in (pair, 2 * pair)]
    main_order = [pair, 2 * pair] + others
    z_groups = [[i | z * pair for z in range(4)] for i in range(n) if not i & (3 * pair)]

    def swap(array, bit):
        return lax.ppermute(array, "dp", [(i, i ^ bit) for i in range(n)])

    def swap_mp(array):
        return lax.ppermute(array, "mp", [(0, 1), (1, 0)])

    def along_z(array):
        return lax.all_to_all(array, "dp", 0, 0, axis_index_groups=z_groups, tiled=True)

    def per_device(
        inputs,
        seq_starts,
        cotangent,
        attn_gain,
        query_weight,
        key_matrix,
        value_matrix,
        out_weight,
        mlp_gain,
        gate_weight,
        up_weight,
        down_weight,
    ):
        micro_count, rows, width = inputs.shape
        middle = rows // 2
        block = width // n
        tokens, pair_tokens = micro_count * rows, 2 * micro_count * rows
        q_cols, k_cols = query_weight.shape[1], key_matrix.shape[1]
        qkv_cols = q_cols + 2 * k_cols
        hidden_cols = gate_weight.shape[1] // 2
        me, mine = lax.axis_index("dp"), lax.axis_index("mp")

        def table(natural):
            entries = []
            for p in range(n):
                entry = jnp.int32(0)
                for axis, bit in enumerate(main_order):
                    digit, weight = ((p // bit) % 2, 1 << axis) if natural else ((p >> axis) % 2, bit)
                    if bit in others:
                        digit = ((me // bit) % 2 + digit) % 2
                    entry = entry + digit * weight
                entries.append(entry)
            return jnp.stack(entries)

        to_table, from_table = table(False), table(True)

        def own_first(array):
            return jnp.where(mine == 0, array, jnp.flip(array, 0))

        window = []

        def close(*results):
            window[:] = results

        def go(array):
            return after(array, *window) if window else array

        def gather_z(first, second):
            return along_z(go(jnp.concatenate([first, second, first, second], axis=0)))

        def gather_y(array):
            pieces = [array]
            for bit in others[:-1]:
                pieces = pieces + [swap(go(piece), bit) for piece in pieces]
            return pieces

        def gather_core(pieces):
            pieces = pieces + [swap(go(piece), 1) for piece in pieces]
            share = len(pieces) // PIECES
            if share > 1:
                pieces = [
                    jnp.concatenate(pieces[i * share : (i + 1) * share]) for i in range(PIECES)
                ]
            return pieces

        def halves(shard):
            return jnp.split(shard, 2, axis=1)

        def stage_columns(left, right, part, columns):
            first, count = part or (0, right.shape[1])
            columns = columns or (count if count < 1024 else 512)
            grid = (count // columns,)
            right = by_columns(right, columns, first // columns)
            return left.shape[0], count, columns, grid, right

        def stage_outs(height, count, columns, of):
            first, total, into = of or (0, count, ())
            out = ((height, total), BF16, (height, columns), lambda j: (0, j + first // columns))
            return out, into

        def for_core(left, right, part=None, of=None, columns=None):
            depth, count, columns, grid, right = stage_columns(left, go(right), part, columns)
            height = width // 2
            out, into = stage_outs(height, count, columns, of)
            return kernel_call(
                send_kernel,
                grid,
                [(left, (depth, height), lambda j: (0, 1)), right],
                [out],
                time=count / 240,
                into=into,
            )[0]

        def keep_core(left, right, other, part=None, of=None, columns=None, arrived=None):
            depth, count, columns, grid, right = stage_columns(left, go(right), part, columns)
            height = width // 2
            out, into = stage_outs(height // 2, count, columns, of)
            arrived = (part or (0, 0))[0] if arrived is None else arrived
            return kernel_call(
                keep_kernel,
                grid,
                [
                    (left, (depth, height), lambda j: (0, 0)),
                    right,
                    by_columns(other, columns, arrived // columns),
                ],
                [out] * 2,
                time=count / 240,
                into=into,
            )

        def swap_y(send):
            return swap(send, others[-2])

        def add_halves(keeps, others_sent):
            parts = [add_low(*pair_of) for pair_of in zip(keeps, others_sent)]
            return reduce_rest(jnp.concatenate(parts, axis=1))

        def reduce_rest(array):
            for bit in others[-3::-1]:
                half = array.shape[0] // 2
                array = add_low(array[:half], swap(array[half:], bit))
            return array

        def scatter_z(array):
            return along_z(go(array))

        def scatter_gains(gradients):
            array = gradients.reshape(2, n, block).transpose(1, 0, 2)
            for bit in others[::-1]:
                half = array.shape[0] // 2
                array = array[:half] + swap(array[half:], bit)
            for bit in (2 * pair, pair):
                array = array.reshape(2, -1, 2, block)
                digit = (me // bit) % 2
                keep = lax.dynamic_index_in_dim(array, digit, 0, False)
                array = keep + swap(lax.dynamic_index_in_dim(array, 1 - digit, 0, False), bit)
            return array[0]

        def gather_square_one(own):
            own = go(own)
            return own, swap_mp(own), swap(own, pair)

        def gather_square_two(own, by_mp, by_pair):
            return own, by_mp, by_pair, swap_mp(go(by_pair))

        def scatter_square_one(parts):
            mp_one, pair_one, mp_two, pair_two = parts
            return swap_mp(go(mp_one)), swap(go(pair_one), pair), mp_two, pair_two

        def scatter_square_two(mp_one, pair_one, mp_two, pair_two):
            mp_two = swap_mp(go(add_low(mp_two, pair_one[middle:])))
            pair_two = swap(go(add_low(pair_two, mp_one[middle:])), pair)
            return mp_one, pair_one, mp_two, pair_two

        def square_operands(own, mp_one, pair_one, mp_two, pair_two):
            top = lambda i: (0, 0)
            shape = (middle, width)
            return [
                by_rows(own, middle),
                (pair_one, shape, top),
                (mp_two, shape, top),
                (mp_one, shape, top),
                (pair_two, shape, top),
            ]

        def norm_back(gain_row, values, passed, sums):
            return kernel_call(
                functools.partial(norm_back_kernel, gain_row),
                (2,),
                [
                    by_rows(values, middle),
                    by_rows(passed, middle),
                    *square_operands(*sums),
                    whole(gains),
                ],
                [
                    ((rows, width), F32, (middle, width), lambda i: (i, 0)),
                    ((rows, width), BF16, (middle, width), lambda i: (i, 0)),
                    ((8, width), F32, (8, width), lambda i: (0, 0)),
                ],
                time=5,
            )

        own_rows = lambda i: (i, 0)
        shape = (1, rows, width)

        gain_cols = jnp.pad(jnp.stack([attn_gain, mlp_gain], axis=1), ((0, 0), (0, 126)))
        cut = q_cols - 128
        last_cols = qkv_cols - cut
        first_shard = query_weight[:, :cut]
        last_shard = jnp.concatenate(
            [query_weight[:, cut:], key_matrix, value_matrix, gain_cols], axis=1
        )
        first_z = gather_z(first_shard, first_shard)
        out_shard, down_shard = transposed(out_weight), transposed(down_weight)
        cot_own = lax.dynamic_index_in_dim(cotangent, mine, 0, True)
        close(first_z, cot_own)

        first_y = gather_y(first_z)
        last_z = gather_z(last_shard, last_shard)
        starts = own_first(seq_starts)
        positions = me * rows + jnp.arange(rows, dtype=jnp.int32)[None] - starts
        tables = rope_tables(positions.reshape(tokens))
        about = [by_rows(t, rows) for t in tables]
        about += [by_rows(starts[:, :, None], 1), by_rows(starts[:, None, :], 1)]
        close(*first_y, last_z, *tables, down_shard)

        last_y = gather_y(last_z)
        first_parts = gather_core(first_y)
        out_z = gather_z(out_shard, out_shard)
        close(*last_y, *first_parts)

        last_parts = gather_core(last_y)
        close(*last_parts, out_z)

        out_y = gather_y(out_z)
        gate_z = gather_z(*halves(gate_weight))
        moved = block % 128 == 0
        all_rows, turn = inputs, mine
        if not moved:
            all_rows, turn = move_blocks(inputs, to_table, mine, BF16), jnp.int32(0)
        rows_in, first_hidden, qkv_rot, attended, gains = kernel_call(
            functools.partial(attend_kernel, n if moved else 0, q_cols, k_cols),
            (2,),
            [
                (all_rows, shape, lambda i, t: ((i + t[n]) % 2, 0, 0)),
                *[whole(p) for p in first_parts],
                *[whole(p) for p in last_parts],
                *about,
            ],
            [
                ((tokens, width), BF16, (rows, width), lambda i, t: (i, 0)),
                ((tokens, width), BF16, (rows, width), lambda i, t: (i, 0)),
                ((tokens, qkv_cols), BF16, (rows, qkv_cols), lambda i, t: (i, 0)),
                ((tokens, q_cols), BF16, (rows, q_cols), lambda i, t: (i, 0)),
                ((8, width), F32, (8, width), lambda i, t: (0, 0)),
            ],
            scalars=(jnp.concatenate([to_table, turn[None]]),),
            scratch=[pltpu.VMEM((rows, qkv_cols), F32)],
            time=15,
        )
        close(attended, *out_y)

        out_parts = gather_core(out_y)
        branch_own, branch_other = times_back([(attended, out_parts)], rows)
        close(branch_other)

        branch_other = swap_mp(go(branch_other))
        close(gate_z, branch_other)
        gate_y = gather_y(gate_z)
        up_z = gather_z(*halves(up_weight))
        after_own, hidden_own = kernel_call(
            forward_norm_kernel,
            (2,),
            [
                by_rows(rows_in, middle),
                by_rows(branch_own, middle),
                by_rows(branch_other, middle),
                whole(gains),
            ],
            [
                ((rows, width), F32, (middle, width), own_rows),
                ((rows, width), BF16, (middle, width), own_rows),
            ],
        )
        close(hidden_own)

        hidden_parts = gather_square_one(hidden_own)
        close(*hidden_parts, *gate_y, up_z)

        hidden_parts = gather_square_two(*hidden_parts)
        gate_parts = gather_core(gate_y)
        up_y = gather_y(up_z)
        down_quarters = jnp.split(down_shard, 4, axis=1)
        down_one_z = gather_z(*down_quarters[::2])
        cot_pair = swap(go(cot_own), pair)
        close(*hidden_parts, *gate_parts)

        columns = 512
        grid = (hidden_cols // columns,)
        half_hidden = hidden_cols // 2
        column_halves = ((0, half_hidden), (half_hidden, half_hidden))
        hidden_out = ((pair_tokens, hidden_cols), BF16, (pair_tokens, columns), lambda j: (0, j))
        hidden_two, gate_val = kernel_call(
            gate_kernel,
            grid,
            [
                *[whole(a) for a in hidden_parts],
                *[by_columns(p, columns) for p in gate_parts],
            ],
            [
                ((pair_tokens, width), BF16, (pair_tokens, width), lambda j: (0, 0)),
                hidden_out,
            ],
            time=14,
        )
        close(*up_y, gate_val)

        up_parts = gather_core(up_y)
        cot_both = swap_mp(go(cot_pair))
        down_two_z = gather_z(*down_quarters[1::2])
        down_one_y = gather_y(down_one_z)
        close(*up_parts)
        up_val, mixed = kernel_call(
            up_kernel,
            grid,
            [
                whole(hidden_two),
                *[by_columns(p, columns) for p in up_parts],
                by_columns(gate_val, columns),
            ],
            [hidden_out, hidden_out],
            time=16,
        )
        cot_all = jnp.zeros((4, rows, width), BF16)
        cot_all = move_blocks(cotangent, to_table, mine, BF16, cot_all)
        none = jnp.int32(0)
        cot_all = move_blocks(cot_pair, to_table, none, BF16, cot_all, 2)
        cot_all = move_blocks(after(cot_both, mixed), to_table, none, BF16, cot_all, 3)
        cot_all = cot_all.reshape(pair_tokens, width)
        close(mixed, *down_one_y, down_two_z, cot_all)

        down_two_y = gather_y(down_two_z)
        down_one = gather_core(down_one_y)
        close(*down_one)

        def mixed_back(parts, first, into=()):
            place = lambda j: (0, j + first)
            out = ((pair_tokens, hidden_cols), BF16, (pair_tokens, columns), place)
            return kernel_call(
                mixed_back_kernel,
                (hidden_cols // columns // 2,),
                [
                    whole(cot_all),
                    *[by_columns(p, columns) for p in parts],
                    by_columns(gate_val, columns, first),
                    by_columns(go(up_val), columns, first),
                ],
                [out, out],
                time=9,
                into=into,
            )

        acts = mixed_back(down_one, 0)
        down_sent = for_core(cot_all, after(mixed, acts[0]))
        close(down_sent, *down_two_y)

        down_two = gather_core(down_two_y)
        down_sent = swap(go(down_sent), 1)
        close(*down_two, down_sent)
        down_keep, down_send = keep_core(cot_all, mixed, down_sent)
        close(down_keep)
        down_arrived = swap_y(go(down_send))
        grad_gate_act, grad_up_act = mixed_back(down_two, hidden_cols // columns // 2, acts)
        gate_sent = for_core(hidden_two, grad_gate_act)
        close(gate_sent)

        gate_sent = swap(go(gate_sent), 1)
        sides = [(grad_gate_act, gate_parts), (go(grad_up_act), up_parts)]
        grad_two_own, *grad_two = times_back(sides, rows)
        close(grad_two_own, gate_sent)

        grad_two = scatter_square_one(grad_two)
        gate_keep, gate_send = zip(
            *[keep_core(hidden_two, grad_gate_act, gate_sent, part) for part in column_halves]
        )
        up_sent = for_core(hidden_two, after(grad_up_act, *gate_keep))
        grad_down = reduce_rest(add_low(go(down_keep), down_arrived))
        close(*grad_two[:2], *gate_keep, up_sent, grad_down)

        grad_two = scatter_square_two(*grad_two)
        gate_first = swap_y(gate_send[0])
        up_sent = swap(go(up_sent), 1)
        close(*grad_two)
        gate_second = swap_y(go(gate_send[1]))
        grad_down = scatter_z(go(grad_down))
        grad_after, grad_branch, gain_two = norm_back(
            1, after_own, cot_all, (grad_two_own, *grad_two)
        )
        close(grad_branch, gate_first)

        branch_other = swap_mp(go(grad_branch))

        def attention_back(branch, which, into=()):
            block_at = lambda i: (which, 0)
            return kernel_call(
                functools.partial(attend_back_kernel, q_cols, k_cols),
                (1,),
                [
                    whole(branch),
                    *[whole(p) for p in (*out_parts, *first_parts, *last_parts)],
                    (go(qkv_rot), (rows, qkv_cols), block_at),
                    *[
                        (array, part, lambda i, d=array.ndim: (which,) + (0,) * (d - 1))
                        for array, part, _ in about
                    ],
                ],
                [
                    ((tokens, width), BF16, (rows, width), block_at),
                    ((tokens, qkv_cols), BF16, (rows, qkv_cols), block_at),
                    ((rows, width), BF16, (rows, width), lambda i: (0, 0)),
                ],
                scratch=[pltpu.VMEM((rows, q_cols), BF16)],
                time=15,
                into=into,
            )

        *backs, one_own = attention_back(grad_branch, 0)
        low, high = column_halves
        up_low = keep_core(hidden_two, after(grad_up_act, one_own, gate_second), up_sent, low)
        close(branch_other, *up_low, one_own, grad_down)

        up_first = swap_y(go(up_low[1]))
        grad_gate = scatter_z(add_halves(gate_keep, (gate_first, gate_second)))
        one_from_other = swap_mp(go(one_own))
        grad_branch, grad_qkv, one_other = attention_back(branch_other, 1, backs)
        up_high = keep_core(hidden_two, after(grad_up_act, one_other), up_sent, high)
        up_keep, up_send = zip(up_low, up_high)
        close(one_other, up_first, up_high[1], one_from_other)

        one_from_own = swap_mp(go(one_other))
        up_second = swap_y(go(up_send[1]))
        total = q_cols + qkv_cols
        sent = for_core(grad_branch, attended, of=(0, total, ()))
        sent = for_core(first_hidden, grad_qkv, of=(q_cols, total, (sent,)))
        sides = [(go(mixed), down_one), (mixed, down_two, 1)]
        branch_two_own, *branch_two = times_back(sides, rows)
        close(sent, up_second, grad_gate, branch_two_own, one_from_own)

        sent = swap(go(sent), 1)
        grad_up = scatter_z(add_halves(up_keep, (up_first, up_second)))
        branch_two = scatter_square_one(branch_two)
        close(sent)
        half, rest = total // 2, total // 2 - q_cols
        group_one = keep_core(grad_branch, attended, sent, None, (0, half, ()), 256)
        group_one = keep_core(
            first_hidden, grad_qkv, sent, (0, rest), (q_cols, half, group_one), 256, q_cols
        )
        group_two = keep_core(
            first_hidden, grad_qkv, sent, (rest, half), (0, half, ()), 256, half
        )
        close(*group_one, *group_two)

        y_one = swap_y(go(group_one[1]))
        y_two = swap_y(after(group_two[1], y_one))
        latest = lambda i, *_: (jnp.minimum(i, 1), 0)
        later = lambda i, *_: (jnp.maximum(i - 2, 0), 0)
        half_rows = (middle, width)
        input_grad, gain_one = kernel_call(
            functools.partial(last_norm_back_kernel, n if moved else 0),
            (4,),
            [
                by_rows(rows_in, middle),
                by_rows(grad_branch, middle),
                (one_own, half_rows, latest),
                (one_other, half_rows, later),
                (one_from_own, half_rows, latest),
                (one_from_other, half_rows, later),
                whole(gains),
            ],
            [
                (
                    (micro_count, rows, width),
                    F32,
                    (1, middle, width),
                    lambda i, t: ((i // 2 + t[n]) % 2, i % 2, 0),
                ),
                ((8, width), F32, (8, width), lambda i, t: (0, 0)),
            ],
            scalars=(jnp.concatenate([from_table, turn[None]]),),
            scratch=[pltpu.VMEM((1, middle, width), F32)],
            time=5,
        )
        if not moved:
            input_grad = move_blocks(input_grad, from_table, mine, F32)
        grad_down = owned(go(grad_down), None, block, True, True)
        grad_gate = owned(go(grad_gate), None, block, True, False)
        sum_one = reduce_rest(add_low(after(group_one[0], gain_one, grad_down, grad_gate), y_one))
        z_one = along_z(after(sum_one, grad_up))
        z_two = along_z(after(reduce_rest(add_low(group_two[0], y_two)), z_one))
        close(y_one, *branch_two[:2])
        branch_two = scatter_square_two(*branch_two)
        result = kernel_call(
            add_kernel,
            (2,),
            [
                by_rows(after_own, middle),
                *square_operands(branch_two_own, *branch_two),
            ],
            [((rows, width), BF16, (middle, width), own_rows)],
        )[0]
        other_result = swap_mp(result)
        gain_two = gain_two[0] + swap_mp(gain_two[0])
        grad_gains = scatter_gains(jnp.stack([gain_one[0], gain_two]))
        grad_up = owned(after(grad_up, result), None, block, True, False)
        output = move_blocks(jnp.stack([result, other_result]), from_table, mine, BF16)
        grad_out, *grad_attn = owned_columns(
            after(z_one, grad_up), z_two, block, (q_cols, rest, k_cols)
        )
        return (
            output,
            input_grad,
            grad_gains[0],
            *grad_attn,
            grad_out,
            grad_gains[1],
            grad_gate,
            grad_up,
            grad_down,
        )

    return per_device


def solution(mesh):
    in_specs = (
        P(None, "dp", None),
        P(None, "dp"),
        P(None, "dp", None),
        P("dp"),
        P("dp", "mp"),
        P("dp", "mp"),
        P("dp", "mp"),
        P("mp", "dp"),
        P("dp"),
        P("dp", "mp"),
        P("dp", "mp"),
        P("mp", "dp"),
    )
    out_specs = (
        P(None, "dp", None),
        P(None, "dp", None),
        P("dp"),
        P("dp", "mp"),
        P("dp", "mp"),
        P("dp", "mp"),
        P("mp", "dp"),
        P("dp"),
        P("dp", "mp"),
        P("dp", "mp"),
        P("mp", "dp"),
    )
    return jax.shard_map(
        make_per_device(mesh.shape["dp"]),
        mesh=mesh,
        in_specs=in_specs,
        out_specs=out_specs,
        check_vma=False,
    )
```

```python
import functools
import math

import jax
import jax.numpy as jnp
from jax import lax
from jax.experimental import pallas as pl
from jax.experimental.pallas import tpu as pltpu
from jax.sharding import PartitionSpec as P

HEAD_SIZE = 64
LANES = 2 * HEAD_SIZE
EPSILON = 1e-05
F32 = jnp.float32
BF16 = jnp.bfloat16
PIECES = 4
VMEM_LIMIT = 56 << 20
TIME_BYTES = 1_000


def dot(left, right, left_dim, right_dim):
    return lax.dot_general(
        left, right, (((left_dim,), (right_dim,)), ((), ())), preferred_element_type=F32
    )


def add_low(left, right):
    return (left.astype(F32) + right.astype(F32)).astype(BF16)


def rope_tables(positions):
    halfway = HEAD_SIZE // 2
    lane = jnp.arange(LANES, dtype=jnp.int32)
    frequency = 500000.0 ** (-((lane % halfway).astype(F32) * 2.0 / HEAD_SIZE))
    angles = positions.astype(F32)[..., None] * frequency
    sign = jnp.where(lane % HEAD_SIZE < halfway, -1.0, 1.0)
    return (jnp.cos(angles), jnp.sin(angles) * sign)


def kernel_call(kernel, grid, ins, outs, scalars=(), scratch=(), time=2, into=()):
    first = len(scalars) + len(ins)

    def spec(array, block, place):
        single = tuple(block) == array.shape or place.__name__ == "fixed"
        mode = pl.Buffered(1) if single and math.prod(grid) > 1 else None
        return pl.BlockSpec(block, place, pipeline_mode=mode)
    return pl.pallas_call(
        kernel,
        grid_spec=pltpu.PrefetchScalarGridSpec(
            num_scalar_prefetch=len(scalars),
            grid=grid,
            in_specs=[spec(*entry) for entry in ins]
            + [pl.BlockSpec(memory_space=pl.ANY)] * len(into),
            out_specs=[pl.BlockSpec(block, place) for _, _, block, place in outs],
            scratch_shapes=list(scratch),
        ),
        out_shape=[jax.ShapeDtypeStruct(shape, kind) for shape, kind, _, _ in outs],
        compiler_params=pltpu.CompilerParams(vmem_limit_bytes=VMEM_LIMIT),
        cost_estimate=pl.CostEstimate(
            flops=1, bytes_accessed=int(time * TIME_BYTES), transcendentals=0
        ),
        input_output_aliases={first + i: i for i in range(len(into))},
    )(*scalars, *[array for array, _, _ in ins], *into)


def whole(array):
    return (array, array.shape, lambda *_: (0,) * array.ndim)


def by_rows(array, rows):
    return (array, (rows,) + array.shape[1:], lambda i, *_: (i,) + (0,) * (array.ndim - 1))


def by_columns(array, columns, first=0):
    return (array, (array.shape[0], columns), lambda j, *_: (0, j + first))


def turn_lanes(pair_rows):
    lane = lax.broadcasted_iota(jnp.int32, pair_rows.shape, 1)
    up = pltpu.roll(pair_rows, LANES - HEAD_SIZE // 2, 1)
    down = pltpu.roll(pair_rows, HEAD_SIZE // 2, 1)
    return jnp.where(lane % HEAD_SIZE < HEAD_SIZE // 2, up, down)


def doubled(pair_rows, second):
    lane = lax.broadcasted_iota(jnp.int32, pair_rows.shape, 1)
    other = pltpu.roll(pair_rows, HEAD_SIZE, 1)
    return jnp.where((lane < HEAD_SIZE) != second, pair_rows, other)


def half_lanes(pair_rows, second):
    lane = lax.broadcasted_iota(jnp.int32, pair_rows.shape, 1)
    return jnp.where((lane < HEAD_SIZE) != second, pair_rows, jnp.zeros_like(pair_rows))


def allowed_pairs(start_col_ref, start_row_ref):
    rows = start_col_ref.shape[1]
    shape = (rows, rows)
    before = lax.broadcasted_iota(jnp.int32, shape, 1) <= lax.broadcasted_iota(jnp.int32, shape, 0)
    return (start_col_ref[0] == start_row_ref[0]) & before


def head_probs(query, key, allowed):
    scores = dot(query, key, 1, 1) * (1.0 / math.sqrt(HEAD_SIZE))
    scores = jnp.where(allowed, scores, -1e30)
    expo = jnp.exp(scores - jnp.max(scores, axis=-1, keepdims=True))
    return expo / jnp.sum(expo, axis=-1, keepdims=True)


def times_pieces(left, refs, columns):
    total = None
    depth = refs[0].shape[0]
    for p, ref in enumerate(refs):
        part = dot(left[:, p * depth : (p + 1) * depth], ref[:, :columns], 1, 0)
        total = part if total is None else total + part
    return total


def attend(q_cols, k_cols, raw_ref, cosine, sine, allowed, rot_ref, out_ref):
    group_width = q_cols // k_cols

    def rope(at):
        rows = raw_ref[:, at : at + LANES]
        return (rows * cosine + turn_lanes(rows) * sine).astype(BF16)

    for kv in range(k_cols // LANES):
        k_at, v_at = q_cols + kv * LANES, q_cols + k_cols + kv * LANES
        key = rope(k_at)
        value = raw_ref[:, v_at : v_at + LANES].astype(BF16)
        rot_ref[:, k_at : k_at + LANES] = key
        rot_ref[:, v_at : v_at + LANES] = value
        for group in (0, 1):
            key_two, value_two = doubled(key, group == 1), doubled(value, group == 1)
            for pair in range(group_width // 2):
                at = ((kv * 2 + group) * group_width + 2 * pair) * HEAD_SIZE
                query = rope(at)
                rot_ref[:, at : at + LANES] = query
                parts = []
                for second in (False, True):
                    probs = head_probs(half_lanes(query, second), key_two, allowed)
                    parts.append(dot(probs.astype(BF16), value_two, 1, 0))
                lane = lax.broadcasted_iota(jnp.int32, parts[0].shape, 1)
                out_ref[:, at : at + LANES] = jnp.where(lane < HEAD_SIZE, *parts).astype(BF16)


def attend_back(q_cols, k_cols, rot_ref, grad_ref, cosine, sine, allowed, out_ref):
    group_width = q_cols // k_cols
    scale = 1.0 / math.sqrt(HEAD_SIZE)

    def unrope(rows):
        return (rows * cosine - turn_lanes(rows) * sine).astype(BF16)

    def folded(rows):
        return rows + pltpu.roll(rows, HEAD_SIZE, 1)

    for kv in range(k_cols // LANES):
        k_at, v_at = q_cols + kv * LANES, q_cols + k_cols + kv * LANES
        key, value = rot_ref[:, k_at : k_at + LANES], rot_ref[:, v_at : v_at + LANES]
        grad_keys, grad_values = [], []
        for group in (0, 1):
            key_two, value_two = doubled(key, group == 1), doubled(value, group == 1)
            grad_key = jnp.zeros(key.shape, F32)
            grad_value = jnp.zeros(key.shape, F32)
            for pair in range(group_width // 2):
                at = ((kv * 2 + group) * group_width + 2 * pair) * HEAD_SIZE
                query, grad = rot_ref[:, at : at + LANES], grad_ref[:, at : at + LANES]
                parts = []
                for second in (False, True):
                    query_one, grad_one = half_lanes(query, second), half_lanes(grad, second)
                    probs = head_probs(query_one, key_two, allowed)
                    grad_probs = dot(grad_one, value_two, 1, 1)
                    inner = jnp.sum(probs * grad_probs, axis=-1, keepdims=True)
                    grad_scores = (probs * (grad_probs - inner)).astype(BF16)
                    parts.append(dot(grad_scores, key_two, 1, 0))
                    grad_key = grad_key + dot(grad_scores, query_one, 0, 0)
                    grad_value = grad_value + dot(probs.astype(BF16), grad_one, 0, 0)
                lane = lax.broadcasted_iota(jnp.int32, parts[0].shape, 1)
                out_ref[:, at : at + LANES] = unrope(jnp.where(lane < HEAD_SIZE, *parts) * scale)
            grad_keys.append(folded(grad_key) * scale)
            grad_values.append(folded(grad_value))
        lane = lax.broadcasted_iota(jnp.int32, key.shape, 1)
        out_ref[:, k_at : k_at + LANES] = unrope(jnp.where(lane < HEAD_SIZE, *grad_keys))
        out_ref[:, v_at : v_at + LANES] = jnp.where(lane < HEAD_SIZE, *grad_values).astype(BF16)


def move_rows(table_ref, count, in_ref, store):
    block = in_ref.shape[-1] // count
    for p in range(count):
        at = pl.multiple_of(table_ref[p] * block, block)
        store(p * block, in_ref[0, :, pl.ds(at, block)])


def move_kernel(count, table_ref, in_ref, *refs):
    out_ref = refs[-1]

    def store(at, rows):
        out_ref[0, :, at : at + rows.shape[1]] = rows.astype(out_ref.dtype)

    move_rows(table_ref, count, in_ref, store)


def move_blocks(array, table, mine, kind, into=None, first=0):
    micro_count, rows, width = array.shape
    count = table.shape[0]
    block = width // count
    if block % 128:
        array = jnp.roll(array, -mine, axis=0)
        pieces = [
            lax.dynamic_slice_in_dim(array, table[p] * block, block, 2) for p in range(count)
        ]
        array = jnp.concatenate(pieces, axis=-1).astype(kind)
        if into is None:
            return array
        return lax.dynamic_update_slice_in_dim(into, array, first, 0)
    shape = array.shape if into is None else into.shape
    return kernel_call(
        functools.partial(move_kernel, count),
        (micro_count,),
        [(array, (1, rows, width), lambda i, t: ((i + t[count]) % micro_count, 0, 0))],
        [(shape, kind, (1, rows, width), lambda i, t: (i + first, 0, 0))],
        scalars=(jnp.concatenate([table, mine[None]]),),
        into=() if into is None else (into,),
    )[0]


def attend_kernel(count, q_cols, k_cols, table_ref, in_ref, *refs):
    weights, lasts, refs = refs[:PIECES], refs[PIECES : 2 * PIECES], refs[2 * PIECES :]
    cos_ref, sin_ref, col_ref, row_ref = refs[:4]
    rows_ref, hidden_ref, rot_ref, out_ref, gains_ref, raw_ref = refs[4:]
    step = pl.program_id(0)
    columns = q_cols + 2 * k_cols
    depth, cut = weights[0].shape

    @pl.when(step == 0)
    def _():
        shape = (8, 128)
        pick = lax.broadcasted_iota(jnp.int32, shape, 0) == lax.broadcasted_iota(jnp.int32, shape, 1)
        for p, ref in enumerate(lasts):
            gains_ref[:, p * depth : (p + 1) * depth] = dot(
                pick.astype(F32).astype(BF16), ref[:, columns - cut :], 1, 1
            )

    def store(at, rows):
        rows_ref[:, at : at + rows.shape[1]] = rows

    if count:
        move_rows(table_ref, count, in_ref, store)
    else:
        rows_ref[...] = in_ref[0]
    rows = rows_ref[...].astype(F32)
    inverse = lax.rsqrt(jnp.mean(rows * rows, axis=-1, keepdims=True) + EPSILON)
    hidden = (rows * inverse * gains_ref[0:1, :]).astype(BF16)
    hidden_ref[...] = hidden
    raw_ref[:, :cut] = times_pieces(hidden, weights, cut)
    raw_ref[:, cut:] = times_pieces(hidden, lasts, columns - cut)
    attend(
        q_cols,
        k_cols,
        raw_ref,
        cos_ref[...],
        sin_ref[...],
        allowed_pairs(col_ref, row_ref),
        rot_ref,
        out_ref,
    )


def attend_back_kernel(q_cols, k_cols, branch_ref, *refs):
    outs, refs = refs[:PIECES], refs[PIECES:]
    weights, lasts, refs = refs[:PIECES], refs[PIECES : 2 * PIECES], refs[2 * PIECES :]
    rot_ref, cos_ref, sin_ref, col_ref, row_ref = refs[:5]
    all_ref, qkv_ref, one_ref, grad_ref = refs[-4:]
    columns = q_cols + 2 * k_cols
    all_ref[...] = branch_ref[...]
    grad_ref[...] = times_pieces(branch_ref[...], outs, q_cols).astype(BF16)
    attend_back(
        q_cols,
        k_cols,
        rot_ref,
        grad_ref,
        cos_ref[...],
        sin_ref[...],
        allowed_pairs(col_ref, row_ref),
        qkv_ref,
    )
    depth, cut = weights[0].shape
    for p, (ref, last) in enumerate(zip(weights, lasts)):
        one = dot(qkv_ref[:, :cut], ref[...], 1, 1)
        one = one + dot(qkv_ref[:, cut:], last[:, : columns - cut], 1, 1)
        one_ref[:, p * depth : (p + 1) * depth] = one.astype(BF16)


def gate_kernel(*refs):
    blocks, weights, (all_ref, gate_ref) = refs[:4], refs[4 : 4 + PIECES], refs[4 + PIECES :]

    @pl.when(pl.program_id(0) == 0)
    def _():
        rows = blocks[0].shape[0]
        for i, ref in enumerate(blocks):
            all_ref[i * rows : (i + 1) * rows, :] = ref[...]

    gate_ref[...] = times_pieces(all_ref[...], weights, gate_ref.shape[1]).astype(BF16)


def up_kernel(all_ref, *refs):
    weights, (gate_ref, up_ref, mixed_ref) = refs[:PIECES], refs[PIECES:]
    up = times_pieces(all_ref[...], weights, up_ref.shape[1])
    gate = gate_ref[...].astype(F32)
    up_ref[...] = up.astype(BF16)
    mixed_ref[...] = (gate * jax.nn.sigmoid(gate) * up).astype(BF16)


def mixed_back_kernel(cot_ref, *refs):
    weights, refs = refs[:PIECES], refs[PIECES:]
    (gate_ref, up_ref), (grad_gate_ref, grad_up_ref) = refs[:2], refs[-2:]
    grad = times_pieces(cot_ref[...], weights, gate_ref.shape[1])
    gate = gate_ref[...].astype(F32)
    sigmoid = jax.nn.sigmoid(gate)
    inner = sigmoid * (1.0 + gate * (1.0 - sigmoid))
    grad_gate_ref[...] = (grad * up_ref[...].astype(F32) * inner).astype(BF16)
    grad_up_ref[...] = (grad * (gate * sigmoid)).astype(BF16)


def back_kernel(per_piece, sides, *refs):
    lefts, refs = refs[:sides], refs[sides:]
    weights, outs = refs[: sides * PIECES], refs[sides * PIECES :]
    rows = outs[0].shape[0]
    for p in range(PIECES):

        @pl.when(pl.program_id(0) // per_piece == p)
        def _(p=p):
            total = None
            for s in range(sides):
                part = dot(lefts[s][...], weights[s * PIECES + p][...], 1, 1)
                total = part if total is None else total + part
            total = total.astype(BF16)
            outs[0][...] = total[:rows]
            if len(outs) == 2:
                outs[1][...] = total[rows:]
                return
            mp_one, pair_one, mp_two, pair_two = outs[1:]
            middle = rows // 2
            mp_two[...] = total[rows : rows + middle]
            mp_one[:middle, :] = total[rows + middle : 2 * rows]
            pair_one[:middle, :] = total[2 * rows : 2 * rows + middle]
            pair_two[...] = total[2 * rows + middle : 3 * rows]
            pair_one[middle:, :] = total[3 * rows : 3 * rows + middle]
            mp_one[middle:, :] = total[3 * rows + middle :]


def times_back(sides, rows):
    depth = sides[0][1][0].shape[0]
    columns = min(depth, 512)
    per_piece = depth // columns
    ins = []
    for left, pieces, *place in sides:
        at = (0, place[0] if place else 0)

        def fixed(j, at=at):
            return at

        ins.append((left, (left.shape[0], pieces[0].shape[1]), fixed))
    for _, pieces, *_ in sides:
        for p, piece in enumerate(pieces):

            def place(j, p=p):
                return (jnp.clip(j - p * per_piece, 0, per_piece - 1), 0)

            ins.append((piece, (columns, piece.shape[1]), place))
    heights = (rows, rows, rows, rows // 2, rows // 2)
    if sides[0][0].shape[0] == 2 * rows:
        heights = (rows, rows)
    return kernel_call(
        functools.partial(back_kernel, per_piece, len(sides)),
        (PIECES * per_piece,),
        ins,
        [((h, depth * PIECES), BF16, (h, columns), lambda j: (0, j)) for h in heights],
        time=7 * len(sides) * sides[0][0].shape[1] / 1024,
    )


def forward_norm_kernel(rows_ref, own_ref, other_ref, gains_ref, after_ref, hidden_ref):
    branch = own_ref[...].astype(F32) + other_ref[...].astype(F32)
    result = rows_ref[...].astype(F32) + branch
    after_ref[...] = result
    square = jnp.mean(result * result, axis=-1, keepdims=True)
    normed = result * lax.rsqrt(square + EPSILON)
    hidden_ref[...] = (normed * gains_ref[1:2, :]).astype(BF16)


def add_kernel(rows_ref, own_ref, pair_one, mp_two, mp_one, pair_two, out_ref):
    step = pl.program_id(0)
    for i, extra in enumerate(((pair_one, mp_two), (mp_one, pair_two))):

        @pl.when(step == i)
        def _(extra=extra):
            branch = own_ref[...].astype(F32)
            branch = branch + (extra[0][...].astype(F32) + extra[1][...].astype(F32))
            out_ref[...] = (rows_ref[...].astype(F32) + branch).astype(BF16)


def norm_back_kernel(gain_row, values_ref, passed_ref, *refs):
    own_ref, pair_one, mp_two, mp_one, pair_two, gains_ref = refs[:6]
    full_ref, low_ref, gain_ref = refs[6:]
    step = pl.program_id(0)

    @pl.when(step == 0)
    def _():
        gain_ref[...] = jnp.zeros_like(gain_ref)

    for i, extra in enumerate(((pair_one, mp_two), (mp_one, pair_two))):

        @pl.when(step == i)
        def _(extra=extra):
            grad = own_ref[...].astype(F32)
            grad = grad + (extra[0][...].astype(F32) + extra[1][...].astype(F32))
            values = values_ref[...].astype(F32)
            square = jnp.mean(values * values, axis=-1, keepdims=True)
            inverse = lax.rsqrt(square + EPSILON)
            normed = values * inverse
            scaled = grad * gains_ref[gain_row : gain_row + 1, :]
            inner = jnp.mean(scaled * normed, axis=-1, keepdims=True)
            result = passed_ref[...].astype(F32) + inverse * (scaled - normed * inner)
            full_ref[...] = result
            low_ref[...] = result.astype(BF16)
            gain_ref[0:1, :] += jnp.sum(grad * normed, axis=0, keepdims=True)


def last_norm_back_kernel(count, table_ref, values_ref, passed_ref, *refs):
    parts, others, gains_ref, out_ref, gain_ref, rows_ref = refs[:2], refs[2:4], *refs[4:]
    step = pl.program_id(0)

    @pl.when(step == 0)
    def _():
        gain_ref[...] = jnp.zeros_like(gain_ref)

    for i in (0, 1):

        @pl.when(step // 2 == i)
        def _(i=i):
            grad = parts[i][...].astype(F32) + others[i][...].astype(F32)
            values = values_ref[...].astype(F32)
            square = jnp.mean(values * values, axis=-1, keepdims=True)
            inverse = lax.rsqrt(square + EPSILON)
            normed = values * inverse
            scaled = grad * gains_ref[0:1, :]
            inner = jnp.mean(scaled * normed, axis=-1, keepdims=True)
            result = passed_ref[...].astype(F32) + inverse * (scaled - normed * inner)
            rows_ref[0, :, :] = result
            gain_ref[0:1, :] += jnp.sum(grad * normed, axis=0, keepdims=True)

    def store(at, rows):
        out_ref[0, :, at : at + rows.shape[1]] = rows

    if count:
        move_rows(table_ref, count, rows_ref, store)
    else:
        out_ref[...] = rows_ref[...]


def send_kernel(left_ref, right_ref, *refs):
    refs[-1][...] = dot(left_ref[...], right_ref[...], 0, 0).astype(BF16)


def keep_kernel(left_ref, right_ref, other_ref, *refs):
    low_ref, high_ref = refs[-2:]
    total = dot(left_ref[...], right_ref[...], 0, 0) + other_ref[...].astype(F32)
    middle = low_ref.shape[0]
    low_ref[...] = total[:middle].astype(BF16)
    high_ref[...] = total[middle:].astype(BF16)


def transpose_kernel(in_ref, out_ref):
    out_ref[...] = in_ref[...].T


def transposed(array):
    rows, columns = array.shape
    if columns % 128:
        return array.T
    return kernel_call(
        transpose_kernel,
        (rows // 512,),
        [(array, (512, columns), lambda i: (i, 0))],
        [((columns, rows), array.dtype, (columns, 512), lambda i: (0, i))],
    )[0]


def owned_kernel(flip, halves, ins, *refs):
    out_ref = refs[-1]
    for i, ref in enumerate(refs[:ins]):
        parts = [ref[k].astype(F32) for k in range(4)]
        if not halves:
            total = (parts[0] + parts[2]) + (parts[1] + parts[3])
            out_ref[...] = total.T if flip else total
            return

        for side in (0, 1):

            @pl.when(pl.program_id(0) == side * ins + i)
            def _(parts=parts, side=side):
                total = parts[side] + parts[side + 2]
                out_ref[...] = total.T if flip else total


def owned(array, second, block, halves, flip):
    arrays = [a.reshape(4, block, a.shape[1]) for a in (array, second) if a is not None]
    if block % 128:
        sides = [[], []]
        for a in arrays:
            parts = a.astype(F32)
            sides[0].append(parts[0] + parts[2])
            sides[1].append(parts[1] + parts[3])
        total = [jnp.concatenate(side, axis=1) for side in sides]
        total = jnp.concatenate(total, axis=1) if halves else total[0] + total[1]
        return total.T if flip else total
    columns = arrays[0].shape[2]
    count = 2 * len(arrays) if halves else 1
    shape, part, place = (block, columns * count), (block, columns), lambda j: (0, j)
    if flip:
        shape, part, place = shape[::-1], part[::-1], lambda j: (j, 0)
    return kernel_call(
        functools.partial(owned_kernel, flip, halves, len(arrays)),
        (count,),
        [whole(a) for a in arrays],
        [(shape, F32, part, place)],
        time=3,
    )[0]


def owned_columns_kernel(cuts, one_ref, two_ref, out_ref, query_ref, key_ref, value_ref):
    one, two = (
        (ref[0].astype(F32) + ref[2].astype(F32)) + (ref[1].astype(F32) + ref[3].astype(F32))
        for ref in (one_ref, two_ref)
    )
    queries, rest, keys = cuts
    out_ref[...] = one[:, :queries].T
    query_ref[:, :rest] = one[:, queries:]
    query_ref[:, rest:] = two[:, : queries - rest]
    key_ref[...] = two[:, queries - rest : queries - rest + keys]
    value_ref[...] = two[:, queries - rest + keys :]


def owned_columns(one, two, block, cuts):
    one, two = (a.reshape(4, block, a.shape[1]) for a in (one, two))
    queries, rest, keys = cuts
    if block % 128:
        one, two = (jnp.sum(a.astype(F32), axis=0) for a in (one, two))
        together = jnp.concatenate([one, two], axis=1)
        parts = jnp.split(together, [queries, 2 * queries, 2 * queries + keys], axis=1)
        return [parts[0].T, *parts[1:]]
    shapes = [(queries, block), (block, queries), (block, keys), (block, keys)]
    return kernel_call(
        functools.partial(owned_columns_kernel, cuts),
        (1,),
        [whole(one), whole(two)],
        [(shape, F32, shape, lambda i: (0, 0)) for shape in shapes],
    )


def after(array, *earlier):
    return lax.optimization_barrier((array, *earlier))[0]


def make_per_device(n):
    pair = 4 if n <= 16 else 8
    others = [1 << b for b in reversed(range(n.bit_length() - 1))]
    others = [v for v in others if v not in (pair, 2 * pair)]
    main_order = [pair, 2 * pair] + others
    z_groups = [[i | z * pair for z in range(4)] for i in range(n) if not i & (3 * pair)]

    def swap(array, bit):
        return lax.ppermute(array, "dp", [(i, i ^ bit) for i in range(n)])

    def swap_mp(array):
        return lax.ppermute(array, "mp", [(0, 1), (1, 0)])

    def along_z(array):
        return lax.all_to_all(array, "dp", 0, 0, axis_index_groups=z_groups, tiled=True)

    def per_device(
        inputs,
        seq_starts,
        cotangent,
        attn_gain,
        query_weight,
        key_matrix,
        value_matrix,
        out_weight,
        mlp_gain,
        gate_weight,
        up_weight,
        down_weight,
    ):
        micro_count, rows, width = inputs.shape
        middle = rows // 2
        block = width // n
        tokens, pair_tokens = micro_count * rows, 2 * micro_count * rows
        q_cols, k_cols = query_weight.shape[1], key_matrix.shape[1]
        qkv_cols = q_cols + 2 * k_cols
        hidden_cols = gate_weight.shape[1] // 2
        me, mine = lax.axis_index("dp"), lax.axis_index("mp")

        def table(natural):
            entries = []
            for p in range(n):
                entry = jnp.int32(0)
                for axis, bit in enumerate(main_order):
                    digit, weight = ((p // bit) % 2, 1 << axis) if natural else ((p >> axis) % 2, bit)
                    if bit in others:
                        digit = ((me // bit) % 2 + digit) % 2
                    entry = entry + digit * weight
                entries.append(entry)
            return jnp.stack(entries)

        to_table, from_table = table(False), table(True)

        def own_first(array):
            return jnp.where(mine == 0, array, jnp.flip(array, 0))

        window = []

        def close(*results):
            window[:] = results

        def go(array):
            return after(array, *window) if window else array

        def gather_z(first, second):
            return along_z(go(jnp.concatenate([first, second, first, second], axis=0)))

        def gather_y(array):
            pieces = [array]
            for bit in others[:-1]:
                pieces = pieces + [swap(go(piece), bit) for piece in pieces]
            return pieces

        def gather_core(pieces):
            pieces = pieces + [swap(go(piece), 1) for piece in pieces]
            share = len(pieces) // PIECES
            if share > 1:
                pieces = [
                    jnp.concatenate(pieces[i * share : (i + 1) * share]) for i in range(PIECES)
                ]
            return pieces

        def halves(shard):
            return jnp.split(shard, 2, axis=1)

        def stage_columns(left, right, part, columns):
            first, count = part or (0, right.shape[1])
            columns = columns or (count if count < 1024 else 512)
            grid = (count // columns,)
            right = by_columns(right, columns, first // columns)
            return left.shape[0], count, columns, grid, right

        def stage_outs(height, count, columns, of):
            first, total, into = of or (0, count, ())
            out = ((height, total), BF16, (height, columns), lambda j: (0, j + first // columns))
            return out, into

        def for_core(left, right, part=None, of=None, columns=None):
            depth, count, columns, grid, right = stage_columns(left, go(right), part, columns)
            height = width // 2
            out, into = stage_outs(height, count, columns, of)
            return kernel_call(
                send_kernel,
                grid,
                [(left, (depth, height), lambda j: (0, 1)), right],
                [out],
                time=count / 240,
                into=into,
            )[0]

        def keep_core(left, right, other, part=None, of=None, columns=None, arrived=None):
            depth, count, columns, grid, right = stage_columns(left, go(right), part, columns)
            height = width // 2
            out, into = stage_outs(height // 2, count, columns, of)
            arrived = (part or (0, 0))[0] if arrived is None else arrived
            return kernel_call(
                keep_kernel,
                grid,
                [
                    (left, (depth, height), lambda j: (0, 0)),
                    right,
                    by_columns(other, columns, arrived // columns),
                ],
                [out] * 2,
                time=count / 240,
                into=into,
            )

        def swap_y(send):
            return swap(send, others[-2])

        def add_halves(keeps, others_sent):
            parts = [add_low(*pair_of) for pair_of in zip(keeps, others_sent)]
            return reduce_rest(jnp.concatenate(parts, axis=1))

        def reduce_rest(array):
            for bit in others[-3::-1]:
                half = array.shape[0] // 2
                array = add_low(array[:half], swap(array[half:], bit))
            return array

        def scatter_z(array):
            return along_z(go(array))

        def scatter_gains(gradients):
            array = gradients.reshape(2, n, block).transpose(1, 0, 2)
            for bit in others[::-1]:
                half = array.shape[0] // 2
                array = array[:half] + swap(array[half:], bit)
            for bit in (2 * pair, pair):
                array = array.reshape(2, -1, 2, block)
                digit = (me // bit) % 2
                keep = lax.dynamic_index_in_dim(array, digit, 0, False)
                array = keep + swap(lax.dynamic_index_in_dim(array, 1 - digit, 0, False), bit)
            return array[0]

        def gather_square_one(own):
            own = go(own)
            return own, swap_mp(own), swap(own, pair)

        def gather_square_two(own, by_mp, by_pair):
            return own, by_mp, by_pair, swap_mp(go(by_pair))

        def scatter_square_one(parts):
            mp_one, pair_one, mp_two, pair_two = parts
            return swap_mp(go(mp_one)), swap(go(pair_one), pair), mp_two, pair_two

        def scatter_square_two(mp_one, pair_one, mp_two, pair_two):
            mp_two = swap_mp(go(add_low(mp_two, pair_one[middle:])))
            pair_two = swap(go(add_low(pair_two, mp_one[middle:])), pair)
            return mp_one, pair_one, mp_two, pair_two

        def square_operands(own, mp_one, pair_one, mp_two, pair_two):
            top = lambda i: (0, 0)
            shape = (middle, width)
            return [
                by_rows(own, middle),
                (pair_one, shape, top),
                (mp_two, shape, top),
                (mp_one, shape, top),
                (pair_two, shape, top),
            ]

        def norm_back(gain_row, values, passed, sums):
            return kernel_call(
                functools.partial(norm_back_kernel, gain_row),
                (2,),
                [
                    by_rows(values, middle),
                    by_rows(passed, middle),
                    *square_operands(*sums),
                    whole(gains),
                ],
                [
                    ((rows, width), F32, (middle, width), lambda i: (i, 0)),
                    ((rows, width), BF16, (middle, width), lambda i: (i, 0)),
                    ((8, width), F32, (8, width), lambda i: (0, 0)),
                ],
                time=5,
            )

        own_rows = lambda i: (i, 0)
        shape = (1, rows, width)

        gain_cols = jnp.pad(jnp.stack([attn_gain, mlp_gain], axis=1), ((0, 0), (0, 126)))
        cut = q_cols - 128
        last_cols = qkv_cols - cut
        first_shard = query_weight[:, :cut]
        last_shard = jnp.concatenate(
            [query_weight[:, cut:], key_matrix, value_matrix, gain_cols], axis=1
        )
        first_z = gather_z(first_shard, first_shard)
        out_shard, down_shard = transposed(out_weight), transposed(down_weight)
        cot_own = lax.dynamic_index_in_dim(cotangent, mine, 0, True)
        close(first_z, cot_own)

        first_y = gather_y(first_z)
        last_z = gather_z(last_shard, last_shard)
        starts = own_first(seq_starts)
        positions = me * rows + jnp.arange(rows, dtype=jnp.int32)[None] - starts
        tables = rope_tables(positions.reshape(tokens))
        about = [by_rows(t, rows) for t in tables]
        about += [by_rows(starts[:, :, None], 1), by_rows(starts[:, None, :], 1)]
        close(*first_y, last_z, *tables, down_shard)

        last_y = gather_y(last_z)
        first_parts = gather_core(first_y)
        out_z = gather_z(out_shard, out_shard)
        close(*last_y, *first_parts)

        last_parts = gather_core(last_y)
        close(*last_parts, out_z)

        out_y = gather_y(out_z)
        gate_z = gather_z(*halves(gate_weight))
        moved = block % 128 == 0
        all_rows, turn = inputs, mine
        if not moved:
            all_rows, turn = move_blocks(inputs, to_table, mine, BF16), jnp.int32(0)
        rows_in, first_hidden, qkv_rot, attended, gains = kernel_call(
            functools.partial(attend_kernel, n if moved else 0, q_cols, k_cols),
            (2,),
            [
                (all_rows, shape, lambda i, t: ((i + t[n]) % 2, 0, 0)),
                *[whole(p) for p in first_parts],
                *[whole(p) for p in last_parts],
                *about,
            ],
            [
                ((tokens, width), BF16, (rows, width), lambda i, t: (i, 0)),
                ((tokens, width), BF16, (rows, width), lambda i, t: (i, 0)),
                ((tokens, qkv_cols), BF16, (rows, qkv_cols), lambda i, t: (i, 0)),
                ((tokens, q_cols), BF16, (rows, q_cols), lambda i, t: (i, 0)),
                ((8, width), F32, (8, width), lambda i, t: (0, 0)),
            ],
            scalars=(jnp.concatenate([to_table, turn[None]]),),
            scratch=[pltpu.VMEM((rows, qkv_cols), F32)],
            time=15,
        )
        close(attended, *out_y)

        out_parts = gather_core(out_y)
        branch_own, branch_other = times_back([(attended, out_parts)], rows)
        close(branch_other)

        branch_other = swap_mp(go(branch_other))
        close(gate_z, branch_other)
        gate_y = gather_y(gate_z)
        up_z = gather_z(*halves(up_weight))
        after_own, hidden_own = kernel_call(
            forward_norm_kernel,
            (2,),
            [
                by_rows(rows_in, middle),
                by_rows(branch_own, middle),
                by_rows(branch_other, middle),
                whole(gains),
            ],
            [
                ((rows, width), F32, (middle, width), own_rows),
                ((rows, width), BF16, (middle, width), own_rows),
            ],
        )
        close(hidden_own)

        hidden_parts = gather_square_one(hidden_own)
        close(*hidden_parts, *gate_y, up_z)

        hidden_parts = gather_square_two(*hidden_parts)
        gate_parts = gather_core(gate_y)
        up_y = gather_y(up_z)
        down_quarters = jnp.split(down_shard, 4, axis=1)
        down_one_z = gather_z(*down_quarters[::2])
        cot_pair = swap(go(cot_own), pair)
        close(*hidden_parts, *gate_parts)

        columns = 512
        grid = (hidden_cols // columns,)
        half_hidden = hidden_cols // 2
        column_halves = ((0, half_hidden), (half_hidden, half_hidden))
        hidden_out = ((pair_tokens, hidden_cols), BF16, (pair_tokens, columns), lambda j: (0, j))
        hidden_two, gate_val = kernel_call(
            gate_kernel,
            grid,
            [
                *[whole(a) for a in hidden_parts],
                *[by_columns(p, columns) for p in gate_parts],
            ],
            [
                ((pair_tokens, width), BF16, (pair_tokens, width), lambda j: (0, 0)),
                hidden_out,
            ],
            time=14,
        )
        close(*up_y, gate_val)

        up_parts = gather_core(up_y)
        cot_both = swap_mp(go(cot_pair))
        down_two_z = gather_z(*down_quarters[1::2])
        down_one_y = gather_y(down_one_z)
        close(*up_parts)
        up_val, mixed = kernel_call(
            up_kernel,
            grid,
            [
                whole(hidden_two),
                *[by_columns(p, columns) for p in up_parts],
                by_columns(gate_val, columns),
            ],
            [hidden_out, hidden_out],
            time=16,
        )
        cot_all = jnp.zeros((4, rows, width), BF16)
        cot_all = move_blocks(cotangent, to_table, mine, BF16, cot_all)
        none = jnp.int32(0)
        cot_all = move_blocks(cot_pair, to_table, none, BF16, cot_all, 2)
        cot_all = move_blocks(after(cot_both, mixed), to_table, none, BF16, cot_all, 3)
        cot_all = cot_all.reshape(pair_tokens, width)
        close(mixed, *down_one_y, down_two_z, cot_all)

        down_two_y = gather_y(down_two_z)
        down_one = gather_core(down_one_y)
        close(*down_one)

        def mixed_back(parts, first, into=()):
            place = lambda j: (0, j + first)
            out = ((pair_tokens, hidden_cols), BF16, (pair_tokens, columns), place)
            return kernel_call(
                mixed_back_kernel,
                (hidden_cols // columns // 2,),
                [
                    whole(cot_all),
                    *[by_columns(p, columns) for p in parts],
                    by_columns(gate_val, columns, first),
                    by_columns(go(up_val), columns, first),
                ],
                [out, out],
                time=9,
                into=into,
            )

        acts = mixed_back(down_one, 0)
        down_sent = for_core(cot_all, after(mixed, acts[0]))
        close(down_sent, *down_two_y)

        down_two = gather_core(down_two_y)
        down_sent = swap(go(down_sent), 1)
        close(*down_two, down_sent)
        down_keep, down_send = keep_core(cot_all, mixed, down_sent)
        close(down_keep)
        down_arrived = swap_y(go(down_send))
        grad_gate_act, grad_up_act = mixed_back(down_two, hidden_cols // columns // 2, acts)
        sides = [(grad_gate_act, gate_parts), (grad_up_act, up_parts)]
        grad_two_own, *grad_two = times_back(sides, rows)
        close(grad_two_own)

        grad_two = scatter_square_one(grad_two)
        gate_sent = for_core(hidden_two, grad_gate_act)
        up_sent = for_core(hidden_two, after(grad_up_act, gate_sent))
        grad_down = reduce_rest(add_low(go(down_keep), down_arrived))
        close(*grad_two[:2], gate_sent, up_sent, grad_down)

        grad_two = scatter_square_two(*grad_two)
        gate_sent, up_sent = swap(go(gate_sent), 1), swap(go(up_sent), 1)
        low, high = column_halves
        gate_low = keep_core(hidden_two, grad_gate_act, gate_sent, low)
        close(*grad_two, *gate_low)
        grad_down = scatter_z(go(grad_down))
        gate_first = swap_y(go(gate_low[1]))
        grad_after, grad_branch, gain_two = norm_back(
            1, after_own, cot_all, (grad_two_own, *grad_two)
        )
        close(grad_branch)

        branch_other = swap_mp(go(grad_branch))
        gate_high = keep_core(hidden_two, grad_gate_act, gate_sent, high)
        gate_second = swap_y(gate_high[1])

        def attention_back(branch, which, into=()):
            block_at = lambda i: (which, 0)
            return kernel_call(
                functools.partial(attend_back_kernel, q_cols, k_cols),
                (1,),
                [
                    whole(branch),
                    *[whole(p) for p in (*out_parts, *first_parts, *last_parts)],
                    (go(qkv_rot), (rows, qkv_cols), block_at),
                    *[
                        (array, part, lambda i, d=array.ndim: (which,) + (0,) * (d - 1))
                        for array, part, _ in about
                    ],
                ],
                [
                    ((tokens, width), BF16, (rows, width), block_at),
                    ((tokens, qkv_cols), BF16, (rows, qkv_cols), block_at),
                    ((rows, width), BF16, (rows, width), lambda i: (0, 0)),
                ],
                scratch=[pltpu.VMEM((rows, q_cols), BF16)],
                time=15,
                into=into,
            )

        *backs, one_own = attention_back(grad_branch, 0)
        up_low = keep_core(hidden_two, after(grad_up_act, one_own), up_sent, low)
        close(branch_other, *up_low, one_own, grad_down, gate_first, gate_second)

        up_first = swap_y(go(up_low[1]))
        grad_gate = scatter_z(add_halves((gate_low[0], gate_high[0]), (gate_first, gate_second)))
        one_from_other = swap_mp(go(one_own))
        grad_branch, grad_qkv, one_other = attention_back(branch_other, 1, backs)
        up_high = keep_core(hidden_two, after(grad_up_act, one_other), up_sent, high)
        up_keep, up_send = zip(up_low, up_high)
        close(one_other, up_first, up_high[1], one_from_other)

        one_from_own = swap_mp(go(one_other))
        up_second = swap_y(go(up_send[1]))
        total = q_cols + qkv_cols
        sent = for_core(grad_branch, attended, of=(0, total, ()))
        sent = for_core(first_hidden, grad_qkv, of=(q_cols, total, (sent,)))
        sides = [(go(mixed), down_one), (mixed, down_two, 1)]
        branch_two_own, *branch_two = times_back(sides, rows)
        close(sent, up_second, grad_gate, branch_two_own, one_from_own)

        sent = swap(go(sent), 1)
        grad_up = scatter_z(add_halves(up_keep, (up_first, up_second)))
        branch_two = scatter_square_one(branch_two)
        close(sent)
        half, rest = total // 2, total // 2 - q_cols
        group_one = keep_core(grad_branch, attended, sent, None, (0, half, ()), 256)
        group_one = keep_core(
            first_hidden, grad_qkv, sent, (0, rest), (q_cols, half, group_one), 256, q_cols
        )
        group_two = keep_core(
            first_hidden, grad_qkv, sent, (rest, half), (0, half, ()), 256, half
        )
        close(*group_one, *group_two)

        y_one = swap_y(go(group_one[1]))
        y_two = swap_y(after(group_two[1], y_one))
        latest = lambda i, *_: (jnp.minimum(i, 1), 0)
        later = lambda i, *_: (jnp.maximum(i - 2, 0), 0)
        half_rows = (middle, width)
        input_grad, gain_one = kernel_call(
            functools.partial(last_norm_back_kernel, n if moved else 0),
            (4,),
            [
                by_rows(rows_in, middle),
                by_rows(grad_branch, middle),
                (one_own, half_rows, latest),
                (one_other, half_rows, later),
                (one_from_own, half_rows, latest),
                (one_from_other, half_rows, later),
                whole(gains),
            ],
            [
                (
                    (micro_count, rows, width),
                    F32,
                    (1, middle, width),
                    lambda i, t: ((i // 2 + t[n]) % 2, i % 2, 0),
                ),
                ((8, width), F32, (8, width), lambda i, t: (0, 0)),
            ],
            scalars=(jnp.concatenate([from_table, turn[None]]),),
            scratch=[pltpu.VMEM((1, middle, width), F32)],
            time=5,
        )
        if not moved:
            input_grad = move_blocks(input_grad, from_table, mine, F32)
        grad_down = owned(go(grad_down), None, block, True, True)
        grad_gate = owned(go(grad_gate), None, block, True, False)
        sum_one = reduce_rest(add_low(after(group_one[0], gain_one, grad_down, grad_gate), y_one))
        z_one = along_z(after(sum_one, grad_up))
        z_two = along_z(after(reduce_rest(add_low(group_two[0], y_two)), z_one))
        close(y_one, *branch_two[:2])
        branch_two = scatter_square_two(*branch_two)
        result = kernel_call(
            add_kernel,
            (2,),
            [
                by_rows(after_own, middle),
                *square_operands(branch_two_own, *branch_two),
            ],
            [((rows, width), BF16, (middle, width), own_rows)],
        )[0]
        other_result = swap_mp(result)
        gain_two = gain_two[0] + swap_mp(gain_two[0])
        grad_gains = scatter_gains(jnp.stack([gain_one[0], gain_two]))
        grad_up = owned(after(grad_up, result), None, block, True, False)
        output = move_blocks(jnp.stack([result, other_result]), from_table, mine, BF16)
        grad_out, *grad_attn = owned_columns(
            after(z_one, grad_up), z_two, block, (q_cols, rest, k_cols)
        )
        return (
            output,
            input_grad,
            grad_gains[0],
            *grad_attn,
            grad_out,
            grad_gains[1],
            grad_gate,
            grad_up,
            grad_down,
        )

    return per_device


def solution(mesh):
    in_specs = (
        P(None, "dp", None),
        P(None, "dp"),
        P(None, "dp", None),
        P("dp"),
        P("dp", "mp"),
        P("dp", "mp"),
        P("dp", "mp"),
        P("mp", "dp"),
        P("dp"),
        P("dp", "mp"),
        P("dp", "mp"),
        P("mp", "dp"),
    )
    out_specs = (
        P(None, "dp", None),
        P(None, "dp", None),
        P("dp"),
        P("dp", "mp"),
        P("dp", "mp"),
        P("dp", "mp"),
        P("mp", "dp"),
        P("dp"),
        P("dp", "mp"),
        P("dp", "mp"),
        P("mp", "dp"),
    )
    return jax.shard_map(
        make_per_device(mesh.shape["dp"]),
        mesh=mesh,
        in_specs=in_specs,
        out_specs=out_specs,
        check_vma=False,
    )
```

```python
import functools
import math

import jax
import jax.numpy as jnp
from jax import lax
from jax.experimental import pallas as pl
from jax.experimental.pallas import tpu as pltpu
from jax.sharding import PartitionSpec as P

HEAD_SIZE = 64
LANES = 2 * HEAD_SIZE
EPSILON = 1e-05
F32 = jnp.float32
BF16 = jnp.bfloat16
PIECES = 4
VMEM_LIMIT = 56 << 20
TIME_BYTES = 1_000


def dot(left, right, left_dim, right_dim):
    return lax.dot_general(
        left, right, (((left_dim,), (right_dim,)), ((), ())), preferred_element_type=F32
    )


def add_low(left, right):
    return (left.astype(F32) + right.astype(F32)).astype(BF16)


def rope_tables(positions):
    halfway = HEAD_SIZE // 2
    lane = jnp.arange(LANES, dtype=jnp.int32)
    frequency = 500000.0 ** (-((lane % halfway).astype(F32) * 2.0 / HEAD_SIZE))
    angles = positions.astype(F32)[..., None] * frequency
    sign = jnp.where(lane % HEAD_SIZE < halfway, -1.0, 1.0)
    return (jnp.cos(angles), jnp.sin(angles) * sign)


def kernel_call(kernel, grid, ins, outs, scalars=(), scratch=(), time=2, into=()):
    first = len(scalars) + len(ins)

    def spec(array, block, place):
        single = tuple(block) == array.shape or place.__name__ == "fixed"
        mode = pl.Buffered(1) if single and math.prod(grid) > 1 else None
        return pl.BlockSpec(block, place, pipeline_mode=mode)
    return pl.pallas_call(
        kernel,
        grid_spec=pltpu.PrefetchScalarGridSpec(
            num_scalar_prefetch=len(scalars),
            grid=grid,
            in_specs=[spec(*entry) for entry in ins]
            + [pl.BlockSpec(memory_space=pl.ANY)] * len(into),
            out_specs=[pl.BlockSpec(block, place) for _, _, block, place in outs],
            scratch_shapes=list(scratch),
        ),
        out_shape=[jax.ShapeDtypeStruct(shape, kind) for shape, kind, _, _ in outs],
        compiler_params=pltpu.CompilerParams(vmem_limit_bytes=VMEM_LIMIT),
        cost_estimate=pl.CostEstimate(
            flops=1, bytes_accessed=int(time * TIME_BYTES), transcendentals=0
        ),
        input_output_aliases={first + i: i for i in range(len(into))},
    )(*scalars, *[array for array, _, _ in ins], *into)


def whole(array):
    return (array, array.shape, lambda *_: (0,) * array.ndim)


def by_rows(array, rows):
    return (array, (rows,) + array.shape[1:], lambda i, *_: (i,) + (0,) * (array.ndim - 1))


def by_columns(array, columns, first=0):
    return (array, (array.shape[0], columns), lambda j, *_: (0, j + first))


def turn_lanes(pair_rows):
    lane = lax.broadcasted_iota(jnp.int32, pair_rows.shape, 1)
    up = pltpu.roll(pair_rows, LANES - HEAD_SIZE // 2, 1)
    down = pltpu.roll(pair_rows, HEAD_SIZE // 2, 1)
    return jnp.where(lane % HEAD_SIZE < HEAD_SIZE // 2, up, down)


def doubled(pair_rows, second):
    lane = lax.broadcasted_iota(jnp.int32, pair_rows.shape, 1)
    other = pltpu.roll(pair_rows, HEAD_SIZE, 1)
    return jnp.where((lane < HEAD_SIZE) != second, pair_rows, other)


def half_lanes(pair_rows, second):
    lane = lax.broadcasted_iota(jnp.int32, pair_rows.shape, 1)
    return jnp.where((lane < HEAD_SIZE) != second, pair_rows, jnp.zeros_like(pair_rows))


def allowed_pairs(start_col_ref, start_row_ref):
    rows = start_col_ref.shape[1]
    shape = (rows, rows)
    before = lax.broadcasted_iota(jnp.int32, shape, 1) <= lax.broadcasted_iota(jnp.int32, shape, 0)
    return (start_col_ref[0] == start_row_ref[0]) & before


def head_probs(query, key, allowed):
    scores = dot(query, key, 1, 1) * (1.0 / math.sqrt(HEAD_SIZE))
    scores = jnp.where(allowed, scores, -1e30)
    expo = jnp.exp(scores - jnp.max(scores, axis=-1, keepdims=True))
    return expo / jnp.sum(expo, axis=-1, keepdims=True)


def times_pieces(left, refs, columns):
    total = None
    depth = refs[0].shape[0]
    for p, ref in enumerate(refs):
        part = dot(left[:, p * depth : (p + 1) * depth], ref[:, :columns], 1, 0)
        total = part if total is None else total + part
    return total


def attend(q_cols, k_cols, raw_ref, cosine, sine, allowed, rot_ref, out_ref):
    group_width = q_cols // k_cols

    def rope(at):
        rows = raw_ref[:, at : at + LANES]
        return (rows * cosine + turn_lanes(rows) * sine).astype(BF16)

    for kv in range(k_cols // LANES):
        k_at, v_at = q_cols + kv * LANES, q_cols + k_cols + kv * LANES
        key = rope(k_at)
        value = raw_ref[:, v_at : v_at + LANES].astype(BF16)
        rot_ref[:, k_at : k_at + LANES] = key
        rot_ref[:, v_at : v_at + LANES] = value
        for group in (0, 1):
            key_two, value_two = doubled(key, group == 1), doubled(value, group == 1)
            for pair in range(group_width // 2):
                at = ((kv * 2 + group) * group_width + 2 * pair) * HEAD_SIZE
                query = rope(at)
                rot_ref[:, at : at + LANES] = query
                parts = []
                for second in (False, True):
                    probs = head_probs(half_lanes(query, second), key_two, allowed)
                    parts.append(dot(probs.astype(BF16), value_two, 1, 0))
                lane = lax.broadcasted_iota(jnp.int32, parts[0].shape, 1)
                out_ref[:, at : at + LANES] = jnp.where(lane < HEAD_SIZE, *parts).astype(BF16)


def attend_back(q_cols, k_cols, rot_ref, grad_ref, cosine, sine, allowed, out_ref):
    group_width = q_cols // k_cols
    scale = 1.0 / math.sqrt(HEAD_SIZE)

    def unrope(rows):
        return (rows * cosine - turn_lanes(rows) * sine).astype(BF16)

    def folded(rows):
        return rows + pltpu.roll(rows, HEAD_SIZE, 1)

    for kv in range(k_cols // LANES):
        k_at, v_at = q_cols + kv * LANES, q_cols + k_cols + kv * LANES
        key, value = rot_ref[:, k_at : k_at + LANES], rot_ref[:, v_at : v_at + LANES]
        grad_keys, grad_values = [], []
        for group in (0, 1):
            key_two, value_two = doubled(key, group == 1), doubled(value, group == 1)
            grad_key = jnp.zeros(key.shape, F32)
            grad_value = jnp.zeros(key.shape, F32)
            for pair in range(group_width // 2):
                at = ((kv * 2 + group) * group_width + 2 * pair) * HEAD_SIZE
                query, grad = rot_ref[:, at : at + LANES], grad_ref[:, at : at + LANES]
                parts = []
                for second in (False, True):
                    query_one, grad_one = half_lanes(query, second), half_lanes(grad, second)
                    probs = head_probs(query_one, key_two, allowed)
                    grad_probs = dot(grad_one, value_two, 1, 1)
                    inner = jnp.sum(probs * grad_probs, axis=-1, keepdims=True)
                    grad_scores = (probs * (grad_probs - inner)).astype(BF16)
                    parts.append(dot(grad_scores, key_two, 1, 0))
                    grad_key = grad_key + dot(grad_scores, query_one, 0, 0)
                    grad_value = grad_value + dot(probs.astype(BF16), grad_one, 0, 0)
                lane = lax.broadcasted_iota(jnp.int32, parts[0].shape, 1)
                out_ref[:, at : at + LANES] = unrope(jnp.where(lane < HEAD_SIZE, *parts) * scale)
            grad_keys.append(folded(grad_key) * scale)
            grad_values.append(folded(grad_value))
        lane = lax.broadcasted_iota(jnp.int32, key.shape, 1)
        out_ref[:, k_at : k_at + LANES] = unrope(jnp.where(lane < HEAD_SIZE, *grad_keys))
        out_ref[:, v_at : v_at + LANES] = jnp.where(lane < HEAD_SIZE, *grad_values).astype(BF16)


def move_rows(table_ref, count, in_ref, store):
    block = in_ref.shape[-1] // count
    for p in range(count):
        at = pl.multiple_of(table_ref[p] * block, block)
        store(p * block, in_ref[0, :, pl.ds(at, block)])


def move_kernel(count, table_ref, in_ref, *refs):
    out_ref = refs[-1]

    def store(at, rows):
        out_ref[0, :, at : at + rows.shape[1]] = rows.astype(out_ref.dtype)

    move_rows(table_ref, count, in_ref, store)


def move_blocks(array, table, mine, kind, into=None, first=0):
    micro_count, rows, width = array.shape
    count = table.shape[0]
    block = width // count
    if block % 128:
        array = jnp.roll(array, -mine, axis=0)
        pieces = [
            lax.dynamic_slice_in_dim(array, table[p] * block, block, 2) for p in range(count)
        ]
        array = jnp.concatenate(pieces, axis=-1).astype(kind)
        if into is None:
            return array
        return lax.dynamic_update_slice_in_dim(into, array, first, 0)
    shape = array.shape if into is None else into.shape
    return kernel_call(
        functools.partial(move_kernel, count),
        (micro_count,),
        [(array, (1, rows, width), lambda i, t: ((i + t[count]) % micro_count, 0, 0))],
        [(shape, kind, (1, rows, width), lambda i, t: (i + first, 0, 0))],
        scalars=(jnp.concatenate([table, mine[None]]),),
        into=() if into is None else (into,),
    )[0]


def attend_kernel(count, q_cols, k_cols, table_ref, in_ref, *refs):
    weights, lasts, refs = refs[:PIECES], refs[PIECES : 2 * PIECES], refs[2 * PIECES :]
    cos_ref, sin_ref, col_ref, row_ref = refs[:4]
    rows_ref, hidden_ref, rot_ref, out_ref, gains_ref, raw_ref = refs[4:]
    step = pl.program_id(0)
    columns = q_cols + 2 * k_cols
    depth, cut = weights[0].shape

    @pl.when(step == 0)
    def _():
        shape = (8, 128)
        pick = lax.broadcasted_iota(jnp.int32, shape, 0) == lax.broadcasted_iota(jnp.int32, shape, 1)
        for p, ref in enumerate(lasts):
            gains_ref[:, p * depth : (p + 1) * depth] = dot(
                pick.astype(F32).astype(BF16), ref[:, columns - cut :], 1, 1
            )

    def store(at, rows):
        rows_ref[:, at : at + rows.shape[1]] = rows

    if count:
        move_rows(table_ref, count, in_ref, store)
    else:
        rows_ref[...] = in_ref[0]
    rows = rows_ref[...].astype(F32)
    inverse = lax.rsqrt(jnp.mean(rows * rows, axis=-1, keepdims=True) + EPSILON)
    hidden = (rows * inverse * gains_ref[0:1, :]).astype(BF16)
    hidden_ref[...] = hidden
    raw_ref[:, :cut] = times_pieces(hidden, weights, cut)
    raw_ref[:, cut:] = times_pieces(hidden, lasts, columns - cut)
    attend(
        q_cols,
        k_cols,
        raw_ref,
        cos_ref[...],
        sin_ref[...],
        allowed_pairs(col_ref, row_ref),
        rot_ref,
        out_ref,
    )


def attend_back_kernel(q_cols, k_cols, branch_ref, *refs):
    outs, refs = refs[:PIECES], refs[PIECES:]
    weights, lasts, refs = refs[:PIECES], refs[PIECES : 2 * PIECES], refs[2 * PIECES :]
    rot_ref, cos_ref, sin_ref, col_ref, row_ref = refs[:5]
    all_ref, qkv_ref, one_ref, grad_ref = refs[-4:]
    columns = q_cols + 2 * k_cols
    all_ref[...] = branch_ref[...]
    grad_ref[...] = times_pieces(branch_ref[...], outs, q_cols).astype(BF16)
    attend_back(
        q_cols,
        k_cols,
        rot_ref,
        grad_ref,
        cos_ref[...],
        sin_ref[...],
        allowed_pairs(col_ref, row_ref),
        qkv_ref,
    )
    depth, cut = weights[0].shape
    for p, (ref, last) in enumerate(zip(weights, lasts)):
        one = dot(qkv_ref[:, :cut], ref[...], 1, 1)
        one = one + dot(qkv_ref[:, cut:], last[:, : columns - cut], 1, 1)
        one_ref[:, p * depth : (p + 1) * depth] = one.astype(BF16)


def gate_kernel(*refs):
    blocks, weights, (all_ref, gate_ref) = refs[:4], refs[4 : 4 + PIECES], refs[4 + PIECES :]

    @pl.when(pl.program_id(0) == 0)
    def _():
        rows = blocks[0].shape[0]
        for i, ref in enumerate(blocks):
            all_ref[i * rows : (i + 1) * rows, :] = ref[...]

    gate_ref[...] = times_pieces(all_ref[...], weights, gate_ref.shape[1]).astype(BF16)


def up_kernel(all_ref, *refs):
    weights, (gate_ref, up_ref, mixed_ref) = refs[:PIECES], refs[PIECES:]
    up = times_pieces(all_ref[...], weights, up_ref.shape[1])
    gate = gate_ref[...].astype(F32)
    up_ref[...] = up.astype(BF16)
    mixed_ref[...] = (gate * jax.nn.sigmoid(gate) * up).astype(BF16)


def mixed_back_kernel(cot_ref, *refs):
    weights, refs = refs[:PIECES], refs[PIECES:]
    (gate_ref, up_ref), (grad_gate_ref, grad_up_ref) = refs[:2], refs[-2:]
    grad = times_pieces(cot_ref[...], weights, gate_ref.shape[1])
    gate = gate_ref[...].astype(F32)
    sigmoid = jax.nn.sigmoid(gate)
    inner = sigmoid * (1.0 + gate * (1.0 - sigmoid))
    grad_gate_ref[...] = (grad * up_ref[...].astype(F32) * inner).astype(BF16)
    grad_up_ref[...] = (grad * (gate * sigmoid)).astype(BF16)


def back_kernel(per_piece, sides, *refs):
    lefts, refs = refs[:sides], refs[sides:]
    weights, outs = refs[: sides * PIECES], refs[sides * PIECES :]
    rows = outs[0].shape[0]
    for p in range(PIECES):

        @pl.when(pl.program_id(0) // per_piece == p)
        def _(p=p):
            total = None
            for s in range(sides):
                part = dot(lefts[s][...], weights[s * PIECES + p][...], 1, 1)
                total = part if total is None else total + part
            total = total.astype(BF16)
            outs[0][...] = total[:rows]
            if len(outs) == 2:
                outs[1][...] = total[rows:]
                return
            mp_one, pair_one, mp_two, pair_two = outs[1:]
            middle = rows // 2
            mp_two[...] = total[rows : rows + middle]
            mp_one[:middle, :] = total[rows + middle : 2 * rows]
            pair_one[:middle, :] = total[2 * rows : 2 * rows + middle]
            pair_two[...] = total[2 * rows + middle : 3 * rows]
            pair_one[middle:, :] = total[3 * rows : 3 * rows + middle]
            mp_one[middle:, :] = total[3 * rows + middle :]


def times_back(sides, rows):
    depth = sides[0][1][0].shape[0]
    columns = min(depth, 512)
    per_piece = depth // columns
    ins = []
    for left, pieces, *place in sides:
        at = (0, place[0] if place else 0)

        def fixed(j, at=at):
            return at

        ins.append((left, (left.shape[0], pieces[0].shape[1]), fixed))
    for _, pieces, *_ in sides:
        for p, piece in enumerate(pieces):

            def place(j, p=p):
                return (jnp.clip(j - p * per_piece, 0, per_piece - 1), 0)

            ins.append((piece, (columns, piece.shape[1]), place))
    heights = (rows, rows, rows, rows // 2, rows // 2)
    if sides[0][0].shape[0] == 2 * rows:
        heights = (rows, rows)
    return kernel_call(
        functools.partial(back_kernel, per_piece, len(sides)),
        (PIECES * per_piece,),
        ins,
        [((h, depth * PIECES), BF16, (h, columns), lambda j: (0, j)) for h in heights],
        time=7 * len(sides) * sides[0][0].shape[1] / 1024,
    )


def forward_norm_kernel(rows_ref, own_ref, other_ref, gains_ref, after_ref, hidden_ref):
    branch = own_ref[...].astype(F32) + other_ref[...].astype(F32)
    result = rows_ref[...].astype(F32) + branch
    after_ref[...] = result
    square = jnp.mean(result * result, axis=-1, keepdims=True)
    normed = result * lax.rsqrt(square + EPSILON)
    hidden_ref[...] = (normed * gains_ref[1:2, :]).astype(BF16)


def add_kernel(rows_ref, own_ref, pair_one, mp_two, mp_one, pair_two, out_ref):
    step = pl.program_id(0)
    for i, extra in enumerate(((pair_one, mp_two), (mp_one, pair_two))):

        @pl.when(step == i)
        def _(extra=extra):
            branch = own_ref[...].astype(F32)
            branch = branch + (extra[0][...].astype(F32) + extra[1][...].astype(F32))
            out_ref[...] = (rows_ref[...].astype(F32) + branch).astype(BF16)


def norm_back_kernel(gain_row, values_ref, passed_ref, *refs):
    own_ref, pair_one, mp_two, mp_one, pair_two, gains_ref = refs[:6]
    full_ref, low_ref, gain_ref = refs[6:]
    step = pl.program_id(0)

    @pl.when(step == 0)
    def _():
        gain_ref[...] = jnp.zeros_like(gain_ref)

    for i, extra in enumerate(((pair_one, mp_two), (mp_one, pair_two))):

        @pl.when(step == i)
        def _(extra=extra):
            grad = own_ref[...].astype(F32)
            grad = grad + (extra[0][...].astype(F32) + extra[1][...].astype(F32))
            values = values_ref[...].astype(F32)
            square = jnp.mean(values * values, axis=-1, keepdims=True)
            inverse = lax.rsqrt(square + EPSILON)
            normed = values * inverse
            scaled = grad * gains_ref[gain_row : gain_row + 1, :]
            inner = jnp.mean(scaled * normed, axis=-1, keepdims=True)
            result = passed_ref[...].astype(F32) + inverse * (scaled - normed * inner)
            full_ref[...] = result
            low_ref[...] = result.astype(BF16)
            gain_ref[0:1, :] += jnp.sum(grad * normed, axis=0, keepdims=True)


def last_norm_back_kernel(count, table_ref, values_ref, passed_ref, *refs):
    parts, others, gains_ref, out_ref, gain_ref, rows_ref = refs[:2], refs[2:4], *refs[4:]
    step = pl.program_id(0)

    @pl.when(step == 0)
    def _():
        gain_ref[...] = jnp.zeros_like(gain_ref)

    for i in (0, 1):

        @pl.when(step // 2 == i)
        def _(i=i):
            grad = parts[i][...].astype(F32) + others[i][...].astype(F32)
            values = values_ref[...].astype(F32)
            square = jnp.mean(values * values, axis=-1, keepdims=True)
            inverse = lax.rsqrt(square + EPSILON)
            normed = values * inverse
            scaled = grad * gains_ref[0:1, :]
            inner = jnp.mean(scaled * normed, axis=-1, keepdims=True)
            result = passed_ref[...].astype(F32) + inverse * (scaled - normed * inner)
            rows_ref[0, :, :] = result
            gain_ref[0:1, :] += jnp.sum(grad * normed, axis=0, keepdims=True)

    def store(at, rows):
        out_ref[0, :, at : at + rows.shape[1]] = rows

    if count:
        move_rows(table_ref, count, rows_ref, store)
    else:
        out_ref[...] = rows_ref[...]


def send_kernel(left_ref, right_ref, *refs):
    refs[-1][...] = dot(left_ref[...], right_ref[...], 0, 0).astype(BF16)


def keep_kernel(left_ref, right_ref, other_ref, *refs):
    low_ref, high_ref = refs[-2:]
    total = dot(left_ref[...], right_ref[...], 0, 0) + other_ref[...].astype(F32)
    middle = low_ref.shape[0]
    low_ref[...] = total[:middle].astype(BF16)
    high_ref[...] = total[middle:].astype(BF16)


def transpose_kernel(in_ref, out_ref):
    out_ref[...] = in_ref[...].T


def transposed(array):
    rows, columns = array.shape
    if columns % 128:
        return array.T
    return kernel_call(
        transpose_kernel,
        (rows // 512,),
        [(array, (512, columns), lambda i: (i, 0))],
        [((columns, rows), array.dtype, (columns, 512), lambda i: (0, i))],
    )[0]


def owned_kernel(flip, halves, ins, *refs):
    out_ref = refs[-1]
    for i, ref in enumerate(refs[:ins]):
        parts = [ref[k].astype(F32) for k in range(4)]
        if not halves:
            total = (parts[0] + parts[2]) + (parts[1] + parts[3])
            out_ref[...] = total.T if flip else total
            return

        for side in (0, 1):

            @pl.when(pl.program_id(0) == side * ins + i)
            def _(parts=parts, side=side):
                total = parts[side] + parts[side + 2]
                out_ref[...] = total.T if flip else total


def owned(array, second, block, halves, flip):
    arrays = [a.reshape(4, block, a.shape[1]) for a in (array, second) if a is not None]
    if block % 128:
        sides = [[], []]
        for a in arrays:
            parts = a.astype(F32)
            sides[0].append(parts[0] + parts[2])
            sides[1].append(parts[1] + parts[3])
        total = [jnp.concatenate(side, axis=1) for side in sides]
        total = jnp.concatenate(total, axis=1) if halves else total[0] + total[1]
        return total.T if flip else total
    columns = arrays[0].shape[2]
    count = 2 * len(arrays) if halves else 1
    shape, part, place = (block, columns * count), (block, columns), lambda j: (0, j)
    if flip:
        shape, part, place = shape[::-1], part[::-1], lambda j: (j, 0)
    return kernel_call(
        functools.partial(owned_kernel, flip, halves, len(arrays)),
        (count,),
        [whole(a) for a in arrays],
        [(shape, F32, part, place)],
        time=3,
    )[0]


def owned_columns_kernel(cuts, one_ref, two_ref, out_ref, query_ref, key_ref, value_ref):
    one, two = (
        (ref[0].astype(F32) + ref[2].astype(F32)) + (ref[1].astype(F32) + ref[3].astype(F32))
        for ref in (one_ref, two_ref)
    )
    queries, rest, keys = cuts
    out_ref[...] = one[:, :queries].T
    query_ref[:, :rest] = one[:, queries:]
    query_ref[:, rest:] = two[:, : queries - rest]
    key_ref[...] = two[:, queries - rest : queries - rest + keys]
    value_ref[...] = two[:, queries - rest + keys :]


def owned_columns(one, two, block, cuts):
    one, two = (a.reshape(4, block, a.shape[1]) for a in (one, two))
    queries, rest, keys = cuts
    if block % 128:
        one, two = (jnp.sum(a.astype(F32), axis=0) for a in (one, two))
        together = jnp.concatenate([one, two], axis=1)
        parts = jnp.split(together, [queries, 2 * queries, 2 * queries + keys], axis=1)
        return [parts[0].T, *parts[1:]]
    shapes = [(queries, block), (block, queries), (block, keys), (block, keys)]
    return kernel_call(
        functools.partial(owned_columns_kernel, cuts),
        (1,),
        [whole(one), whole(two)],
        [(shape, F32, shape, lambda i: (0, 0)) for shape in shapes],
    )


def after(array, *earlier):
    return lax.optimization_barrier((array, *earlier))[0]


def make_per_device(n):
    pair = 4 if n <= 16 else 8
    others = [1 << b for b in reversed(range(n.bit_length() - 1))]
    others = [v for v in others if v not in (pair, 2 * pair)]
    main_order = [pair, 2 * pair] + others
    z_groups = [[i | z * pair for z in range(4)] for i in range(n) if not i & (3 * pair)]

    def swap(array, bit):
        return lax.ppermute(array, "dp", [(i, i ^ bit) for i in range(n)])

    def swap_mp(array):
        return lax.ppermute(array, "mp", [(0, 1), (1, 0)])

    def along_z(array):
        return lax.all_to_all(array, "dp", 0, 0, axis_index_groups=z_groups, tiled=True)

    def per_device(
        inputs,
        seq_starts,
        cotangent,
        attn_gain,
        query_weight,
        key_matrix,
        value_matrix,
        out_weight,
        mlp_gain,
        gate_weight,
        up_weight,
        down_weight,
    ):
        micro_count, rows, width = inputs.shape
        middle = rows // 2
        block = width // n
        tokens, pair_tokens = micro_count * rows, 2 * micro_count * rows
        q_cols, k_cols = query_weight.shape[1], key_matrix.shape[1]
        qkv_cols = q_cols + 2 * k_cols
        hidden_cols = gate_weight.shape[1] // 2
        me, mine = lax.axis_index("dp"), lax.axis_index("mp")

        def table(natural):
            entries = []
            for p in range(n):
                entry = jnp.int32(0)
                for axis, bit in enumerate(main_order):
                    digit, weight = ((p // bit) % 2, 1 << axis) if natural else ((p >> axis) % 2, bit)
                    if bit in others:
                        digit = ((me // bit) % 2 + digit) % 2
                    entry = entry + digit * weight
                entries.append(entry)
            return jnp.stack(entries)

        to_table, from_table = table(False), table(True)

        def own_first(array):
            return jnp.where(mine == 0, array, jnp.flip(array, 0))

        window = []

        def close(*results):
            window[:] = results

        def go(array):
            return after(array, *window) if window else array

        def gather_z(first, second):
            return along_z(go(jnp.concatenate([first, second, first, second], axis=0)))

        def gather_y(array):
            pieces = [array]
            for bit in others[:-1]:
                pieces = pieces + [swap(go(piece), bit) for piece in pieces]
            return pieces

        def gather_core(pieces):
            pieces = pieces + [swap(go(piece), 1) for piece in pieces]
            share = len(pieces) // PIECES
            if share > 1:
                pieces = [
                    jnp.concatenate(pieces[i * share : (i + 1) * share]) for i in range(PIECES)
                ]
            return pieces

        def halves(shard):
            return jnp.split(shard, 2, axis=1)

        def stage_columns(left, right, part, columns):
            first, count = part or (0, right.shape[1])
            columns = columns or (count if count < 1024 else 512)
            grid = (count // columns,)
            right = by_columns(right, columns, first // columns)
            return left.shape[0], count, columns, grid, right

        def stage_outs(height, count, columns, of):
            first, total, into = of or (0, count, ())
            out = ((height, total), BF16, (height, columns), lambda j: (0, j + first // columns))
            return out, into

        def for_core(left, right, part=None, of=None, columns=None):
            depth, count, columns, grid, right = stage_columns(left, go(right), part, columns)
            height = width // 2
            out, into = stage_outs(height, count, columns, of)
            return kernel_call(
                send_kernel,
                grid,
                [(left, (depth, height), lambda j: (0, 1)), right],
                [out],
                time=count / 240,
                into=into,
            )[0]

        def keep_core(left, right, other, part=None, of=None, columns=None, arrived=None):
            depth, count, columns, grid, right = stage_columns(left, go(right), part, columns)
            height = width // 2
            out, into = stage_outs(height // 2, count, columns, of)
            arrived = (part or (0, 0))[0] if arrived is None else arrived
            return kernel_call(
                keep_kernel,
                grid,
                [
                    (left, (depth, height), lambda j: (0, 0)),
                    right,
                    by_columns(other, columns, arrived // columns),
                ],
                [out] * 2,
                time=count / 240,
                into=into,
            )

        def swap_y(send):
            return swap(send, others[-2])

        def add_halves(keeps, others_sent):
            parts = [add_low(*pair_of) for pair_of in zip(keeps, others_sent)]
            return reduce_rest(jnp.concatenate(parts, axis=1))

        def reduce_rest(array):
            for bit in others[-3::-1]:
                half = array.shape[0] // 2
                array = add_low(array[:half], swap(array[half:], bit))
            return array

        def scatter_z(array):
            return along_z(go(array))

        def scatter_gains(gradients, *earlier):
            array = gradients.reshape(2, n, block).transpose(1, 0, 2)
            for bit in others[::-1]:
                half = array.shape[0] // 2
                array = array[:half] + swap(array[half:], bit)
            array = after(array, *earlier)
            for bit in (2 * pair, pair):
                array = array.reshape(2, -1, 2, block)
                digit = (me // bit) % 2
                keep = lax.dynamic_index_in_dim(array, digit, 0, False)
                array = keep + swap(lax.dynamic_index_in_dim(array, 1 - digit, 0, False), bit)
            return array[0]

        def gather_square_one(own):
            own = go(own)
            return own, swap_mp(own), swap(own, pair)

        def gather_square_two(own, by_mp, by_pair):
            return own, by_mp, by_pair, swap_mp(go(by_pair))

        def scatter_square_one(parts):
            mp_one, pair_one, mp_two, pair_two = parts
            return swap_mp(go(mp_one)), swap(go(pair_one), pair), mp_two, pair_two

        def scatter_square_two(mp_one, pair_one, mp_two, pair_two):
            mp_two = swap_mp(go(add_low(mp_two, pair_one[middle:])))
            pair_two = swap(go(add_low(pair_two, mp_one[middle:])), pair)
            return mp_one, pair_one, mp_two, pair_two

        def square_operands(own, mp_one, pair_one, mp_two, pair_two):
            top = lambda i: (0, 0)
            shape = (middle, width)
            return [
                by_rows(own, middle),
                (pair_one, shape, top),
                (mp_two, shape, top),
                (mp_one, shape, top),
                (pair_two, shape, top),
            ]

        def norm_back(gain_row, values, passed, sums):
            return kernel_call(
                functools.partial(norm_back_kernel, gain_row),
                (2,),
                [
                    by_rows(values, middle),
                    by_rows(passed, middle),
                    *square_operands(*sums),
                    whole(gains),
                ],
                [
                    ((rows, width), F32, (middle, width), lambda i: (i, 0)),
                    ((rows, width), BF16, (middle, width), lambda i: (i, 0)),
                    ((8, width), F32, (8, width), lambda i: (0, 0)),
                ],
                time=5,
            )

        own_rows = lambda i: (i, 0)
        shape = (1, rows, width)

        gain_cols = jnp.pad(jnp.stack([attn_gain, mlp_gain], axis=1), ((0, 0), (0, 126)))
        cut = q_cols - 128
        last_cols = qkv_cols - cut
        first_shard = query_weight[:, :cut]
        last_shard = jnp.concatenate(
            [query_weight[:, cut:], key_matrix, value_matrix, gain_cols], axis=1
        )
        first_z = gather_z(first_shard, first_shard)
        out_shard, down_shard = transposed(out_weight), transposed(down_weight)
        cot_own = lax.dynamic_index_in_dim(cotangent, mine, 0, True)
        close(first_z, cot_own)

        first_y = gather_y(first_z)
        last_z = gather_z(last_shard, last_shard)
        starts = own_first(seq_starts)
        positions = me * rows + jnp.arange(rows, dtype=jnp.int32)[None] - starts
        tables = rope_tables(positions.reshape(tokens))
        about = [by_rows(t, rows) for t in tables]
        about += [by_rows(starts[:, :, None], 1), by_rows(starts[:, None, :], 1)]
        close(*first_y, last_z, *tables, down_shard)

        last_y = gather_y(last_z)
        first_parts = gather_core(first_y)
        out_z = gather_z(out_shard, out_shard)
        close(*last_y, *first_parts)

        last_parts = gather_core(last_y)
        close(*last_parts, out_z)

        out_y = gather_y(out_z)
        gate_z = gather_z(*halves(gate_weight))
        moved = block % 128 == 0
        all_rows, turn = inputs, mine
        if not moved:
            all_rows, turn = move_blocks(inputs, to_table, mine, BF16), jnp.int32(0)
        rows_in, first_hidden, qkv_rot, attended, gains = kernel_call(
            functools.partial(attend_kernel, n if moved else 0, q_cols, k_cols),
            (2,),
            [
                (all_rows, shape, lambda i, t: ((i + t[n]) % 2, 0, 0)),
                *[whole(p) for p in first_parts],
                *[whole(p) for p in last_parts],
                *about,
            ],
            [
                ((tokens, width), BF16, (rows, width), lambda i, t: (i, 0)),
                ((tokens, width), BF16, (rows, width), lambda i, t: (i, 0)),
                ((tokens, qkv_cols), BF16, (rows, qkv_cols), lambda i, t: (i, 0)),
                ((tokens, q_cols), BF16, (rows, q_cols), lambda i, t: (i, 0)),
                ((8, width), F32, (8, width), lambda i, t: (0, 0)),
            ],
            scalars=(jnp.concatenate([to_table, turn[None]]),),
            scratch=[pltpu.VMEM((rows, qkv_cols), F32)],
            time=15,
        )
        close(attended, *out_y)

        out_parts = gather_core(out_y)
        branch_own, branch_other = times_back([(attended, out_parts)], rows)
        close(branch_other)

        branch_other = swap_mp(go(branch_other))
        close(gate_z, branch_other)
        gate_y = gather_y(gate_z)
        up_z = gather_z(*halves(up_weight))
        after_own, hidden_own = kernel_call(
            forward_norm_kernel,
            (2,),
            [
                by_rows(rows_in, middle),
                by_rows(branch_own, middle),
                by_rows(branch_other, middle),
                whole(gains),
            ],
            [
                ((rows, width), F32, (middle, width), own_rows),
                ((rows, width), BF16, (middle, width), own_rows),
            ],
        )
        close(hidden_own)

        hidden_parts = gather_square_one(hidden_own)
        close(*hidden_parts, *gate_y, up_z)

        hidden_parts = gather_square_two(*hidden_parts)
        gate_parts = gather_core(gate_y)
        up_y = gather_y(up_z)
        down_quarters = jnp.split(down_shard, 4, axis=1)
        down_one_z = gather_z(*down_quarters[::2])
        cot_pair = swap(go(cot_own), pair)
        close(*hidden_parts, *gate_parts)

        columns = 512
        grid = (hidden_cols // columns,)
        half_hidden = hidden_cols // 2
        column_halves = ((0, half_hidden), (half_hidden, half_hidden))
        hidden_out = ((pair_tokens, hidden_cols), BF16, (pair_tokens, columns), lambda j: (0, j))
        hidden_two, gate_val = kernel_call(
            gate_kernel,
            grid,
            [
                *[whole(a) for a in hidden_parts],
                *[by_columns(p, columns) for p in gate_parts],
            ],
            [
                ((pair_tokens, width), BF16, (pair_tokens, width), lambda j: (0, 0)),
                hidden_out,
            ],
            time=14,
        )
        close(*up_y, gate_val)

        up_parts = gather_core(up_y)
        cot_both = swap_mp(go(cot_pair))
        down_two_z = gather_z(*down_quarters[1::2])
        down_one_y = gather_y(down_one_z)
        close(*up_parts)
        up_val, mixed = kernel_call(
            up_kernel,
            grid,
            [
                whole(hidden_two),
                *[by_columns(p, columns) for p in up_parts],
                by_columns(gate_val, columns),
            ],
            [hidden_out, hidden_out],
            time=16,
        )
        cot_all = jnp.zeros((4, rows, width), BF16)
        cot_all = move_blocks(cotangent, to_table, mine, BF16, cot_all)
        none = jnp.int32(0)
        cot_all = move_blocks(cot_pair, to_table, none, BF16, cot_all, 2)
        cot_all = move_blocks(after(cot_both, mixed), to_table, none, BF16, cot_all, 3)
        cot_all = cot_all.reshape(pair_tokens, width)
        close(mixed, *down_one_y, down_two_z, cot_all)

        down_two_y = gather_y(down_two_z)
        down_one = gather_core(down_one_y)
        close(*down_one)

        def mixed_back(parts, first, into=()):
            place = lambda j: (0, j + first)
            out = ((pair_tokens, hidden_cols), BF16, (pair_tokens, columns), place)
            return kernel_call(
                mixed_back_kernel,
                (hidden_cols // columns // 2,),
                [
                    whole(cot_all),
                    *[by_columns(p, columns) for p in parts],
                    by_columns(gate_val, columns, first),
                    by_columns(go(up_val), columns, first),
                ],
                [out, out],
                time=9,
                into=into,
            )

        acts = mixed_back(down_one, 0)
        down_sent = for_core(cot_all, after(mixed, acts[0]))
        close(down_sent, *down_two_y)

        down_two = gather_core(down_two_y)
        down_sent = swap(go(down_sent), 1)
        close(*down_two, down_sent)
        down_keep, down_send = keep_core(cot_all, mixed, down_sent)
        close(down_keep)
        down_arrived = swap_y(go(down_send))
        grad_gate_act, grad_up_act = mixed_back(down_two, hidden_cols // columns // 2, acts)
        sides = [(grad_gate_act, gate_parts), (grad_up_act, up_parts)]
        grad_two_own, *grad_two = times_back(sides, rows)
        close(grad_two_own)

        grad_two = scatter_square_one(grad_two)
        gate_sent = for_core(hidden_two, grad_gate_act)
        up_sent = for_core(hidden_two, after(grad_up_act, gate_sent))
        grad_down = reduce_rest(add_low(go(down_keep), down_arrived))
        close(*grad_two[:2], gate_sent, up_sent, grad_down)

        grad_two = scatter_square_two(*grad_two)
        gate_sent, up_sent = swap(go(gate_sent), 1), swap(go(up_sent), 1)
        low, high = column_halves
        gate_low = keep_core(hidden_two, grad_gate_act, gate_sent, low)
        close(*grad_two)
        grad_down = scatter_z(go(grad_down))
        close(*grad_two, *gate_low)
        gate_first = swap_y(go(gate_low[1]))
        grad_after, grad_branch, gain_two = norm_back(
            1, after_own, cot_all, (grad_two_own, *grad_two)
        )
        close(grad_branch)

        branch_other = swap_mp(go(grad_branch))
        gate_high = keep_core(hidden_two, grad_gate_act, gate_sent, high)
        gate_second = swap_y(gate_high[1])

        def attention_back(branch, which, into=()):
            block_at = lambda i: (which, 0)
            return kernel_call(
                functools.partial(attend_back_kernel, q_cols, k_cols),
                (1,),
                [
                    whole(branch),
                    *[whole(p) for p in (*out_parts, *first_parts, *last_parts)],
                    (go(qkv_rot), (rows, qkv_cols), block_at),
                    *[
                        (array, part, lambda i, d=array.ndim: (which,) + (0,) * (d - 1))
                        for array, part, _ in about
                    ],
                ],
                [
                    ((tokens, width), BF16, (rows, width), block_at),
                    ((tokens, qkv_cols), BF16, (rows, qkv_cols), block_at),
                    ((rows, width), BF16, (rows, width), lambda i: (0, 0)),
                ],
                scratch=[pltpu.VMEM((rows, q_cols), BF16)],
                time=15,
                into=into,
            )

        *backs, one_own = attention_back(grad_branch, 0)
        up_low = keep_core(hidden_two, after(grad_up_act, one_own), up_sent, low)
        close(branch_other, *up_low, one_own, grad_down, gate_first, gate_second)

        up_first = swap_y(go(up_low[1]))
        grad_gate = scatter_z(add_halves((gate_low[0], gate_high[0]), (gate_first, gate_second)))
        one_from_other = swap_mp(go(one_own))
        grad_branch, grad_qkv, one_other = attention_back(branch_other, 1, backs)
        up_high = keep_core(hidden_two, after(grad_up_act, one_other), up_sent, high)
        up_keep, up_send = zip(up_low, up_high)
        close(one_other, up_first, up_high[1], one_from_other)

        one_from_own = swap_mp(go(one_other))
        up_second = swap_y(go(up_send[1]))
        total = q_cols + qkv_cols
        sent = for_core(grad_branch, attended, of=(0, total, ()))
        sent = for_core(first_hidden, grad_qkv, of=(q_cols, total, (sent,)))
        sides = [(go(mixed), down_one), (mixed, down_two, 1)]
        branch_two_own, *branch_two = times_back(sides, rows)
        close(sent, up_second, grad_gate, branch_two_own, one_from_own)

        sent = swap(go(sent), 1)
        grad_up = scatter_z(add_halves(up_keep, (up_first, up_second)))
        branch_two = scatter_square_one(branch_two)
        close(sent)
        half, rest = total // 2, total // 2 - q_cols
        group_one = keep_core(grad_branch, attended, sent, None, (0, half, ()), 256)
        group_one = keep_core(
            first_hidden, grad_qkv, sent, (0, rest), (q_cols, half, group_one), 256, q_cols
        )
        group_two = keep_core(
            first_hidden, grad_qkv, sent, (rest, half), (0, half, ()), 256, half
        )
        close(*group_one, *group_two)

        y_one = swap_y(go(group_one[1]))
        y_two = swap_y(after(group_two[1], y_one))
        latest = lambda i, *_: (jnp.minimum(i, 1), 0)
        later = lambda i, *_: (jnp.maximum(i - 2, 0), 0)
        half_rows = (middle, width)
        input_grad, gain_one = kernel_call(
            functools.partial(last_norm_back_kernel, n if moved else 0),
            (4,),
            [
                by_rows(rows_in, middle),
                by_rows(grad_branch, middle),
                (one_own, half_rows, latest),
                (one_other, half_rows, later),
                (one_from_own, half_rows, latest),
                (one_from_other, half_rows, later),
                whole(gains),
            ],
            [
                (
                    (micro_count, rows, width),
                    F32,
                    (1, middle, width),
                    lambda i, t: ((i // 2 + t[n]) % 2, i % 2, 0),
                ),
                ((8, width), F32, (8, width), lambda i, t: (0, 0)),
            ],
            scalars=(jnp.concatenate([from_table, turn[None]]),),
            scratch=[pltpu.VMEM((1, middle, width), F32)],
            time=5,
        )
        if not moved:
            input_grad = move_blocks(input_grad, from_table, mine, F32)
        grad_down = owned(go(grad_down), None, block, True, True)
        grad_gate = owned(go(grad_gate), None, block, True, False)
        sum_one = reduce_rest(add_low(after(group_one[0], gain_one, grad_down, grad_gate), y_one))
        z_one = along_z(after(sum_one, grad_up))
        z_two = along_z(after(reduce_rest(add_low(group_two[0], y_two)), z_one))
        close(y_one, *branch_two[:2])
        branch_two = scatter_square_two(*branch_two)
        result = kernel_call(
            add_kernel,
            (2,),
            [
                by_rows(after_own, middle),
                *square_operands(branch_two_own, *branch_two),
            ],
            [((rows, width), BF16, (middle, width), own_rows)],
        )[0]
        other_result = swap_mp(result)
        gain_two = gain_two[0] + swap_mp(gain_two[0])
        grad_up = owned(after(grad_up, result), None, block, True, False)
        grad_gains = scatter_gains(jnp.stack([gain_one[0], gain_two]), grad_up)
        output = move_blocks(jnp.stack([result, other_result]), from_table, mine, BF16)
        grad_out, *grad_attn = owned_columns(
            after(z_one, grad_up), z_two, block, (q_cols, rest, k_cols)
        )
        return (
            output,
            input_grad,
            grad_gains[0],
            *grad_attn,
            grad_out,
            grad_gains[1],
            grad_gate,
            grad_up,
            grad_down,
        )

    return per_device


def solution(mesh):
    in_specs = (
        P(None, "dp", None),
        P(None, "dp"),
        P(None, "dp", None),
        P("dp"),
        P("dp", "mp"),
        P("dp", "mp"),
        P("dp", "mp"),
        P("mp", "dp"),
        P("dp"),
        P("dp", "mp"),
        P("dp", "mp"),
        P("mp", "dp"),
    )
    out_specs = (
        P(None, "dp", None),
        P(None, "dp", None),
        P("dp"),
        P("dp", "mp"),
        P("dp", "mp"),
        P("dp", "mp"),
        P("mp", "dp"),
        P("dp"),
        P("dp", "mp"),
        P("dp", "mp"),
        P("mp", "dp"),
    )
    return jax.shard_map(
        make_per_device(mesh.shape["dp"]),
        mesh=mesh,
        in_specs=in_specs,
        out_specs=out_specs,
        check_vma=False,
    )
```

```python
import functools
import math

import jax
import jax.numpy as jnp
from jax import lax
from jax.experimental import pallas as pl
from jax.experimental.pallas import tpu as pltpu
from jax.sharding import PartitionSpec as P

HEAD_SIZE = 64
LANES = 2 * HEAD_SIZE
EPSILON = 1e-05
F32 = jnp.float32
BF16 = jnp.bfloat16
PIECES = 4
VMEM_LIMIT = 56 << 20
TIME_BYTES = 1_000


def dot(left, right, left_dim, right_dim):
    return lax.dot_general(
        left, right, (((left_dim,), (right_dim,)), ((), ())), preferred_element_type=F32
    )


def add_low(left, right):
    return (left.astype(F32) + right.astype(F32)).astype(BF16)


def rope_tables(positions):
    halfway = HEAD_SIZE // 2
    lane = jnp.arange(LANES, dtype=jnp.int32)
    frequency = 500000.0 ** (-((lane % halfway).astype(F32) * 2.0 / HEAD_SIZE))
    angles = positions.astype(F32)[..., None] * frequency
    sign = jnp.where(lane % HEAD_SIZE < halfway, -1.0, 1.0)
    return (jnp.cos(angles), jnp.sin(angles) * sign)


def kernel_call(kernel, grid, ins, outs, scalars=(), scratch=(), time=2, into=()):
    first = len(scalars) + len(ins)

    def spec(array, block, place):
        if block is None:
            return pl.BlockSpec(memory_space=pl.ANY)
        single = tuple(block) == array.shape or place.__name__ == "fixed"
        mode = pl.Buffered(1) if single and math.prod(grid) > 1 else None
        return pl.BlockSpec(block, place, pipeline_mode=mode)
    return pl.pallas_call(
        kernel,
        grid_spec=pltpu.PrefetchScalarGridSpec(
            num_scalar_prefetch=len(scalars),
            grid=grid,
            in_specs=[spec(*entry) for entry in ins]
            + [pl.BlockSpec(memory_space=pl.ANY)] * len(into),
            out_specs=[pl.BlockSpec(block, place) for _, _, block, place in outs],
            scratch_shapes=list(scratch),
        ),
        out_shape=[jax.ShapeDtypeStruct(shape, kind) for shape, kind, _, _ in outs],
        compiler_params=pltpu.CompilerParams(vmem_limit_bytes=VMEM_LIMIT),
        cost_estimate=pl.CostEstimate(
            flops=1, bytes_accessed=int(time * TIME_BYTES), transcendentals=0
        ),
        input_output_aliases={first + i: i for i in range(len(into))},
    )(*scalars, *[array for array, _, _ in ins], *into)


def whole(array):
    return (array, array.shape, lambda *_: (0,) * array.ndim)


def by_rows(array, rows):
    return (array, (rows,) + array.shape[1:], lambda i, *_: (i,) + (0,) * (array.ndim - 1))


def by_columns(array, columns, first=0):
    return (array, (array.shape[0], columns), lambda j, *_: (0, j + first))


def turn_lanes(pair_rows):
    lane = lax.broadcasted_iota(jnp.int32, pair_rows.shape, 1)
    up = pltpu.roll(pair_rows, LANES - HEAD_SIZE // 2, 1)
    down = pltpu.roll(pair_rows, HEAD_SIZE // 2, 1)
    return jnp.where(lane % HEAD_SIZE < HEAD_SIZE // 2, up, down)


def doubled(pair_rows, second):
    lane = lax.broadcasted_iota(jnp.int32, pair_rows.shape, 1)
    other = pltpu.roll(pair_rows, HEAD_SIZE, 1)
    return jnp.where((lane < HEAD_SIZE) != second, pair_rows, other)


def half_lanes(pair_rows, second):
    lane = lax.broadcasted_iota(jnp.int32, pair_rows.shape, 1)
    return jnp.where((lane < HEAD_SIZE) != second, pair_rows, jnp.zeros_like(pair_rows))


def allowed_pairs(start_col_ref, start_row_ref):
    rows = start_col_ref.shape[1]
    shape = (rows, rows)
    before = lax.broadcasted_iota(jnp.int32, shape, 1) <= lax.broadcasted_iota(jnp.int32, shape, 0)
    return (start_col_ref[0] == start_row_ref[0]) & before


def head_probs(query, key, allowed):
    scores = dot(query, key, 1, 1) * (1.0 / math.sqrt(HEAD_SIZE))
    scores = jnp.where(allowed, scores, -1e30)
    expo = jnp.exp(scores - jnp.max(scores, axis=-1, keepdims=True))
    return expo / jnp.sum(expo, axis=-1, keepdims=True)


def times_pieces(left, refs, columns):
    total = None
    depth = refs[0].shape[0]
    for p, ref in enumerate(refs):
        part = dot(left[:, p * depth : (p + 1) * depth], ref[:, :columns], 1, 0)
        total = part if total is None else total + part
    return total


def attend(q_cols, k_cols, raw_ref, cosine, sine, allowed, rot_ref, out_ref):
    group_width = q_cols // k_cols

    def rope(at):
        rows = raw_ref[:, at : at + LANES]
        return (rows * cosine + turn_lanes(rows) * sine).astype(BF16)

    for kv in range(k_cols // LANES):
        k_at, v_at = q_cols + kv * LANES, q_cols + k_cols + kv * LANES
        key = rope(k_at)
        value = raw_ref[:, v_at : v_at + LANES].astype(BF16)
        rot_ref[:, k_at : k_at + LANES] = key
        rot_ref[:, v_at : v_at + LANES] = value
        for group in (0, 1):
            key_two, value_two = doubled(key, group == 1), doubled(value, group == 1)
            for pair in range(group_width // 2):
                at = ((kv * 2 + group) * group_width + 2 * pair) * HEAD_SIZE
                query = rope(at)
                rot_ref[:, at : at + LANES] = query
                parts = []
                for second in (False, True):
                    probs = head_probs(half_lanes(query, second), key_two, allowed)
                    parts.append(dot(probs.astype(BF16), value_two, 1, 0))
                lane = lax.broadcasted_iota(jnp.int32, parts[0].shape, 1)
                out_ref[:, at : at + LANES] = jnp.where(lane < HEAD_SIZE, *parts).astype(BF16)


def attend_back(q_cols, k_cols, rot_ref, grad_ref, cosine, sine, allowed, out_ref):
    group_width = q_cols // k_cols
    scale = 1.0 / math.sqrt(HEAD_SIZE)

    def unrope(rows):
        return (rows * cosine - turn_lanes(rows) * sine).astype(BF16)

    def folded(rows):
        return rows + pltpu.roll(rows, HEAD_SIZE, 1)

    for kv in range(k_cols // LANES):
        k_at, v_at = q_cols + kv * LANES, q_cols + k_cols + kv * LANES
        key, value = rot_ref[:, k_at : k_at + LANES], rot_ref[:, v_at : v_at + LANES]
        grad_keys, grad_values = [], []
        for group in (0, 1):
            key_two, value_two = doubled(key, group == 1), doubled(value, group == 1)
            grad_key = jnp.zeros(key.shape, F32)
            grad_value = jnp.zeros(key.shape, F32)
            for pair in range(group_width // 2):
                at = ((kv * 2 + group) * group_width + 2 * pair) * HEAD_SIZE
                query, grad = rot_ref[:, at : at + LANES], grad_ref[:, at : at + LANES]
                parts = []
                for second in (False, True):
                    query_one, grad_one = half_lanes(query, second), half_lanes(grad, second)
                    probs = head_probs(query_one, key_two, allowed)
                    grad_probs = dot(grad_one, value_two, 1, 1)
                    inner = jnp.sum(probs * grad_probs, axis=-1, keepdims=True)
                    grad_scores = (probs * (grad_probs - inner)).astype(BF16)
                    parts.append(dot(grad_scores, key_two, 1, 0))
                    grad_key = grad_key + dot(grad_scores, query_one, 0, 0)
                    grad_value = grad_value + dot(probs.astype(BF16), grad_one, 0, 0)
                lane = lax.broadcasted_iota(jnp.int32, parts[0].shape, 1)
                out_ref[:, at : at + LANES] = unrope(jnp.where(lane < HEAD_SIZE, *parts) * scale)
            grad_keys.append(folded(grad_key) * scale)
            grad_values.append(folded(grad_value))
        lane = lax.broadcasted_iota(jnp.int32, key.shape, 1)
        out_ref[:, k_at : k_at + LANES] = unrope(jnp.where(lane < HEAD_SIZE, *grad_keys))
        out_ref[:, v_at : v_at + LANES] = jnp.where(lane < HEAD_SIZE, *grad_values).astype(BF16)


def move_rows(table_ref, count, in_ref, store):
    block = in_ref.shape[-1] // count
    for p in range(count):
        at = pl.multiple_of(table_ref[p] * block, block)
        store(p * block, in_ref[0, :, pl.ds(at, block)])


def move_kernel(count, table_ref, in_ref, *refs):
    out_ref = refs[-1]

    def store(at, rows):
        out_ref[0, :, at : at + rows.shape[1]] = rows.astype(out_ref.dtype)

    move_rows(table_ref, count, in_ref, store)


def move_blocks(array, table, mine, kind, into=None, first=0):
    micro_count, rows, width = array.shape
    count = table.shape[0]
    block = width // count
    if block % 128:
        array = jnp.roll(array, -mine, axis=0)
        pieces = [
            lax.dynamic_slice_in_dim(array, table[p] * block, block, 2) for p in range(count)
        ]
        array = jnp.concatenate(pieces, axis=-1).astype(kind)
        if into is None:
            return array
        return lax.dynamic_update_slice_in_dim(into, array, first, 0)
    shape = array.shape if into is None else into.shape
    return kernel_call(
        functools.partial(move_kernel, count),
        (micro_count,),
        [(array, (1, rows, width), lambda i, t: ((i + t[count]) % micro_count, 0, 0))],
        [(shape, kind, (1, rows, width), lambda i, t: (i + first, 0, 0))],
        scalars=(jnp.concatenate([table, mine[None]]),),
        into=() if into is None else (into,),
    )[0]


def attend_kernel(count, q_cols, k_cols, table_ref, in_ref, *refs):
    weights, lasts, refs = refs[:PIECES], refs[PIECES : 2 * PIECES], refs[2 * PIECES :]
    cos_ref, sin_ref, col_ref, row_ref = refs[:4]
    rows_ref, hidden_ref, rot_ref, out_ref, gains_ref, raw_ref = refs[4:]
    step = pl.program_id(0)
    columns = q_cols + 2 * k_cols
    depth, cut = weights[0].shape

    @pl.when(step == 0)
    def _():
        shape = (8, 128)
        pick = lax.broadcasted_iota(jnp.int32, shape, 0) == lax.broadcasted_iota(jnp.int32, shape, 1)
        for p, ref in enumerate(lasts):
            gains_ref[:, p * depth : (p + 1) * depth] = dot(
                pick.astype(F32).astype(BF16), ref[:, columns - cut :], 1, 1
            )

    def store(at, rows):
        rows_ref[:, at : at + rows.shape[1]] = rows

    if count:
        move_rows(table_ref, count, in_ref, store)
    else:
        rows_ref[...] = in_ref[0]
    rows = rows_ref[...].astype(F32)
    inverse = lax.rsqrt(jnp.mean(rows * rows, axis=-1, keepdims=True) + EPSILON)
    hidden = (rows * inverse * gains_ref[0:1, :]).astype(BF16)
    hidden_ref[...] = hidden
    raw_ref[:, :cut] = times_pieces(hidden, weights, cut)
    raw_ref[:, cut:] = times_pieces(hidden, lasts, columns - cut)
    attend(
        q_cols,
        k_cols,
        raw_ref,
        cos_ref[...],
        sin_ref[...],
        allowed_pairs(col_ref, row_ref),
        rot_ref,
        out_ref,
    )


def attend_back_kernel(q_cols, k_cols, branch_ref, *refs):
    outs, refs = refs[:PIECES], refs[PIECES:]
    weights, lasts, refs = refs[:PIECES], refs[PIECES : 2 * PIECES], refs[2 * PIECES :]
    rot_ref, cos_ref, sin_ref, col_ref, row_ref = refs[:5]
    all_ref, qkv_ref, one_ref, grad_ref = refs[-4:]
    columns = q_cols + 2 * k_cols
    all_ref[...] = branch_ref[...]
    grad_ref[...] = times_pieces(branch_ref[...], outs, q_cols).astype(BF16)
    attend_back(
        q_cols,
        k_cols,
        rot_ref,
        grad_ref,
        cos_ref[...],
        sin_ref[...],
        allowed_pairs(col_ref, row_ref),
        qkv_ref,
    )
    depth, cut = weights[0].shape
    for p, (ref, last) in enumerate(zip(weights, lasts)):
        one = dot(qkv_ref[:, :cut], ref[...], 1, 1)
        one = one + dot(qkv_ref[:, cut:], last[:, : columns - cut], 1, 1)
        one_ref[:, p * depth : (p + 1) * depth] = one.astype(BF16)


def gate_kernel(*refs):
    blocks, weights, (all_ref, gate_ref) = refs[:4], refs[4 : 4 + PIECES], refs[4 + PIECES :]

    @pl.when(pl.program_id(0) == 0)
    def _():
        rows = blocks[0].shape[0]
        for i, ref in enumerate(blocks):
            all_ref[i * rows : (i + 1) * rows, :] = ref[...]

    gate_ref[...] = times_pieces(all_ref[...], weights, gate_ref.shape[1]).astype(BF16)


def up_kernel(all_ref, *refs):
    weights, (gate_ref, up_ref, mixed_ref) = refs[:PIECES], refs[PIECES:]
    up = times_pieces(all_ref[...], weights, up_ref.shape[1])
    gate = gate_ref[...].astype(F32)
    up_ref[...] = up.astype(BF16)
    mixed_ref[...] = (gate * jax.nn.sigmoid(gate) * up).astype(BF16)


def mixed_back_kernel(cot_ref, *refs):
    weights, refs = refs[:PIECES], refs[PIECES:]
    (gate_ref, up_ref), (grad_gate_ref, grad_up_ref) = refs[:2], refs[-2:]
    grad = times_pieces(cot_ref[...], weights, gate_ref.shape[1])
    gate = gate_ref[...].astype(F32)
    sigmoid = jax.nn.sigmoid(gate)
    inner = sigmoid * (1.0 + gate * (1.0 - sigmoid))
    grad_gate_ref[...] = (grad * up_ref[...].astype(F32) * inner).astype(BF16)
    grad_up_ref[...] = (grad * (gate * sigmoid)).astype(BF16)


def back_kernel(sides, *refs):
    lefts, refs = refs[:sides], refs[sides:]
    weights, outs = refs[: sides * PIECES], refs[sides * PIECES : -2]
    held_ref, sems = refs[-2:]
    rows = outs[0].shape[0]

    def copies(p):
        return [
            pltpu.make_async_copy(
                weights[s * PIECES + p], held_ref.at[p % 2, s], sems.at[p % 2, s]
            )
            for s in range(sides)
        ]

    for p in range(PIECES):

        @pl.when(pl.program_id(0) == p)
        def _(p=p):
            for ahead in (0, 1) if p == 0 else (p + 1,):
                if ahead < PIECES:
                    for copy in copies(ahead):
                        copy.start()
            for copy in copies(p):
                copy.wait()
            total = None
            for s in range(sides):
                part = dot(lefts[s][...], held_ref[p % 2, s], 1, 1)
                total = part if total is None else total + part
            total = total.astype(BF16)
            outs[0][...] = total[:rows]
            if len(outs) == 2:
                outs[1][...] = total[rows:]
                return
            mp_one, pair_one, mp_two, pair_two = outs[1:]
            middle = rows // 2
            mp_two[...] = total[rows : rows + middle]
            mp_one[:middle, :] = total[rows + middle : 2 * rows]
            pair_one[:middle, :] = total[2 * rows : 2 * rows + middle]
            pair_two[...] = total[2 * rows + middle : 3 * rows]
            pair_one[middle:, :] = total[3 * rows : 3 * rows + middle]
            mp_one[middle:, :] = total[3 * rows + middle :]


def times_back(sides, rows):
    depth, count = sides[0][1][0].shape
    ins = []
    for left, pieces, *place in sides:
        at = (0, place[0] if place else 0)

        def fixed(j, at=at):
            return at

        ins.append((left, (left.shape[0], count), fixed))
    for _, pieces, *_ in sides:
        ins += [(piece, None, None) for piece in pieces]
    heights = (rows, rows, rows, rows // 2, rows // 2)
    if sides[0][0].shape[0] == 2 * rows:
        heights = (rows, rows)
    return kernel_call(
        functools.partial(back_kernel, len(sides)),
        (PIECES,),
        ins,
        [((h, depth * PIECES), BF16, (h, depth), lambda j: (0, j)) for h in heights],
        scratch=[
            pltpu.VMEM((2, len(sides), depth, count), BF16),
            pltpu.SemaphoreType.DMA((2, len(sides))),
        ],
        time=7 * len(sides) * count / 1024,
    )


def forward_norm_kernel(rows_ref, own_ref, other_ref, gains_ref, after_ref, hidden_ref):
    branch = own_ref[...].astype(F32) + other_ref[...].astype(F32)
    result = rows_ref[...].astype(F32) + branch
    after_ref[...] = result
    square = jnp.mean(result * result, axis=-1, keepdims=True)
    normed = result * lax.rsqrt(square + EPSILON)
    hidden_ref[...] = (normed * gains_ref[1:2, :]).astype(BF16)


def add_kernel(rows_ref, own_ref, pair_one, mp_two, mp_one, pair_two, out_ref):
    step = pl.program_id(0)
    for i, extra in enumerate(((pair_one, mp_two), (mp_one, pair_two))):

        @pl.when(step == i)
        def _(extra=extra):
            branch = own_ref[...].astype(F32)
            branch = branch + (extra[0][...].astype(F32) + extra[1][...].astype(F32))
            out_ref[...] = (rows_ref[...].astype(F32) + branch).astype(BF16)


def norm_back_kernel(gain_row, values_ref, passed_ref, *refs):
    own_ref, pair_one, mp_two, mp_one, pair_two, gains_ref = refs[:6]
    full_ref, low_ref, gain_ref = refs[6:]
    step = pl.program_id(0)

    @pl.when(step == 0)
    def _():
        gain_ref[...] = jnp.zeros_like(gain_ref)

    for i, extra in enumerate(((pair_one, mp_two), (mp_one, pair_two))):

        @pl.when(step == i)
        def _(extra=extra):
            grad = own_ref[...].astype(F32)
            grad = grad + (extra[0][...].astype(F32) + extra[1][...].astype(F32))
            values = values_ref[...].astype(F32)
            square = jnp.mean(values * values, axis=-1, keepdims=True)
            inverse = lax.rsqrt(square + EPSILON)
            normed = values * inverse
            scaled = grad * gains_ref[gain_row : gain_row + 1, :]
            inner = jnp.mean(scaled * normed, axis=-1, keepdims=True)
            result = passed_ref[...].astype(F32) + inverse * (scaled - normed * inner)
            full_ref[...] = result
            low_ref[...] = result.astype(BF16)
            gain_ref[0:1, :] += jnp.sum(grad * normed, axis=0, keepdims=True)


def last_norm_back_kernel(count, table_ref, values_ref, passed_ref, *refs):
    parts, others, gains_ref, out_ref, gain_ref, rows_ref = refs[:2], refs[2:4], *refs[4:]
    step = pl.program_id(0)

    @pl.when(step == 0)
    def _():
        gain_ref[...] = jnp.zeros_like(gain_ref)

    for i in (0, 1):

        @pl.when(step // 2 == i)
        def _(i=i):
            grad = parts[i][...].astype(F32) + others[i][...].astype(F32)
            values = values_ref[...].astype(F32)
            square = jnp.mean(values * values, axis=-1, keepdims=True)
            inverse = lax.rsqrt(square + EPSILON)
            normed = values * inverse
            scaled = grad * gains_ref[0:1, :]
            inner = jnp.mean(scaled * normed, axis=-1, keepdims=True)
            result = passed_ref[...].astype(F32) + inverse * (scaled - normed * inner)
            rows_ref[0, :, :] = result
            gain_ref[0:1, :] += jnp.sum(grad * normed, axis=0, keepdims=True)

    def store(at, rows):
        out_ref[0, :, at : at + rows.shape[1]] = rows

    if count:
        move_rows(table_ref, count, rows_ref, store)
    else:
        out_ref[...] = rows_ref[...]


def send_kernel(left_ref, right_ref, *refs):
    refs[-1][...] = dot(left_ref[...], right_ref[...], 0, 0).astype(BF16)


def keep_kernel(left_ref, right_ref, other_ref, *refs):
    low_ref, high_ref = refs[-2:]
    total = dot(left_ref[...], right_ref[...], 0, 0) + other_ref[...].astype(F32)
    middle = low_ref.shape[0]
    low_ref[...] = total[:middle].astype(BF16)
    high_ref[...] = total[middle:].astype(BF16)


def transpose_kernel(in_ref, out_ref):
    out_ref[...] = in_ref[...].T


def transposed(array):
    rows, columns = array.shape
    if columns % 128:
        return array.T
    return kernel_call(
        transpose_kernel,
        (rows // 512,),
        [(array, (512, columns), lambda i: (i, 0))],
        [((columns, rows), array.dtype, (columns, 512), lambda i: (0, i))],
    )[0]


def owned_kernel(flip, halves, ins, *refs):
    out_ref = refs[-1]
    for i, ref in enumerate(refs[:ins]):
        parts = [ref[k].astype(F32) for k in range(4)]
        if not halves:
            total = (parts[0] + parts[2]) + (parts[1] + parts[3])
            out_ref[...] = total.T if flip else total
            return

        for side in (0, 1):

            @pl.when(pl.program_id(0) == side * ins + i)
            def _(parts=parts, side=side):
                total = parts[side] + parts[side + 2]
                out_ref[...] = total.T if flip else total


def owned(array, second, block, halves, flip):
    arrays = [a.reshape(4, block, a.shape[1]) for a in (array, second) if a is not None]
    if block % 128:
        sides = [[], []]
        for a in arrays:
            parts = a.astype(F32)
            sides[0].append(parts[0] + parts[2])
            sides[1].append(parts[1] + parts[3])
        total = [jnp.concatenate(side, axis=1) for side in sides]
        total = jnp.concatenate(total, axis=1) if halves else total[0] + total[1]
        return total.T if flip else total
    columns = arrays[0].shape[2]
    count = 2 * len(arrays) if halves else 1
    shape, part, place = (block, columns * count), (block, columns), lambda j: (0, j)
    if flip:
        shape, part, place = shape[::-1], part[::-1], lambda j: (j, 0)
    return kernel_call(
        functools.partial(owned_kernel, flip, halves, len(arrays)),
        (count,),
        [whole(a) for a in arrays],
        [(shape, F32, part, place)],
        time=3,
    )[0]


def owned_columns_kernel(cuts, one_ref, two_ref, out_ref, query_ref, key_ref, value_ref):
    one, two = (
        (ref[0].astype(F32) + ref[2].astype(F32)) + (ref[1].astype(F32) + ref[3].astype(F32))
        for ref in (one_ref, two_ref)
    )
    queries, rest, keys = cuts
    out_ref[...] = one[:, :queries].T
    query_ref[:, :rest] = one[:, queries:]
    query_ref[:, rest:] = two[:, : queries - rest]
    key_ref[...] = two[:, queries - rest : queries - rest + keys]
    value_ref[...] = two[:, queries - rest + keys :]


def owned_columns(one, two, block, cuts):
    one, two = (a.reshape(4, block, a.shape[1]) for a in (one, two))
    queries, rest, keys = cuts
    if block % 128:
        one, two = (jnp.sum(a.astype(F32), axis=0) for a in (one, two))
        together = jnp.concatenate([one, two], axis=1)
        parts = jnp.split(together, [queries, 2 * queries, 2 * queries + keys], axis=1)
        return [parts[0].T, *parts[1:]]
    shapes = [(queries, block), (block, queries), (block, keys), (block, keys)]
    return kernel_call(
        functools.partial(owned_columns_kernel, cuts),
        (1,),
        [whole(one), whole(two)],
        [(shape, F32, shape, lambda i: (0, 0)) for shape in shapes],
    )


def after(array, *earlier):
    return lax.optimization_barrier((array, *earlier))[0]


def make_per_device(n):
    pair = 4 if n <= 16 else 8
    others = [1 << b for b in reversed(range(n.bit_length() - 1))]
    others = [v for v in others if v not in (pair, 2 * pair)]
    main_order = [pair, 2 * pair] + others
    z_groups = [[i | z * pair for z in range(4)] for i in range(n) if not i & (3 * pair)]

    def swap(array, bit):
        return lax.ppermute(array, "dp", [(i, i ^ bit) for i in range(n)])

    def swap_mp(array):
        return lax.ppermute(array, "mp", [(0, 1), (1, 0)])

    def along_z(array):
        return lax.all_to_all(array, "dp", 0, 0, axis_index_groups=z_groups, tiled=True)

    def per_device(
        inputs,
        seq_starts,
        cotangent,
        attn_gain,
        query_weight,
        key_matrix,
        value_matrix,
        out_weight,
        mlp_gain,
        gate_weight,
        up_weight,
        down_weight,
    ):
        micro_count, rows, width = inputs.shape
        middle = rows // 2
        block = width // n
        tokens, pair_tokens = micro_count * rows, 2 * micro_count * rows
        q_cols, k_cols = query_weight.shape[1], key_matrix.shape[1]
        qkv_cols = q_cols + 2 * k_cols
        hidden_cols = gate_weight.shape[1] // 2
        me, mine = lax.axis_index("dp"), lax.axis_index("mp")

        def table(natural):
            entries = []
            for p in range(n):
                entry = jnp.int32(0)
                for axis, bit in enumerate(main_order):
                    digit, weight = ((p // bit) % 2, 1 << axis) if natural else ((p >> axis) % 2, bit)
                    if bit in others:
                        digit = ((me // bit) % 2 + digit) % 2
                    entry = entry + digit * weight
                entries.append(entry)
            return jnp.stack(entries)

        to_table, from_table = table(False), table(True)

        def own_first(array):
            return jnp.where(mine == 0, array, jnp.flip(array, 0))

        window = []

        def close(*results):
            window[:] = results

        def go(array):
            return after(array, *window) if window else array

        def gather_z(first, second):
            return along_z(go(jnp.concatenate([first, second, first, second], axis=0)))

        def gather_y(array):
            pieces = [array]
            for bit in others[:-1]:
                pieces = pieces + [swap(go(piece), bit) for piece in pieces]
            return pieces

        def gather_core(pieces):
            pieces = pieces + [swap(go(piece), 1) for piece in pieces]
            share = len(pieces) // PIECES
            if share > 1:
                pieces = [
                    jnp.concatenate(pieces[i * share : (i + 1) * share]) for i in range(PIECES)
                ]
            return pieces

        def halves(shard):
            return jnp.split(shard, 2, axis=1)

        def stage_columns(left, right, part, columns):
            first, count = part or (0, right.shape[1])
            columns = columns or (count if count < 1024 else 512)
            grid = (count // columns,)
            right = by_columns(right, columns, first // columns)
            return left.shape[0], count, columns, grid, right

        def stage_outs(height, count, columns, of):
            first, total, into = of or (0, count, ())
            out = ((height, total), BF16, (height, columns), lambda j: (0, j + first // columns))
            return out, into

        def for_core(left, right, part=None, of=None, columns=None):
            depth, count, columns, grid, right = stage_columns(left, go(right), part, columns)
            height = width // 2
            out, into = stage_outs(height, count, columns, of)
            return kernel_call(
                send_kernel,
                grid,
                [(left, (depth, height), lambda j: (0, 1)), right],
                [out],
                time=count / 240,
                into=into,
            )[0]

        def keep_core(left, right, other, part=None, of=None, columns=None, arrived=None):
            depth, count, columns, grid, right = stage_columns(left, go(right), part, columns)
            height = width // 2
            out, into = stage_outs(height // 2, count, columns, of)
            arrived = (part or (0, 0))[0] if arrived is None else arrived
            return kernel_call(
                keep_kernel,
                grid,
                [
                    (left, (depth, height), lambda j: (0, 0)),
                    right,
                    by_columns(other, columns, arrived // columns),
                ],
                [out] * 2,
                time=count / 240,
                into=into,
            )

        def swap_y(send):
            return swap(send, others[-2])

        def add_halves(keeps, others_sent):
            parts = [add_low(*pair_of) for pair_of in zip(keeps, others_sent)]
            return reduce_rest(jnp.concatenate(parts, axis=1))

        def reduce_rest(array):
            for bit in others[-3::-1]:
                half = array.shape[0] // 2
                array = add_low(array[:half], swap(array[half:], bit))
            return array

        def scatter_z(array):
            return along_z(go(array))

        def scatter_gains(gradients, *earlier):
            array = gradients.reshape(2, n, block).transpose(1, 0, 2)
            for bit in others[::-1]:
                half = array.shape[0] // 2
                array = array[:half] + swap(array[half:], bit)
            array = after(array, *earlier)
            for bit in (2 * pair, pair):
                array = array.reshape(2, -1, 2, block)
                digit = (me // bit) % 2
                keep = lax.dynamic_index_in_dim(array, digit, 0, False)
                array = keep + swap(lax.dynamic_index_in_dim(array, 1 - digit, 0, False), bit)
            return array[0]

        def gather_square_one(own):
            own = go(own)
            return own, swap_mp(own), swap(own, pair)

        def gather_square_two(own, by_mp, by_pair):
            return own, by_mp, by_pair, swap_mp(go(by_pair))

        def scatter_square_one(parts):
            mp_one, pair_one, mp_two, pair_two = parts
            return swap_mp(go(mp_one)), swap(go(pair_one), pair), mp_two, pair_two

        def scatter_square_two(mp_one, pair_one, mp_two, pair_two):
            mp_two = swap_mp(go(add_low(mp_two, pair_one[middle:])))
            pair_two = swap(go(add_low(pair_two, mp_one[middle:])), pair)
            return mp_one, pair_one, mp_two, pair_two

        def square_operands(own, mp_one, pair_one, mp_two, pair_two):
            top = lambda i: (0, 0)
            shape = (middle, width)
            return [
                by_rows(own, middle),
                (pair_one, shape, top),
                (mp_two, shape, top),
                (mp_one, shape, top),
                (pair_two, shape, top),
            ]

        def norm_back(gain_row, values, passed, sums):
            return kernel_call(
                functools.partial(norm_back_kernel, gain_row),
                (2,),
                [
                    by_rows(values, middle),
                    by_rows(passed, middle),
                    *square_operands(*sums),
                    whole(gains),
                ],
                [
                    ((rows, width), F32, (middle, width), lambda i: (i, 0)),
                    ((rows, width), BF16, (middle, width), lambda i: (i, 0)),
                    ((8, width), F32, (8, width), lambda i: (0, 0)),
                ],
                time=5,
            )

        own_rows = lambda i: (i, 0)
        shape = (1, rows, width)

        gain_cols = jnp.pad(jnp.stack([attn_gain, mlp_gain], axis=1), ((0, 0), (0, 126)))
        cut = q_cols - 128
        last_cols = qkv_cols - cut
        first_shard = query_weight[:, :cut]
        last_shard = jnp.concatenate(
            [query_weight[:, cut:], key_matrix, value_matrix, gain_cols], axis=1
        )
        first_z = gather_z(first_shard, first_shard)
        out_shard, down_shard = transposed(out_weight), transposed(down_weight)
        cot_own = lax.dynamic_index_in_dim(cotangent, mine, 0, True)
        close(first_z, cot_own)

        first_y = gather_y(first_z)
        last_z = gather_z(last_shard, last_shard)
        starts = own_first(seq_starts)
        positions = me * rows + jnp.arange(rows, dtype=jnp.int32)[None] - starts
        tables = rope_tables(positions.reshape(tokens))
        about = [by_rows(t, rows) for t in tables]
        about += [by_rows(starts[:, :, None], 1), by_rows(starts[:, None, :], 1)]
        close(*first_y, last_z, *tables, down_shard)

        last_y = gather_y(last_z)
        first_parts = gather_core(first_y)
        out_z = gather_z(out_shard, out_shard)
        close(*last_y, *first_parts)

        last_parts = gather_core(last_y)
        close(*last_parts, out_z)

        out_y = gather_y(out_z)
        gate_z = gather_z(*halves(gate_weight))
        moved = block % 128 == 0
        all_rows, turn = inputs, mine
        if not moved:
            all_rows, turn = move_blocks(inputs, to_table, mine, BF16), jnp.int32(0)
        rows_in, first_hidden, qkv_rot, attended, gains = kernel_call(
            functools.partial(attend_kernel, n if moved else 0, q_cols, k_cols),
            (2,),
            [
                (all_rows, shape, lambda i, t: ((i + t[n]) % 2, 0, 0)),
                *[whole(p) for p in first_parts],
                *[whole(p) for p in last_parts],
                *about,
            ],
            [
                ((tokens, width), BF16, (rows, width), lambda i, t: (i, 0)),
                ((tokens, width), BF16, (rows, width), lambda i, t: (i, 0)),
                ((tokens, qkv_cols), BF16, (rows, qkv_cols), lambda i, t: (i, 0)),
                ((tokens, q_cols), BF16, (rows, q_cols), lambda i, t: (i, 0)),
                ((8, width), F32, (8, width), lambda i, t: (0, 0)),
            ],
            scalars=(jnp.concatenate([to_table, turn[None]]),),
            scratch=[pltpu.VMEM((rows, qkv_cols), F32)],
            time=15,
        )
        close(attended, *out_y)

        out_parts = gather_core(out_y)
        branch_own, branch_other = times_back([(attended, out_parts)], rows)
        close(branch_other)

        branch_other = swap_mp(go(branch_other))
        close(gate_z, branch_other)
        gate_y = gather_y(gate_z)
        up_z = gather_z(*halves(up_weight))
        after_own, hidden_own = kernel_call(
            forward_norm_kernel,
            (2,),
            [
                by_rows(rows_in, middle),
                by_rows(branch_own, middle),
                by_rows(branch_other, middle),
                whole(gains),
            ],
            [
                ((rows, width), F32, (middle, width), own_rows),
                ((rows, width), BF16, (middle, width), own_rows),
            ],
        )
        close(hidden_own)

        hidden_parts = gather_square_one(hidden_own)
        close(*hidden_parts, *gate_y, up_z)

        hidden_parts = gather_square_two(*hidden_parts)
        gate_parts = gather_core(gate_y)
        up_y = gather_y(up_z)
        down_quarters = jnp.split(down_shard, 4, axis=1)
        down_one_z = gather_z(*down_quarters[::2])
        cot_pair = swap(go(cot_own), pair)
        close(*hidden_parts, *gate_parts)

        columns = 512
        grid = (hidden_cols // columns,)
        half_hidden = hidden_cols // 2
        column_halves = ((0, half_hidden), (half_hidden, half_hidden))
        hidden_out = ((pair_tokens, hidden_cols), BF16, (pair_tokens, columns), lambda j: (0, j))
        hidden_two, gate_val = kernel_call(
            gate_kernel,
            grid,
            [
                *[whole(a) for a in hidden_parts],
                *[by_columns(p, columns) for p in gate_parts],
            ],
            [
                ((pair_tokens, width), BF16, (pair_tokens, width), lambda j: (0, 0)),
                hidden_out,
            ],
            time=14,
        )
        close(*up_y, gate_val)

        up_parts = gather_core(up_y)
        cot_both = swap_mp(go(cot_pair))
        down_two_z = gather_z(*down_quarters[1::2])
        down_one_y = gather_y(down_one_z)
        close(*up_parts)
        up_val, mixed = kernel_call(
            up_kernel,
            grid,
            [
                whole(hidden_two),
                *[by_columns(p, columns) for p in up_parts],
                by_columns(gate_val, columns),
            ],
            [hidden_out, hidden_out],
            time=16,
        )
        cot_all = jnp.zeros((4, rows, width), BF16)
        cot_all = move_blocks(cotangent, to_table, mine, BF16, cot_all)
        none = jnp.int32(0)
        cot_all = move_blocks(cot_pair, to_table, none, BF16, cot_all, 2)
        cot_all = move_blocks(after(cot_both, mixed), to_table, none, BF16, cot_all, 3)
        cot_all = cot_all.reshape(pair_tokens, width)
        close(mixed, *down_one_y, down_two_z, cot_all)

        down_two_y = gather_y(down_two_z)
        down_one = gather_core(down_one_y)
        close(*down_one)

        def mixed_back(parts, first, into=()):
            place = lambda j: (0, j + first)
            out = ((pair_tokens, hidden_cols), BF16, (pair_tokens, columns), place)
            return kernel_call(
                mixed_back_kernel,
                (hidden_cols // columns // 2,),
                [
                    whole(cot_all),
                    *[by_columns(p, columns) for p in parts],
                    by_columns(gate_val, columns, first),
                    by_columns(go(up_val), columns, first),
                ],
                [out, out],
                time=9,
                into=into,
            )

        acts = mixed_back(down_one, 0)
        down_sent = for_core(cot_all, after(mixed, acts[0]))
        close(down_sent, *down_two_y)

        down_two = gather_core(down_two_y)
        down_sent = swap(go(down_sent), 1)
        close(*down_two, down_sent)
        down_keep, down_send = keep_core(cot_all, mixed, down_sent)
        close(down_keep)
        down_arrived = swap_y(go(down_send))
        grad_gate_act, grad_up_act = mixed_back(down_two, hidden_cols // columns // 2, acts)
        sides = [(grad_gate_act, gate_parts), (grad_up_act, up_parts)]
        grad_two_own, *grad_two = times_back(sides, rows)
        close(grad_two_own)

        grad_two = scatter_square_one(grad_two)
        gate_sent = for_core(hidden_two, grad_gate_act)
        up_sent = for_core(hidden_two, after(grad_up_act, gate_sent))
        grad_down = reduce_rest(add_low(go(down_keep), down_arrived))
        close(*grad_two[:2], gate_sent, up_sent, grad_down)

        grad_two = scatter_square_two(*grad_two)
        gate_sent, up_sent = swap(go(gate_sent), 1), swap(go(up_sent), 1)
        low, high = column_halves
        gate_low = keep_core(hidden_two, grad_gate_act, gate_sent, low)
        close(*grad_two)
        grad_down = scatter_z(go(grad_down))
        close(*grad_two, *gate_low)
        gate_first = swap_y(go(gate_low[1]))
        grad_after, grad_branch, gain_two = norm_back(
            1, after_own, cot_all, (grad_two_own, *grad_two)
        )
        close(grad_branch)

        branch_other = swap_mp(go(grad_branch))
        gate_high = keep_core(hidden_two, grad_gate_act, gate_sent, high)
        gate_second = swap_y(gate_high[1])

        def attention_back(branch, which, into=()):
            block_at = lambda i: (which, 0)
            return kernel_call(
                functools.partial(attend_back_kernel, q_cols, k_cols),
                (1,),
                [
                    whole(branch),
                    *[whole(p) for p in (*out_parts, *first_parts, *last_parts)],
                    (go(qkv_rot), (rows, qkv_cols), block_at),
                    *[
                        (array, part, lambda i, d=array.ndim: (which,) + (0,) * (d - 1))
                        for array, part, _ in about
                    ],
                ],
                [
                    ((tokens, width), BF16, (rows, width), block_at),
                    ((tokens, qkv_cols), BF16, (rows, qkv_cols), block_at),
                    ((rows, width), BF16, (rows, width), lambda i: (0, 0)),
                ],
                scratch=[pltpu.VMEM((rows, q_cols), BF16)],
                time=15,
                into=into,
            )

        *backs, one_own = attention_back(grad_branch, 0)
        up_low = keep_core(hidden_two, after(grad_up_act, one_own), up_sent, low)
        close(branch_other, *up_low, one_own, grad_down, gate_first, gate_second)

        up_first = swap_y(go(up_low[1]))
        grad_gate = scatter_z(add_halves((gate_low[0], gate_high[0]), (gate_first, gate_second)))
        one_from_other = swap_mp(go(one_own))
        grad_branch, grad_qkv, one_other = attention_back(branch_other, 1, backs)
        up_high = keep_core(hidden_two, after(grad_up_act, one_other), up_sent, high)
        up_keep, up_send = zip(up_low, up_high)
        close(one_other, up_first, up_high[1], one_from_other)

        one_from_own = swap_mp(go(one_other))
        up_second = swap_y(go(up_send[1]))
        total = q_cols + qkv_cols
        sent = for_core(grad_branch, attended, of=(0, total, ()))
        sent = for_core(first_hidden, grad_qkv, of=(q_cols, total, (sent,)))
        sides = [(go(mixed), down_one), (mixed, down_two, 1)]
        branch_two_own, *branch_two = times_back(sides, rows)
        close(sent, up_second, grad_gate, branch_two_own, one_from_own)

        sent = swap(go(sent), 1)
        grad_up = scatter_z(add_halves(up_keep, (up_first, up_second)))
        branch_two = scatter_square_one(branch_two)
        close(sent)
        half, rest = total // 2, total // 2 - q_cols
        group_one = keep_core(grad_branch, attended, sent, None, (0, half, ()), 256)
        group_one = keep_core(
            first_hidden, grad_qkv, sent, (0, rest), (q_cols, half, group_one), 256, q_cols
        )
        group_two = keep_core(
            first_hidden, grad_qkv, sent, (rest, half), (0, half, ()), 256, half
        )
        close(*group_one, *group_two)

        y_one = swap_y(go(group_one[1]))
        y_two = swap_y(after(group_two[1], y_one))
        latest = lambda i, *_: (jnp.minimum(i, 1), 0)
        later = lambda i, *_: (jnp.maximum(i - 2, 0), 0)
        half_rows = (middle, width)
        input_grad, gain_one = kernel_call(
            functools.partial(last_norm_back_kernel, n if moved else 0),
            (4,),
            [
                by_rows(rows_in, middle),
                by_rows(grad_branch, middle),
                (one_own, half_rows, latest),
                (one_other, half_rows, later),
                (one_from_own, half_rows, latest),
                (one_from_other, half_rows, later),
                whole(gains),
            ],
            [
                (
                    (micro_count, rows, width),
                    F32,
                    (1, middle, width),
                    lambda i, t: ((i // 2 + t[n]) % 2, i % 2, 0),
                ),
                ((8, width), F32, (8, width), lambda i, t: (0, 0)),
            ],
            scalars=(jnp.concatenate([from_table, turn[None]]),),
            scratch=[pltpu.VMEM((1, middle, width), F32)],
            time=5,
        )
        if not moved:
            input_grad = move_blocks(input_grad, from_table, mine, F32)
        grad_down = owned(go(grad_down), None, block, True, True)
        grad_gate = owned(go(grad_gate), None, block, True, False)
        sum_one = reduce_rest(add_low(after(group_one[0], gain_one, grad_down, grad_gate), y_one))
        z_one = along_z(after(sum_one, grad_up))
        z_two = along_z(after(reduce_rest(add_low(group_two[0], y_two)), z_one))
        close(y_one, *branch_two[:2])
        branch_two = scatter_square_two(*branch_two)
        result = kernel_call(
            add_kernel,
            (2,),
            [
                by_rows(after_own, middle),
                *square_operands(branch_two_own, *branch_two),
            ],
            [((rows, width), BF16, (middle, width), own_rows)],
        )[0]
        other_result = swap_mp(result)
        gain_two = gain_two[0] + swap_mp(gain_two[0])
        grad_up = owned(after(grad_up, result), None, block, True, False)
        grad_gains = scatter_gains(jnp.stack([gain_one[0], gain_two]), grad_up)
        output = move_blocks(jnp.stack([result, other_result]), from_table, mine, BF16)
        grad_out, *grad_attn = owned_columns(
            after(z_one, grad_up), z_two, block, (q_cols, rest, k_cols)
        )
        return (
            output,
            input_grad,
            grad_gains[0],
            *grad_attn,
            grad_out,
            grad_gains[1],
            grad_gate,
            grad_up,
            grad_down,
        )

    return per_device


def solution(mesh):
    in_specs = (
        P(None, "dp", None),
        P(None, "dp"),
        P(None, "dp", None),
        P("dp"),
        P("dp", "mp"),
        P("dp", "mp"),
        P("dp", "mp"),
        P("mp", "dp"),
        P("dp"),
        P("dp", "mp"),
        P("dp", "mp"),
        P("mp", "dp"),
    )
    out_specs = (
        P(None, "dp", None),
        P(None, "dp", None),
        P("dp"),
        P("dp", "mp"),
        P("dp", "mp"),
        P("dp", "mp"),
        P("mp", "dp"),
        P("dp"),
        P("dp", "mp"),
        P("dp", "mp"),
        P("mp", "dp"),
    )
    return jax.shard_map(
        make_per_device(mesh.shape["dp"]),
        mesh=mesh,
        in_specs=in_specs,
        out_specs=out_specs,
        check_vma=False,
    )
```

```python
import functools
import math

import jax
import jax.numpy as jnp
from jax import lax
from jax.experimental import pallas as pl
from jax.experimental.pallas import tpu as pltpu
from jax.sharding import PartitionSpec as P

HEAD_SIZE = 64
LANES = 2 * HEAD_SIZE
EPSILON = 1e-05
F32 = jnp.float32
BF16 = jnp.bfloat16
PIECES = 4
VMEM_LIMIT = 56 << 20
TIME_BYTES = 1_000


def dot(left, right, left_dim, right_dim):
    return lax.dot_general(
        left, right, (((left_dim,), (right_dim,)), ((), ())), preferred_element_type=F32
    )


def add_low(left, right):
    return (left.astype(F32) + right.astype(F32)).astype(BF16)


def rope_tables(positions):
    halfway = HEAD_SIZE // 2
    lane = jnp.arange(LANES, dtype=jnp.int32)
    frequency = 500000.0 ** (-((lane % halfway).astype(F32) * 2.0 / HEAD_SIZE))
    angles = positions.astype(F32)[..., None] * frequency
    sign = jnp.where(lane % HEAD_SIZE < halfway, -1.0, 1.0)
    return (jnp.cos(angles), jnp.sin(angles) * sign)


def kernel_call(kernel, grid, ins, outs, scalars=(), scratch=(), time=2, into=()):
    first = len(scalars) + len(ins)

    def spec(array, block, place):
        if block is None:
            return pl.BlockSpec(memory_space=pl.ANY)
        single = tuple(block) == array.shape or place.__name__ == "fixed"
        mode = pl.Buffered(1) if single and math.prod(grid) > 1 else None
        return pl.BlockSpec(block, place, pipeline_mode=mode)
    return pl.pallas_call(
        kernel,
        grid_spec=pltpu.PrefetchScalarGridSpec(
            num_scalar_prefetch=len(scalars),
            grid=grid,
            in_specs=[spec(*entry) for entry in ins]
            + [pl.BlockSpec(memory_space=pl.ANY)] * len(into),
            out_specs=[pl.BlockSpec(block, place) for _, _, block, place in outs],
            scratch_shapes=list(scratch),
        ),
        out_shape=[jax.ShapeDtypeStruct(shape, kind) for shape, kind, _, _ in outs],
        compiler_params=pltpu.CompilerParams(vmem_limit_bytes=VMEM_LIMIT),
        cost_estimate=pl.CostEstimate(
            flops=1, bytes_accessed=int(time * TIME_BYTES), transcendentals=0
        ),
        input_output_aliases={first + i: i for i in range(len(into))},
    )(*scalars, *[array for array, _, _ in ins], *into)


def whole(array):
    return (array, array.shape, lambda *_: (0,) * array.ndim)


def by_rows(array, rows):
    return (array, (rows,) + array.shape[1:], lambda i, *_: (i,) + (0,) * (array.ndim - 1))


def by_columns(array, columns, first=0):
    return (array, (array.shape[0], columns), lambda j, *_: (0, j + first))


def turn_lanes(pair_rows):
    lane = lax.broadcasted_iota(jnp.int32, pair_rows.shape, 1)
    up = pltpu.roll(pair_rows, LANES - HEAD_SIZE // 2, 1)
    down = pltpu.roll(pair_rows, HEAD_SIZE // 2, 1)
    return jnp.where(lane % HEAD_SIZE < HEAD_SIZE // 2, up, down)


def doubled(pair_rows, second):
    lane = lax.broadcasted_iota(jnp.int32, pair_rows.shape, 1)
    other = pltpu.roll(pair_rows, HEAD_SIZE, 1)
    return jnp.where((lane < HEAD_SIZE) != second, pair_rows, other)


def half_lanes(pair_rows, second):
    lane = lax.broadcasted_iota(jnp.int32, pair_rows.shape, 1)
    return jnp.where((lane < HEAD_SIZE) != second, pair_rows, jnp.zeros_like(pair_rows))


def allowed_pairs(start_col_ref, start_row_ref):
    rows = start_col_ref.shape[1]
    shape = (rows, rows)
    before = lax.broadcasted_iota(jnp.int32, shape, 1) <= lax.broadcasted_iota(jnp.int32, shape, 0)
    return (start_col_ref[0] == start_row_ref[0]) & before


def head_probs(query, key, allowed):
    scores = dot(query, key, 1, 1) * (1.0 / math.sqrt(HEAD_SIZE))
    scores = jnp.where(allowed, scores, -1e30)
    expo = jnp.exp(scores - jnp.max(scores, axis=-1, keepdims=True))
    return expo / jnp.sum(expo, axis=-1, keepdims=True)


def times_pieces(left, refs, columns):
    total = None
    depth = refs[0].shape[0]
    for p, ref in enumerate(refs):
        part = dot(left[:, p * depth : (p + 1) * depth], ref[:, :columns], 1, 0)
        total = part if total is None else total + part
    return total


def attend(q_cols, k_cols, raw_ref, cosine, sine, allowed, rot_ref, out_ref):
    group_width = q_cols // k_cols

    def rope(at):
        rows = raw_ref[:, at : at + LANES]
        return (rows * cosine + turn_lanes(rows) * sine).astype(BF16)

    for kv in range(k_cols // LANES):
        k_at, v_at = q_cols + kv * LANES, q_cols + k_cols + kv * LANES
        key = rope(k_at)
        value = raw_ref[:, v_at : v_at + LANES].astype(BF16)
        rot_ref[:, k_at : k_at + LANES] = key
        rot_ref[:, v_at : v_at + LANES] = value
        for group in (0, 1):
            key_two, value_two = doubled(key, group == 1), doubled(value, group == 1)
            for pair in range(group_width // 2):
                at = ((kv * 2 + group) * group_width + 2 * pair) * HEAD_SIZE
                query = rope(at)
                rot_ref[:, at : at + LANES] = query
                parts = []
                for second in (False, True):
                    probs = head_probs(half_lanes(query, second), key_two, allowed)
                    parts.append(dot(probs.astype(BF16), value_two, 1, 0))
                lane = lax.broadcasted_iota(jnp.int32, parts[0].shape, 1)
                out_ref[:, at : at + LANES] = jnp.where(lane < HEAD_SIZE, *parts).astype(BF16)


def attend_back(q_cols, k_cols, rot_ref, grad_ref, cosine, sine, allowed, out_ref):
    group_width = q_cols // k_cols
    scale = 1.0 / math.sqrt(HEAD_SIZE)

    def unrope(rows):
        return (rows * cosine - turn_lanes(rows) * sine).astype(BF16)

    def folded(rows):
        return rows + pltpu.roll(rows, HEAD_SIZE, 1)

    for kv in range(k_cols // LANES):
        k_at, v_at = q_cols + kv * LANES, q_cols + k_cols + kv * LANES
        key, value = rot_ref[:, k_at : k_at + LANES], rot_ref[:, v_at : v_at + LANES]
        grad_keys, grad_values = [], []
        for group in (0, 1):
            key_two, value_two = doubled(key, group == 1), doubled(value, group == 1)
            grad_key = jnp.zeros(key.shape, F32)
            grad_value = jnp.zeros(key.shape, F32)
            for pair in range(group_width // 2):
                at = ((kv * 2 + group) * group_width + 2 * pair) * HEAD_SIZE
                query, grad = rot_ref[:, at : at + LANES], grad_ref[:, at : at + LANES]
                parts = []
                for second in (False, True):
                    query_one, grad_one = half_lanes(query, second), half_lanes(grad, second)
                    probs = head_probs(query_one, key_two, allowed)
                    grad_probs = dot(grad_one, value_two, 1, 1)
                    inner = jnp.sum(probs * grad_probs, axis=-1, keepdims=True)
                    grad_scores = (probs * (grad_probs - inner)).astype(BF16)
                    parts.append(dot(grad_scores, key_two, 1, 0))
                    grad_key = grad_key + dot(grad_scores, query_one, 0, 0)
                    grad_value = grad_value + dot(probs.astype(BF16), grad_one, 0, 0)
                lane = lax.broadcasted_iota(jnp.int32, parts[0].shape, 1)
                out_ref[:, at : at + LANES] = unrope(jnp.where(lane < HEAD_SIZE, *parts) * scale)
            grad_keys.append(folded(grad_key) * scale)
            grad_values.append(folded(grad_value))
        lane = lax.broadcasted_iota(jnp.int32, key.shape, 1)
        out_ref[:, k_at : k_at + LANES] = unrope(jnp.where(lane < HEAD_SIZE, *grad_keys))
        out_ref[:, v_at : v_at + LANES] = jnp.where(lane < HEAD_SIZE, *grad_values).astype(BF16)


def move_rows(table_ref, count, in_ref, store):
    block = in_ref.shape[-1] // count
    for p in range(count):
        at = pl.multiple_of(table_ref[p] * block, block)
        store(p * block, in_ref[0, :, pl.ds(at, block)])


def move_kernel(count, table_ref, in_ref, *refs):
    out_ref = refs[-1]

    def store(at, rows):
        out_ref[0, :, at : at + rows.shape[1]] = rows.astype(out_ref.dtype)

    move_rows(table_ref, count, in_ref, store)


def move_blocks(array, table, mine, kind, into=None, first=0):
    micro_count, rows, width = array.shape
    count = table.shape[0]
    block = width // count
    if block % 128:
        array = jnp.roll(array, -mine, axis=0)
        pieces = [
            lax.dynamic_slice_in_dim(array, table[p] * block, block, 2) for p in range(count)
        ]
        array = jnp.concatenate(pieces, axis=-1).astype(kind)
        if into is None:
            return array
        return lax.dynamic_update_slice_in_dim(into, array, first, 0)
    shape = array.shape if into is None else into.shape
    return kernel_call(
        functools.partial(move_kernel, count),
        (micro_count,),
        [(array, (1, rows, width), lambda i, t: ((i + t[count]) % micro_count, 0, 0))],
        [(shape, kind, (1, rows, width), lambda i, t: (i + first, 0, 0))],
        scalars=(jnp.concatenate([table, mine[None]]),),
        into=() if into is None else (into,),
    )[0]


def attend_kernel(count, q_cols, k_cols, table_ref, in_ref, *refs):
    weights, lasts, refs = refs[:PIECES], refs[PIECES : 2 * PIECES], refs[2 * PIECES :]
    cos_ref, sin_ref, col_ref, row_ref = refs[:4]
    rows_ref, hidden_ref, rot_ref, out_ref, gains_ref, raw_ref = refs[4:]
    step = pl.program_id(0)
    columns = q_cols + 2 * k_cols
    depth, cut = weights[0].shape

    @pl.when(step == 0)
    def _():
        shape = (8, 128)
        pick = lax.broadcasted_iota(jnp.int32, shape, 0) == lax.broadcasted_iota(jnp.int32, shape, 1)
        for p, ref in enumerate(lasts):
            gains_ref[:, p * depth : (p + 1) * depth] = dot(
                pick.astype(F32).astype(BF16), ref[:, columns - cut :], 1, 1
            )

    def store(at, rows):
        rows_ref[:, at : at + rows.shape[1]] = rows

    if count:
        move_rows(table_ref, count, in_ref, store)
    else:
        rows_ref[...] = in_ref[0]
    rows = rows_ref[...].astype(F32)
    inverse = lax.rsqrt(jnp.mean(rows * rows, axis=-1, keepdims=True) + EPSILON)
    hidden = (rows * inverse * gains_ref[0:1, :]).astype(BF16)
    hidden_ref[...] = hidden
    raw_ref[:, :cut] = times_pieces(hidden, weights, cut)
    raw_ref[:, cut:] = times_pieces(hidden, lasts, columns - cut)
    attend(
        q_cols,
        k_cols,
        raw_ref,
        cos_ref[...],
        sin_ref[...],
        allowed_pairs(col_ref, row_ref),
        rot_ref,
        out_ref,
    )


def attend_back_kernel(q_cols, k_cols, branch_ref, *refs):
    outs, refs = refs[:PIECES], refs[PIECES:]
    weights, lasts, refs = refs[:PIECES], refs[PIECES : 2 * PIECES], refs[2 * PIECES :]
    rot_ref, cos_ref, sin_ref, col_ref, row_ref = refs[:5]
    all_ref, qkv_ref, one_ref, grad_ref, weights_held, lasts_held, sems = refs[-7:]
    columns = q_cols + 2 * k_cols
    copies = []
    for i, (sources, held) in enumerate(((weights, weights_held), (lasts, lasts_held))):
        for p, source in enumerate(sources):
            copies.append(pltpu.make_async_copy(source, held.at[p], sems.at[i, p]))
    for copy in copies:
        copy.start()
    all_ref[...] = branch_ref[...]
    grad_ref[...] = times_pieces(branch_ref[...], outs, q_cols).astype(BF16)
    attend_back(
        q_cols,
        k_cols,
        rot_ref,
        grad_ref,
        cos_ref[...],
        sin_ref[...],
        allowed_pairs(col_ref, row_ref),
        qkv_ref,
    )
    depth, cut = weights[0].shape
    for copy in copies:
        copy.wait()
    for p in range(PIECES):
        one = dot(qkv_ref[:, :cut], weights_held[p], 1, 1)
        one = one + dot(qkv_ref[:, cut:], lasts_held[p, :, : columns - cut], 1, 1)
        one_ref[:, p * depth : (p + 1) * depth] = one.astype(BF16)


def gate_kernel(*refs):
    blocks, weights, (all_ref, gate_ref) = refs[:4], refs[4 : 4 + PIECES], refs[4 + PIECES :]

    @pl.when(pl.program_id(0) == 0)
    def _():
        rows = blocks[0].shape[0]
        for i, ref in enumerate(blocks):
            all_ref[i * rows : (i + 1) * rows, :] = ref[...]

    gate_ref[...] = times_pieces(all_ref[...], weights, gate_ref.shape[1]).astype(BF16)


def up_kernel(all_ref, *refs):
    weights, (gate_ref, up_ref, mixed_ref) = refs[:PIECES], refs[PIECES:]
    up = times_pieces(all_ref[...], weights, up_ref.shape[1])
    gate = gate_ref[...].astype(F32)
    up_ref[...] = up.astype(BF16)
    mixed_ref[...] = (gate * jax.nn.sigmoid(gate) * up).astype(BF16)


def mixed_back_kernel(cot_ref, *refs):
    weights, refs = refs[:PIECES], refs[PIECES:]
    (gate_ref, up_ref), (grad_gate_ref, grad_up_ref) = refs[:2], refs[-2:]
    grad = times_pieces(cot_ref[...], weights, gate_ref.shape[1])
    gate = gate_ref[...].astype(F32)
    sigmoid = jax.nn.sigmoid(gate)
    inner = sigmoid * (1.0 + gate * (1.0 - sigmoid))
    grad_gate_ref[...] = (grad * up_ref[...].astype(F32) * inner).astype(BF16)
    grad_up_ref[...] = (grad * (gate * sigmoid)).astype(BF16)


def back_kernel(sides, *refs):
    lefts, refs = refs[:sides], refs[sides:]
    weights, outs = refs[: sides * PIECES], refs[sides * PIECES : -2]
    held_ref, sems = refs[-2:]
    rows = outs[0].shape[0]

    def copies(p):
        return [
            pltpu.make_async_copy(
                weights[s * PIECES + p], held_ref.at[p % 2, s], sems.at[p % 2, s]
            )
            for s in range(sides)
        ]

    for p in range(PIECES):

        @pl.when(pl.program_id(0) == p)
        def _(p=p):
            for ahead in (0, 1) if p == 0 else (p + 1,):
                if ahead < PIECES:
                    for copy in copies(ahead):
                        copy.start()
            for copy in copies(p):
                copy.wait()
            total = None
            for s in range(sides):
                part = dot(lefts[s][...], held_ref[p % 2, s], 1, 1)
                total = part if total is None else total + part
            total = total.astype(BF16)
            outs[0][...] = total[:rows]
            if len(outs) == 2:
                outs[1][...] = total[rows:]
                return
            mp_one, pair_one, mp_two, pair_two = outs[1:]
            middle = rows // 2
            mp_two[...] = total[rows : rows + middle]
            mp_one[:middle, :] = total[rows + middle : 2 * rows]
            pair_one[:middle, :] = total[2 * rows : 2 * rows + middle]
            pair_two[...] = total[2 * rows + middle : 3 * rows]
            pair_one[middle:, :] = total[3 * rows : 3 * rows + middle]
            mp_one[middle:, :] = total[3 * rows + middle :]


def times_back(sides, rows):
    depth, count = sides[0][1][0].shape
    ins = []
    for left, pieces, *place in sides:
        at = (0, place[0] if place else 0)

        def fixed(j, at=at):
            return at

        ins.append((left, (left.shape[0], count), fixed))
    for _, pieces, *_ in sides:
        ins += [(piece, None, None) for piece in pieces]
    heights = (rows, rows, rows, rows // 2, rows // 2)
    if sides[0][0].shape[0] == 2 * rows:
        heights = (rows, rows)
    return kernel_call(
        functools.partial(back_kernel, len(sides)),
        (PIECES,),
        ins,
        [((h, depth * PIECES), BF16, (h, depth), lambda j: (0, j)) for h in heights],
        scratch=[
            pltpu.VMEM((2, len(sides), depth, count), BF16),
            pltpu.SemaphoreType.DMA((2, len(sides))),
        ],
        time=7 * len(sides) * count / 1024,
    )


def forward_norm_kernel(rows_ref, own_ref, other_ref, gains_ref, after_ref, hidden_ref):
    branch = own_ref[...].astype(F32) + other_ref[...].astype(F32)
    result = rows_ref[...].astype(F32) + branch
    after_ref[...] = result
    square = jnp.mean(result * result, axis=-1, keepdims=True)
    normed = result * lax.rsqrt(square + EPSILON)
    hidden_ref[...] = (normed * gains_ref[1:2, :]).astype(BF16)


def add_kernel(rows_ref, own_ref, pair_one, mp_two, mp_one, pair_two, out_ref):
    step = pl.program_id(0)
    for i, extra in enumerate(((pair_one, mp_two), (mp_one, pair_two))):

        @pl.when(step == i)
        def _(extra=extra):
            branch = own_ref[...].astype(F32)
            branch = branch + (extra[0][...].astype(F32) + extra[1][...].astype(F32))
            out_ref[...] = (rows_ref[...].astype(F32) + branch).astype(BF16)


def norm_back_kernel(gain_row, values_ref, passed_ref, *refs):
    own_ref, pair_one, mp_two, mp_one, pair_two, gains_ref = refs[:6]
    full_ref, low_ref, gain_ref = refs[6:]
    step = pl.program_id(0)

    @pl.when(step == 0)
    def _():
        gain_ref[...] = jnp.zeros_like(gain_ref)

    for i, extra in enumerate(((pair_one, mp_two), (mp_one, pair_two))):

        @pl.when(step == i)
        def _(extra=extra):
            grad = own_ref[...].astype(F32)
            grad = grad + (extra[0][...].astype(F32) + extra[1][...].astype(F32))
            values = values_ref[...].astype(F32)
            square = jnp.mean(values * values, axis=-1, keepdims=True)
            inverse = lax.rsqrt(square + EPSILON)
            normed = values * inverse
            scaled = grad * gains_ref[gain_row : gain_row + 1, :]
            inner = jnp.mean(scaled * normed, axis=-1, keepdims=True)
            result = passed_ref[...].astype(F32) + inverse * (scaled - normed * inner)
            full_ref[...] = result
            low_ref[...] = result.astype(BF16)
            gain_ref[0:1, :] += jnp.sum(grad * normed, axis=0, keepdims=True)


def last_norm_back_kernel(count, table_ref, values_ref, passed_ref, *refs):
    parts, others, gains_ref, out_ref, gain_ref, rows_ref = refs[:2], refs[2:4], *refs[4:]
    step = pl.program_id(0)

    @pl.when(step == 0)
    def _():
        gain_ref[...] = jnp.zeros_like(gain_ref)

    for i in (0, 1):

        @pl.when(step // 2 == i)
        def _(i=i):
            grad = parts[i][...].astype(F32) + others[i][...].astype(F32)
            values = values_ref[...].astype(F32)
            square = jnp.mean(values * values, axis=-1, keepdims=True)
            inverse = lax.rsqrt(square + EPSILON)
            normed = values * inverse
            scaled = grad * gains_ref[0:1, :]
            inner = jnp.mean(scaled * normed, axis=-1, keepdims=True)
            result = passed_ref[...].astype(F32) + inverse * (scaled - normed * inner)
            rows_ref[0, :, :] = result
            gain_ref[0:1, :] += jnp.sum(grad * normed, axis=0, keepdims=True)

    def store(at, rows):
        out_ref[0, :, at : at + rows.shape[1]] = rows

    if count:
        move_rows(table_ref, count, rows_ref, store)
    else:
        out_ref[...] = rows_ref[...]


def send_kernel(left_ref, right_ref, *refs):
    refs[-1][...] = dot(left_ref[...], right_ref[...], 0, 0).astype(BF16)


def keep_kernel(left_ref, right_ref, other_ref, *refs):
    low_ref, high_ref = refs[-2:]
    total = dot(left_ref[...], right_ref[...], 0, 0) + other_ref[...].astype(F32)
    middle = low_ref.shape[0]
    low_ref[...] = total[:middle].astype(BF16)
    high_ref[...] = total[middle:].astype(BF16)


def transpose_kernel(in_ref, out_ref):
    out_ref[...] = in_ref[...].T


def transposed(array):
    rows, columns = array.shape
    if columns % 128:
        return array.T
    return kernel_call(
        transpose_kernel,
        (rows // 512,),
        [(array, (512, columns), lambda i: (i, 0))],
        [((columns, rows), array.dtype, (columns, 512), lambda i: (0, i))],
    )[0]


def owned_kernel(flip, halves, ins, *refs):
    out_ref = refs[-1]
    for i, ref in enumerate(refs[:ins]):
        parts = [ref[k].astype(F32) for k in range(4)]
        if not halves:
            total = (parts[0] + parts[2]) + (parts[1] + parts[3])
            out_ref[...] = total.T if flip else total
            return

        for side in (0, 1):

            @pl.when(pl.program_id(0) == side * ins + i)
            def _(parts=parts, side=side):
                total = parts[side] + parts[side + 2]
                out_ref[...] = total.T if flip else total


def owned(array, second, block, halves, flip):
    arrays = [a.reshape(4, block, a.shape[1]) for a in (array, second) if a is not None]
    if block % 128:
        sides = [[], []]
        for a in arrays:
            parts = a.astype(F32)
            sides[0].append(parts[0] + parts[2])
            sides[1].append(parts[1] + parts[3])
        total = [jnp.concatenate(side, axis=1) for side in sides]
        total = jnp.concatenate(total, axis=1) if halves else total[0] + total[1]
        return total.T if flip else total
    columns = arrays[0].shape[2]
    count = 2 * len(arrays) if halves else 1
    shape, part, place = (block, columns * count), (block, columns), lambda j: (0, j)
    if flip:
        shape, part, place = shape[::-1], part[::-1], lambda j: (j, 0)
    return kernel_call(
        functools.partial(owned_kernel, flip, halves, len(arrays)),
        (count,),
        [whole(a) for a in arrays],
        [(shape, F32, part, place)],
        time=3,
    )[0]


def owned_columns_kernel(cuts, one_ref, two_ref, out_ref, query_ref, key_ref, value_ref):
    one, two = (
        (ref[0].astype(F32) + ref[2].astype(F32)) + (ref[1].astype(F32) + ref[3].astype(F32))
        for ref in (one_ref, two_ref)
    )
    queries, rest, keys = cuts
    out_ref[...] = one[:, :queries].T
    query_ref[:, :rest] = one[:, queries:]
    query_ref[:, rest:] = two[:, : queries - rest]
    key_ref[...] = two[:, queries - rest : queries - rest + keys]
    value_ref[...] = two[:, queries - rest + keys :]


def owned_columns(one, two, block, cuts):
    one, two = (a.reshape(4, block, a.shape[1]) for a in (one, two))
    queries, rest, keys = cuts
    if block % 128:
        one, two = (jnp.sum(a.astype(F32), axis=0) for a in (one, two))
        together = jnp.concatenate([one, two], axis=1)
        parts = jnp.split(together, [queries, 2 * queries, 2 * queries + keys], axis=1)
        return [parts[0].T, *parts[1:]]
    shapes = [(queries, block), (block, queries), (block, keys), (block, keys)]
    return kernel_call(
        functools.partial(owned_columns_kernel, cuts),
        (1,),
        [whole(one), whole(two)],
        [(shape, F32, shape, lambda i: (0, 0)) for shape in shapes],
    )


def after(array, *earlier):
    return lax.optimization_barrier((array, *earlier))[0]


def make_per_device(n):
    pair = 4 if n <= 16 else 8
    others = [1 << b for b in reversed(range(n.bit_length() - 1))]
    others = [v for v in others if v not in (pair, 2 * pair)]
    main_order = [pair, 2 * pair] + others
    z_groups = [[i | z * pair for z in range(4)] for i in range(n) if not i & (3 * pair)]

    def swap(array, bit):
        return lax.ppermute(array, "dp", [(i, i ^ bit) for i in range(n)])

    def swap_mp(array):
        return lax.ppermute(array, "mp", [(0, 1), (1, 0)])

    def along_z(array):
        return lax.all_to_all(array, "dp", 0, 0, axis_index_groups=z_groups, tiled=True)

    def per_device(
        inputs,
        seq_starts,
        cotangent,
        attn_gain,
        query_weight,
        key_matrix,
        value_matrix,
        out_weight,
        mlp_gain,
        gate_weight,
        up_weight,
        down_weight,
    ):
        micro_count, rows, width = inputs.shape
        middle = rows // 2
        block = width // n
        tokens, pair_tokens = micro_count * rows, 2 * micro_count * rows
        q_cols, k_cols = query_weight.shape[1], key_matrix.shape[1]
        qkv_cols = q_cols + 2 * k_cols
        hidden_cols = gate_weight.shape[1] // 2
        me, mine = lax.axis_index("dp"), lax.axis_index("mp")

        def table(natural):
            entries = []
            for p in range(n):
                entry = jnp.int32(0)
                for axis, bit in enumerate(main_order):
                    digit, weight = ((p // bit) % 2, 1 << axis) if natural else ((p >> axis) % 2, bit)
                    if bit in others:
                        digit = ((me // bit) % 2 + digit) % 2
                    entry = entry + digit * weight
                entries.append(entry)
            return jnp.stack(entries)

        to_table, from_table = table(False), table(True)

        def own_first(array):
            return jnp.where(mine == 0, array, jnp.flip(array, 0))

        window = []

        def close(*results):
            window[:] = results

        def go(array):
            return after(array, *window) if window else array

        def gather_z(first, second):
            return along_z(go(jnp.concatenate([first, second, first, second], axis=0)))

        def gather_y(array):
            pieces = [array]
            for bit in others[:-1]:
                pieces = pieces + [swap(go(piece), bit) for piece in pieces]
            return pieces

        def gather_core(pieces):
            pieces = pieces + [swap(go(piece), 1) for piece in pieces]
            share = len(pieces) // PIECES
            if share > 1:
                pieces = [
                    jnp.concatenate(pieces[i * share : (i + 1) * share]) for i in range(PIECES)
                ]
            return pieces

        def halves(shard):
            return jnp.split(shard, 2, axis=1)

        def stage_columns(left, right, part, columns):
            first, count = part or (0, right.shape[1])
            columns = columns or (count if count < 1024 else 512)
            grid = (count // columns,)
            right = by_columns(right, columns, first // columns)
            return left.shape[0], count, columns, grid, right

        def stage_outs(height, count, columns, of):
            first, total, into = of or (0, count, ())
            out = ((height, total), BF16, (height, columns), lambda j: (0, j + first // columns))
            return out, into

        def for_core(left, right, part=None, of=None, columns=None):
            depth, count, columns, grid, right = stage_columns(left, go(right), part, columns)
            height = width // 2
            out, into = stage_outs(height, count, columns, of)
            return kernel_call(
                send_kernel,
                grid,
                [(left, (depth, height), lambda j: (0, 1)), right],
                [out],
                time=count / 240,
                into=into,
            )[0]

        def keep_core(left, right, other, part=None, of=None, columns=None, arrived=None):
            depth, count, columns, grid, right = stage_columns(left, go(right), part, columns)
            height = width // 2
            out, into = stage_outs(height // 2, count, columns, of)
            arrived = (part or (0, 0))[0] if arrived is None else arrived
            return kernel_call(
                keep_kernel,
                grid,
                [
                    (left, (depth, height), lambda j: (0, 0)),
                    right,
                    by_columns(other, columns, arrived // columns),
                ],
                [out] * 2,
                time=count / 240,
                into=into,
            )

        def swap_y(send):
            return swap(send, others[-2])

        def add_halves(keeps, others_sent):
            parts = [add_low(*pair_of) for pair_of in zip(keeps, others_sent)]
            return reduce_rest(jnp.concatenate(parts, axis=1))

        def reduce_rest(array):
            for bit in others[-3::-1]:
                half = array.shape[0] // 2
                array = add_low(array[:half], swap(array[half:], bit))
            return array

        def scatter_z(array):
            return along_z(go(array))

        def scatter_gains(gradients, *earlier):
            array = gradients.reshape(2, n, block).transpose(1, 0, 2)
            for bit in others[::-1]:
                half = array.shape[0] // 2
                array = array[:half] + swap(array[half:], bit)
            array = after(array, *earlier)
            for bit in (2 * pair, pair):
                array = array.reshape(2, -1, 2, block)
                digit = (me // bit) % 2
                keep = lax.dynamic_index_in_dim(array, digit, 0, False)
                array = keep + swap(lax.dynamic_index_in_dim(array, 1 - digit, 0, False), bit)
            return array[0]

        def gather_square_one(own):
            own = go(own)
            return own, swap_mp(own), swap(own, pair)

        def gather_square_two(own, by_mp, by_pair):
            return own, by_mp, by_pair, swap_mp(go(by_pair))

        def scatter_square_one(parts):
            mp_one, pair_one, mp_two, pair_two = parts
            return swap_mp(go(mp_one)), swap(go(pair_one), pair), mp_two, pair_two

        def scatter_square_two(mp_one, pair_one, mp_two, pair_two):
            mp_two = swap_mp(go(add_low(mp_two, pair_one[middle:])))
            pair_two = swap(go(add_low(pair_two, mp_one[middle:])), pair)
            return mp_one, pair_one, mp_two, pair_two

        def square_operands(own, mp_one, pair_one, mp_two, pair_two):
            top = lambda i: (0, 0)
            shape = (middle, width)
            return [
                by_rows(own, middle),
                (pair_one, shape, top),
                (mp_two, shape, top),
                (mp_one, shape, top),
                (pair_two, shape, top),
            ]

        def norm_back(gain_row, values, passed, sums):
            return kernel_call(
                functools.partial(norm_back_kernel, gain_row),
                (2,),
                [
                    by_rows(values, middle),
                    by_rows(passed, middle),
                    *square_operands(*sums),
                    whole(gains),
                ],
                [
                    ((rows, width), F32, (middle, width), lambda i: (i, 0)),
                    ((rows, width), BF16, (middle, width), lambda i: (i, 0)),
                    ((8, width), F32, (8, width), lambda i: (0, 0)),
                ],
                time=5,
            )

        own_rows = lambda i: (i, 0)
        shape = (1, rows, width)

        gain_cols = jnp.pad(jnp.stack([attn_gain, mlp_gain], axis=1), ((0, 0), (0, 126)))
        cut = q_cols - 128
        last_cols = qkv_cols - cut
        first_shard = query_weight[:, :cut]
        last_shard = jnp.concatenate(
            [query_weight[:, cut:], key_matrix, value_matrix, gain_cols], axis=1
        )
        first_z = gather_z(first_shard, first_shard)
        out_shard, down_shard = transposed(out_weight), transposed(down_weight)
        cot_own = lax.dynamic_index_in_dim(cotangent, mine, 0, True)
        close(first_z, cot_own)

        first_y = gather_y(first_z)
        last_z = gather_z(last_shard, last_shard)
        starts = own_first(seq_starts)
        positions = me * rows + jnp.arange(rows, dtype=jnp.int32)[None] - starts
        tables = rope_tables(positions.reshape(tokens))
        about = [by_rows(t, rows) for t in tables]
        about += [by_rows(starts[:, :, None], 1), by_rows(starts[:, None, :], 1)]
        close(*first_y, last_z, *tables, down_shard)

        last_y = gather_y(last_z)
        first_parts = gather_core(first_y)
        out_z = gather_z(out_shard, out_shard)
        close(*last_y, *first_parts)

        last_parts = gather_core(last_y)
        close(*last_parts, out_z)

        out_y = gather_y(out_z)
        gate_z = gather_z(*halves(gate_weight))
        moved = block % 128 == 0
        all_rows, turn = inputs, mine
        if not moved:
            all_rows, turn = move_blocks(inputs, to_table, mine, BF16), jnp.int32(0)
        rows_in, first_hidden, qkv_rot, attended, gains = kernel_call(
            functools.partial(attend_kernel, n if moved else 0, q_cols, k_cols),
            (2,),
            [
                (all_rows, shape, lambda i, t: ((i + t[n]) % 2, 0, 0)),
                *[whole(p) for p in first_parts],
                *[whole(p) for p in last_parts],
                *about,
            ],
            [
                ((tokens, width), BF16, (rows, width), lambda i, t: (i, 0)),
                ((tokens, width), BF16, (rows, width), lambda i, t: (i, 0)),
                ((tokens, qkv_cols), BF16, (rows, qkv_cols), lambda i, t: (i, 0)),
                ((tokens, q_cols), BF16, (rows, q_cols), lambda i, t: (i, 0)),
                ((8, width), F32, (8, width), lambda i, t: (0, 0)),
            ],
            scalars=(jnp.concatenate([to_table, turn[None]]),),
            scratch=[pltpu.VMEM((rows, qkv_cols), F32)],
            time=15,
        )
        close(attended, *out_y)

        out_parts = gather_core(out_y)
        branch_own, branch_other = times_back([(attended, out_parts)], rows)
        close(branch_other)

        branch_other = swap_mp(go(branch_other))
        close(gate_z, branch_other)
        gate_y = gather_y(gate_z)
        up_z = gather_z(*halves(up_weight))
        after_own, hidden_own = kernel_call(
            forward_norm_kernel,
            (2,),
            [
                by_rows(rows_in, middle),
                by_rows(branch_own, middle),
                by_rows(branch_other, middle),
                whole(gains),
            ],
            [
                ((rows, width), F32, (middle, width), own_rows),
                ((rows, width), BF16, (middle, width), own_rows),
            ],
        )
        close(hidden_own)

        hidden_parts = gather_square_one(hidden_own)
        close(*hidden_parts, *gate_y, up_z)

        hidden_parts = gather_square_two(*hidden_parts)
        gate_parts = gather_core(gate_y)
        up_y = gather_y(up_z)
        down_quarters = jnp.split(down_shard, 4, axis=1)
        down_one_z = gather_z(*down_quarters[::2])
        cot_pair = swap(go(cot_own), pair)
        close(*hidden_parts, *gate_parts)

        columns = 512
        grid = (hidden_cols // columns,)
        half_hidden = hidden_cols // 2
        column_halves = ((0, half_hidden), (half_hidden, half_hidden))
        hidden_out = ((pair_tokens, hidden_cols), BF16, (pair_tokens, columns), lambda j: (0, j))
        hidden_two, gate_val = kernel_call(
            gate_kernel,
            grid,
            [
                *[whole(a) for a in hidden_parts],
                *[by_columns(p, columns) for p in gate_parts],
            ],
            [
                ((pair_tokens, width), BF16, (pair_tokens, width), lambda j: (0, 0)),
                hidden_out,
            ],
            time=14,
        )
        close(*up_y, gate_val)

        up_parts = gather_core(up_y)
        cot_both = swap_mp(go(cot_pair))
        down_two_z = gather_z(*down_quarters[1::2])
        down_one_y = gather_y(down_one_z)
        close(*up_parts)
        up_val, mixed = kernel_call(
            up_kernel,
            grid,
            [
                whole(hidden_two),
                *[by_columns(p, columns) for p in up_parts],
                by_columns(gate_val, columns),
            ],
            [hidden_out, hidden_out],
            time=16,
        )
        cot_all = jnp.zeros((4, rows, width), BF16)
        cot_all = move_blocks(cotangent, to_table, mine, BF16, cot_all)
        none = jnp.int32(0)
        cot_all = move_blocks(cot_pair, to_table, none, BF16, cot_all, 2)
        cot_all = move_blocks(after(cot_both, mixed), to_table, none, BF16, cot_all, 3)
        cot_all = cot_all.reshape(pair_tokens, width)
        close(mixed, *down_one_y, down_two_z, cot_all)

        down_two_y = gather_y(down_two_z)
        down_one = gather_core(down_one_y)
        close(*down_one)

        def mixed_back(parts, first, into=()):
            place = lambda j: (0, j + first)
            out = ((pair_tokens, hidden_cols), BF16, (pair_tokens, columns), place)
            return kernel_call(
                mixed_back_kernel,
                (hidden_cols // columns // 2,),
                [
                    whole(cot_all),
                    *[by_columns(p, columns) for p in parts],
                    by_columns(gate_val, columns, first),
                    by_columns(go(up_val), columns, first),
                ],
                [out, out],
                time=9,
                into=into,
            )

        acts = mixed_back(down_one, 0)
        down_sent = for_core(cot_all, after(mixed, acts[0]))
        close(down_sent, *down_two_y)

        down_two = gather_core(down_two_y)
        down_sent = swap(go(down_sent), 1)
        close(*down_two, down_sent)
        down_keep, down_send = keep_core(cot_all, mixed, down_sent)
        close(down_keep)
        down_arrived = swap_y(go(down_send))
        grad_gate_act, grad_up_act = mixed_back(down_two, hidden_cols // columns // 2, acts)
        sides = [(grad_gate_act, gate_parts), (grad_up_act, up_parts)]
        grad_two_own, *grad_two = times_back(sides, rows)
        close(grad_two_own)

        grad_two = scatter_square_one(grad_two)
        gate_sent = for_core(hidden_two, grad_gate_act)
        up_sent = for_core(hidden_two, after(grad_up_act, gate_sent))
        grad_down = reduce_rest(add_low(go(down_keep), down_arrived))
        close(*grad_two[:2], gate_sent, up_sent, grad_down)

        grad_two = scatter_square_two(*grad_two)
        gate_sent, up_sent = swap(go(gate_sent), 1), swap(go(up_sent), 1)
        low, high = column_halves
        gate_low = keep_core(hidden_two, grad_gate_act, gate_sent, low)
        close(*grad_two)
        grad_down = scatter_z(go(grad_down))
        close(*grad_two, *gate_low)
        gate_first = swap_y(go(gate_low[1]))
        grad_after, grad_branch, gain_two = norm_back(
            1, after_own, cot_all, (grad_two_own, *grad_two)
        )
        close(grad_branch)

        branch_other = swap_mp(go(grad_branch))
        gate_high = keep_core(hidden_two, grad_gate_act, gate_sent, high)
        gate_second = swap_y(gate_high[1])

        def attention_back(branch, which, into=()):
            block_at = lambda i: (which, 0)
            return kernel_call(
                functools.partial(attend_back_kernel, q_cols, k_cols),
                (1,),
                [
                    whole(branch),
                    *[whole(p) for p in out_parts],
                    *[(p, None, None) for p in (*first_parts, *last_parts)],
                    (go(qkv_rot), (rows, qkv_cols), block_at),
                    *[
                        (array, part, lambda i, d=array.ndim: (which,) + (0,) * (d - 1))
                        for array, part, _ in about
                    ],
                ],
                [
                    ((tokens, width), BF16, (rows, width), block_at),
                    ((tokens, qkv_cols), BF16, (rows, qkv_cols), block_at),
                    ((rows, width), BF16, (rows, width), lambda i: (0, 0)),
                ],
                scratch=[
                    pltpu.VMEM((rows, q_cols), BF16),
                    *[pltpu.VMEM((PIECES,) + w[0].shape, BF16) for w in (first_parts, last_parts)],
                    pltpu.SemaphoreType.DMA((2, PIECES)),
                ],
                time=15,
                into=into,
            )

        *backs, one_own = attention_back(grad_branch, 0)
        up_low = keep_core(hidden_two, after(grad_up_act, one_own), up_sent, low)
        close(branch_other, *up_low, one_own, grad_down, gate_first, gate_second)

        up_first = swap_y(go(up_low[1]))
        grad_gate = scatter_z(add_halves((gate_low[0], gate_high[0]), (gate_first, gate_second)))
        one_from_other = swap_mp(go(one_own))
        grad_branch, grad_qkv, one_other = attention_back(branch_other, 1, backs)
        up_high = keep_core(hidden_two, after(grad_up_act, one_other), up_sent, high)
        up_keep, up_send = zip(up_low, up_high)
        close(one_other, up_first, up_high[1], one_from_other)

        one_from_own = swap_mp(go(one_other))
        up_second = swap_y(go(up_send[1]))
        total = q_cols + qkv_cols
        sent = for_core(grad_branch, attended, of=(0, total, ()))
        sent = for_core(first_hidden, grad_qkv, of=(q_cols, total, (sent,)))
        sides = [(go(mixed), down_one), (mixed, down_two, 1)]
        branch_two_own, *branch_two = times_back(sides, rows)
        close(sent, up_second, grad_gate, branch_two_own, one_from_own)

        sent = swap(go(sent), 1)
        grad_up = scatter_z(add_halves(up_keep, (up_first, up_second)))
        branch_two = scatter_square_one(branch_two)
        close(sent)
        half, rest = total // 2, total // 2 - q_cols
        group_one = keep_core(grad_branch, attended, sent, None, (0, half, ()), 256)
        group_one = keep_core(
            first_hidden, grad_qkv, sent, (0, rest), (q_cols, half, group_one), 256, q_cols
        )
        group_two = keep_core(
            first_hidden, grad_qkv, sent, (rest, half), (0, half, ()), 256, half
        )
        close(*group_one, *group_two)

        y_one = swap_y(go(group_one[1]))
        y_two = swap_y(after(group_two[1], y_one))
        latest = lambda i, *_: (jnp.minimum(i, 1), 0)
        later = lambda i, *_: (jnp.maximum(i - 2, 0), 0)
        half_rows = (middle, width)
        input_grad, gain_one = kernel_call(
            functools.partial(last_norm_back_kernel, n if moved else 0),
            (4,),
            [
                by_rows(rows_in, middle),
                by_rows(grad_branch, middle),
                (one_own, half_rows, latest),
                (one_other, half_rows, later),
                (one_from_own, half_rows, latest),
                (one_from_other, half_rows, later),
                whole(gains),
            ],
            [
                (
                    (micro_count, rows, width),
                    F32,
                    (1, middle, width),
                    lambda i, t: ((i // 2 + t[n]) % 2, i % 2, 0),
                ),
                ((8, width), F32, (8, width), lambda i, t: (0, 0)),
            ],
            scalars=(jnp.concatenate([from_table, turn[None]]),),
            scratch=[pltpu.VMEM((1, middle, width), F32)],
            time=5,
        )
        if not moved:
            input_grad = move_blocks(input_grad, from_table, mine, F32)
        grad_down = owned(go(grad_down), None, block, True, True)
        grad_gate = owned(go(grad_gate), None, block, True, False)
        sum_one = reduce_rest(add_low(after(group_one[0], gain_one, grad_down, grad_gate), y_one))
        z_one = along_z(after(sum_one, grad_up))
        z_two = along_z(after(reduce_rest(add_low(group_two[0], y_two)), z_one))
        close(y_one, *branch_two[:2])
        branch_two = scatter_square_two(*branch_two)
        result = kernel_call(
            add_kernel,
            (2,),
            [
                by_rows(after_own, middle),
                *square_operands(branch_two_own, *branch_two),
            ],
            [((rows, width), BF16, (middle, width), own_rows)],
        )[0]
        other_result = swap_mp(result)
        gain_two = gain_two[0] + swap_mp(gain_two[0])
        grad_up = owned(after(grad_up, result), None, block, True, False)
        grad_gains = scatter_gains(jnp.stack([gain_one[0], gain_two]), grad_up)
        output = move_blocks(jnp.stack([result, other_result]), from_table, mine, BF16)
        grad_out, *grad_attn = owned_columns(
            after(z_one, grad_up), z_two, block, (q_cols, rest, k_cols)
        )
        return (
            output,
            input_grad,
            grad_gains[0],
            *grad_attn,
            grad_out,
            grad_gains[1],
            grad_gate,
            grad_up,
            grad_down,
        )

    return per_device


def solution(mesh):
    in_specs = (
        P(None, "dp", None),
        P(None, "dp"),
        P(None, "dp", None),
        P("dp"),
        P("dp", "mp"),
        P("dp", "mp"),
        P("dp", "mp"),
        P("mp", "dp"),
        P("dp"),
        P("dp", "mp"),
        P("dp", "mp"),
        P("mp", "dp"),
    )
    out_specs = (
        P(None, "dp", None),
        P(None, "dp", None),
        P("dp"),
        P("dp", "mp"),
        P("dp", "mp"),
        P("dp", "mp"),
        P("mp", "dp"),
        P("dp"),
        P("dp", "mp"),
        P("dp", "mp"),
        P("mp", "dp"),
    )
    return jax.shard_map(
        make_per_device(mesh.shape["dp"]),
        mesh=mesh,
        in_specs=in_specs,
        out_specs=out_specs,
        check_vma=False,
    )
```
